32 devices in a mesh: brow: 4 (over y, x), bcol: 8 (over z, core).
Axes of the slice: x: 2, y: 2, z: 4, core: 2. Of those that a mesh axis runs over, the one named last changes fastest.
Arguments:
- panel_points: bfloat16 [3, 6144], P(None, ('brow', 'bcol')), may hold values from 0 to 1
- panel_map: int32 [3, 6144], replicated, may hold values from 0 to 2047, as said below
- element_nodes: int32 [125, 1024], P(None, ('brow', 'bcol')), may hold values from 0 to 2047
- element_coef: float32 [1024], P(('brow', 'bcol')), may hold values from 0.1 to 1
- element_matrix: float32 [125, 125], replicated, as said below
- node_mass: float32 [65536], P(('brow', 'bcol')), may hold values from 2 to 4
- forcing: float32 [64, 65536], P(None, ('brow', 'bcol')), may hold values from -6 to 6
- field_start: float32 [64, 65536], P(None, ('brow', 'bcol')), may hold values from -6 to 6
- potential_start: float32 [64, 6144], P(None, ('brow', 'bcol')), may hold values from -6 to 6
Outputs:
- fem_field: float32 [64, 65536], P(None, ('brow', 'bcol'))
- potential: float32 [64, 6144], P(None, ('brow', 'bcol'))
The draws below stay inside these ranges and needn't reach their ends.
Inputs may be any that keep to these rules, and one draw needn't show every extreme that they name: `panel_map`: row 0 is an index over brow+bcol (brow slowest), row 2 a local node below 2048. In each aligned block of 192 panels every group owns either no panel or exactly 12 of them, whose row 1 values are 0 to 11, each once. `element_nodes`: local node numbers within the element's own group. `element_matrix`: Symmetric.
All inputs are finite; a program needn't handle non-finite values.
Results may differ from the reference program's by a relative error of at most 0.0015.
The reference program's roundings to bfloat16 on the way (of `densities`, `loads` and `turned`) count: a program that leaves them out, or rounds other values in their place, can miss the bound.
Values may be sent and summed in bfloat16 or wider, within the bound.
No kernel may reach another device: no remote copies, remote signals or barrier semaphores. Data moves between devices by JAX's collectives and lax.ppermute only.
A program may use at most 128 MiB of HBM per device.

```python
import math
import jax
import jax.numpy as jnp
from jax import lax

RHS = 32
COLS = 64
PANEL_DEV = 192
PANELS = 6144
CAP = 12
NPE = 125
ELEM_DEV = 32
ELEMENTS = 1024
NODES_DEV = 2048
NODES = 65536
RIM = 128
SWEEPS = 3
ITERS = 2
DEVICES = 32


def draw_panel_map(key, part):
    blocks = PANELS // PANEL_DEV
    owners = PANEL_DEV // CAP
    key_bias, key_noise, key_order, key_node = jax.random.split(jax.random.fold_in(key, 11), 4)
    owner_bias = jax.random.permutation(key_bias, blocks).astype(jnp.int32)
    random_part = jax.random.randint(key_noise, (blocks, blocks), 0, blocks, dtype=jnp.int32)
    scores = (random_part + owner_bias[None, :]) * blocks + jnp.arange(blocks, dtype=jnp.int32)[None, :]
    values_top, chosen = lax.top_k(scores, owners)
    positions = jnp.arange(PANEL_DEV, dtype=jnp.int32)
    owner_seq = jnp.take(chosen.astype(jnp.int32), positions // CAP, axis=1)
    slot_seq = jnp.broadcast_to(positions % CAP, (blocks, PANEL_DEV))
    sort_keys = jax.random.randint(key_order, (blocks, PANEL_DEV), 0, PANEL_DEV, dtype=jnp.int32) * PANEL_DEV + positions[None, :]
    ordering = jnp.argsort(sort_keys, axis=1, stable=True)
    panel_owner = jnp.take_along_axis(owner_seq, ordering, axis=1).reshape(-1)
    panel_slot = jnp.take_along_axis(slot_seq, ordering, axis=1).reshape(-1)
    local_node = jax.random.randint(key_node, (PANELS,), 0, NODES_DEV, dtype=jnp.int32)
    return jnp.stack([panel_owner, panel_slot, local_node]).astype(jnp.int32)


def draw_element_matrix(key, part):
    key_off, key_diag = jax.random.split(jax.random.fold_in(key, 23))
    entries = jax.random.normal(key_off, (NPE, NPE), jnp.float32)
    coupling_part = (entries + entries.T) * (0.5 / math.sqrt(2.0 * NPE))
    diagonal_part = jax.random.uniform(key_diag, (NPE,), jnp.float32, 1.0, 2.0)
    return (coupling_part + jnp.diag(diagonal_part)).astype(jnp.float32)


def plant(values, stream_key, least, high):
    place = [jax.random.randint(jax.random.fold_in(stream_key, axis), (), 0, length) for axis, length in enumerate(values.shape)]
    main_axis = values.shape.index(max(values.shape))
    beside = place[:main_axis] + [(place[main_axis] + 1) % values.shape[main_axis]] + place[main_axis + 1:]
    return values.at[tuple(place)].set(least).at[tuple(beside)].set(high)


def level_of(key, extent, cuts, low, top_value):
    level = 1.0
    for position, blocks in cuts:
        heights = jax.random.uniform(jax.random.fold_in(jax.random.fold_in(key, 6), position), (blocks,), jnp.float32, low / len(cuts), top_value / len(cuts))
        level = level * jnp.repeat(jnp.exp(heights), extent[position] // blocks).reshape((-1,) + (1,) * (len(extent) - 1 - position))
    return level


def noise(rng, shape, deviation, bound, shards=(), kind=jnp.bfloat16):
    level = level_of(rng, shape, shards, -0.22, 0.18) if shards else 1.0
    values = jax.random.normal(rng, shape, jnp.float32) * deviation * level
    return jnp.minimum(jnp.maximum(values, -bound), bound).astype(kind)


def setup_inputs(seed: int = 0) -> dict:
    seeds = jax.random.split(jax.random.key(seed), 10)
    return {
        "panel_points": jnp.clip(1.0 * jax.random.uniform(seeds[0], (3, PANELS), jnp.float32) ** level_of(seeds[0], (3, PANELS), ((1, 32),), -0.2, 0.2), 0.0, 1.0).astype(jnp.bfloat16),
        "panel_map": draw_panel_map(jax.random.fold_in(seeds[9], 71), 0),
        "element_nodes": plant(jax.random.randint(seeds[2], (NPE, ELEMENTS), 0, NODES_DEV), jax.random.fold_in(seeds[2], 1), 0, NODES_DEV - 1).astype(jnp.int32),
        "element_coef": jnp.clip(jnp.exp(math.log(1.0) - 2.3025851 * jax.random.uniform(seeds[3], (ELEMENTS,), jnp.float32) ** level_of(seeds[3], (ELEMENTS,), ((0, 32),), -0.2, 0.2)), 0.1, 1.0),
        "element_matrix": draw_element_matrix(jax.random.fold_in(seeds[9], 71), 0),
        "node_mass": jnp.clip(2.0 + 2.0 * jax.random.uniform(seeds[5], (NODES,), jnp.float32) ** level_of(seeds[5], (NODES,), ((0, 32),), -0.2, 0.2), 2.0, 4.0),
        "forcing": noise(seeds[6], (COLS, NODES), 1.0, 6.0, ((1, 32),), jnp.float32),
        "field_start": noise(seeds[7], (COLS, NODES), 1.0, 6.0, ((1, 32),), jnp.float32),
        "potential_start": noise(seeds[8], (COLS, PANELS), 1.0, 6.0, ((1, 32),), jnp.float32),
    }


wave_number = 20.0
penalty = 0.5

def kernel_pair(sources, targets, count_all):
    src_xyz = sources.astype(jnp.float32)
    tgt_xyz = targets.astype(jnp.float32)
    delta_xyz = src_xyz[:, :, None] - tgt_xyz[:, None, :]
    dist_sq = lax.optimization_barrier(jnp.sum(delta_xyz * delta_xyz, axis=0))
    soften = 0.5 * float(count_all) ** (-1.0 / 3.0)
    radius = jnp.sqrt(dist_sq + soften * soften)
    scaling = 1.0 / (radius * math.sqrt(float(count_all)))
    real_tile = (jnp.cos(wave_number * radius) * scaling).astype(jnp.bfloat16)
    imag_tile = (jnp.sin(wave_number * radius) * scaling).astype(jnp.bfloat16)
    return (real_tile, imag_tile)

def bem_apply(densities, panel_points):
    turned = jnp.concatenate([-densities[RHS:], densities[:RHS]], axis=0).astype(jnp.float32)
    dense_full = densities.astype(jnp.float32)
    target_blocks = panel_points.reshape(3, DEVICES, PANEL_DEV).transpose(1, 0, 2)

    def one_block(targets):
        real_tile, imag_tile = kernel_pair(panel_points, targets, PANELS)
        first = jnp.dot(dense_full, real_tile.astype(jnp.float32), precision=lax.Precision.HIGHEST)
        second = jnp.dot(turned, imag_tile.astype(jnp.float32), precision=lax.Precision.HIGHEST)
        return first + second
    result = lax.map(one_block, target_blocks)
    return result.transpose(1, 0, 2).reshape(COLS, PANELS)

def operate(field_now, global_nodes, element_coef, element_matrix, node_mass):
    gathered = jnp.take(field_now, global_nodes, axis=1)
    stiffness = jnp.einsum('jk,cke->cje', element_matrix, gathered, precision=lax.Precision.HIGHEST) * element_coef
    result = node_mass * field_now + jnp.zeros_like(field_now).at[:, global_nodes].add(stiffness)
    shaped = field_now.reshape(COLS, DEVICES, NODES_DEV)
    zero_rim = jnp.zeros((COLS, 1, RIM), jnp.float32)
    from_left = jnp.concatenate([zero_rim, shaped[:, :-1, NODES_DEV - RIM:]], axis=1)
    from_right = jnp.concatenate([shaped[:, 1:, :RIM], zero_rim], axis=1)
    middle = jnp.zeros((COLS, DEVICES, NODES_DEV - 2 * RIM), jnp.float32)
    couple = jnp.concatenate([from_left, middle, from_right], axis=2).reshape(COLS, NODES)
    return result - penalty * couple

def reference(panel_points, panel_map, element_nodes, element_coef, element_matrix, node_mass, forcing, field_start, potential_start):
    panel_node = (panel_map[0] * NODES_DEV + panel_map[2]).astype(jnp.int32)
    group_base = (jnp.arange(ELEMENTS, dtype=jnp.int32) // ELEM_DEV * NODES_DEV).astype(jnp.int32)
    global_nodes = (element_nodes + group_base[None, :]).astype(jnp.int32)
    field_now = field_start
    potential_now = potential_start
    for turn_index in range(ITERS):
        densities = jnp.take(field_now, panel_node, axis=1).astype(jnp.bfloat16)
        loads = lax.optimization_barrier(potential_now.astype(jnp.bfloat16)).astype(jnp.float32)
        rhs = forcing + jnp.zeros_like(forcing).at[:, panel_node].add(loads)
        new_field = field_now
        for sweep in range(SWEEPS):
            weight = 1.0 / (1.25 + 0.75 * math.cos(math.pi * (2 * sweep + 1) / (2.0 * SWEEPS)))
            residual = rhs - operate(new_field, global_nodes, element_coef, element_matrix, node_mass)
            new_field = new_field + weight * residual / node_mass
        potential_now = bem_apply(densities, panel_points)
        field_now = new_field
    return (field_now, potential_now)
```

```python
import functools
import math

import jax
import jax.numpy as jnp
from jax import lax
from jax.experimental import pallas as pl
from jax.experimental.pallas import tpu as pltpu
from jax.sharding import PartitionSpec as P

RIM = 128
SWEEPS = 3
LANES = 128
SLOT_ROWS = 8
HALVES = 2

wave_number = 20.0
penalty = 0.5

AXES = ("brow", "bcol")
F32 = jnp.float32
BF16 = jnp.bfloat16

SIN_POLY = (3.14159264, -5.16771008, 2.55007752, -0.59829129, 0.07765766)
COS_POLY = (0.99999995, -4.93479283, 4.05841135, -1.33187657, 0.21968961)

VMEM_LIMIT = 56 * 1024 * 1024


def weight_of(sweep):
    return 1.0 / (1.25 + 0.75 * math.cos(math.pi * (2 * sweep + 1) / (2.0 * SWEEPS)))


def call(kernel, out_shape, cost, **more):
    return pl.pallas_call(
        kernel,
        out_shape=out_shape,
        compiler_params=pltpu.CompilerParams(vmem_limit_bytes=VMEM_LIMIT),
        cost_estimate=pl.CostEstimate(flops=cost, bytes_accessed=1 << 20, transcendentals=0),
        **more,
    )


def shape_of(shape, dtype):
    return jax.ShapeDtypeStruct(shape, dtype)


def dot(a, b):
    return jnp.dot(a, b, preferred_element_type=F32)


def dot_nt(a, b):
    return lax.dot_general(a, b, (((1,), (1,)), ((), ())), preferred_element_type=F32)


def split_two(value):
    high = value.astype(BF16)
    return high, (value - high.astype(F32)).astype(BF16)


def low_part(value, size):
    return value & (size - 1) if size & (size - 1) == 0 else value % size


def high_part(value, size):
    return value >> (size.bit_length() - 1) if size & (size - 1) == 0 else value // size


def stack_parts(value, parts):
    width = value.shape[1] // parts
    return jnp.concatenate([value[:, i * width : (i + 1) * width] for i in range(parts)], axis=0)


def one_hot_rows(key, rows):
    seen = lax.broadcasted_iota(jnp.int32, (rows, key.shape[1]), 0)
    return jnp.where(seen == key, 1.0, 0.0).astype(BF16)


def pick_part(stacked, part, parts):
    rows = stacked.shape[0] // parts
    picked = stacked[(parts - 1) * rows :]
    for i in reversed(range(parts - 1)):
        picked = jnp.where(part == i, stacked[i * rows : (i + 1) * rows], picked)
    return picked


def gather_nodes(field, nodes, parts):
    width = field.shape[1] // parts
    hot = one_hot_rows(jnp.where(nodes < 0, -1, low_part(nodes, width)), width)
    found = dot(stack_parts(field.astype(BF16), parts), hot)
    return pick_part(found, high_part(nodes, width), parts)


def scatter_nodes(values, nodes, parts, count):
    width = count // parts
    hot = one_hot_rows(jnp.where(nodes < 0, -1, low_part(nodes, width)), width)
    masked = jnp.concatenate(
        [jnp.where(high_part(nodes, width) == i, values, 0.0) for i in range(parts)], axis=0
    ).astype(BF16)
    added = dot_nt(masked, hot)
    rows = values.shape[0]
    return jnp.concatenate([added[i * rows : (i + 1) * rows] for i in range(parts)], axis=1)


def trace_rows(field, nodes, parts, brow):
    found = gather_nodes(field, nodes, parts)
    turned = jnp.transpose(found)
    span = turned.shape[0] // (HALVES * brow)
    pieces = []
    for r in range(brow):
        base = r * HALVES * span
        pieces.append(
            jnp.concatenate(
                [turned[base : base + span], turned[base + span : base + HALVES * span]], axis=1
            ).astype(BF16)
        )
    return pieces


def load_rows(potential, own_map, devices):
    owner, slot = own_map[0:1], own_map[1:2]
    half_rows = devices * SLOT_ROWS
    key = high_part(slot, SLOT_ROWS) * half_rows + owner * SLOT_ROWS + low_part(slot, SLOT_ROWS)
    rows = dot_nt(one_hot_rows(key, HALVES * half_rows), potential.astype(BF16))
    return jnp.concatenate([rows[:half_rows], rows[half_rows:]], axis=1)


def setup_kernel(
    parts, brow, bcol, panel_dev, rank_ref, map_ref, own_ref, field_ref, potential_ref, points_ref,
    nodes_ref, small_ref, trace_ref, rim_low_ref, rim_high_ref,
):
    rank = rank_ref[0]
    devices = brow * bcol
    row_panels = bcol * panel_dev
    row_slots = HALVES * bcol * SLOT_ROWS
    lane = lax.broadcasted_iota(jnp.int32, (1, row_panels), 1).astype(F32)
    block = jnp.floor((lane + 0.5) * (1.0 / panel_dev)).astype(jnp.int32)
    row_id = lax.broadcasted_iota(jnp.int32, (8, row_panels), 0)
    tables = []
    for r in range(brow):
        span = slice(r * row_panels, (r + 1) * row_panels)
        owner, slot, node = map_ref[0:1, span], map_ref[1:2, span], map_ref[2:3, span]
        key = high_part(slot, SLOT_ROWS) * (bcol * SLOT_ROWS) + block * SLOT_ROWS + low_part(slot, SLOT_ROWS)
        key = jnp.where(owner == rank, key, -1)
        hot = one_hot_rows(key, row_slots)
        values = jnp.where(
            row_id == 0, high_part(node, 256), jnp.where(row_id == 1, low_part(node, 256), 1)
        ).astype(F32).astype(BF16)
        found = dot_nt(values, hot)
        table = jnp.where(found[2:3] > 0.5, found[0:1] * 256.0 + found[1:2], -1.0)
        tables.append(table.astype(jnp.int32))
    nodes = jnp.concatenate(tables, axis=1)
    nodes_ref[...] = jnp.broadcast_to(nodes, nodes_ref.shape)
    field = field_ref[...]
    rim_low_ref[...] = field[:, :RIM].astype(BF16)
    rim_high_ref[...] = field[:, field.shape[1] - RIM :].astype(BF16)
    loads = load_rows(potential_ref[...], own_ref[...], devices)
    loads = loads.reshape(devices, SLOT_ROWS, LANES)
    points = jnp.broadcast_to(points_ref[...].astype(F32)[None], (devices, 8, LANES))
    small_ref[...] = jnp.concatenate([loads, points], axis=1).astype(BF16)
    write_traces(trace_rows(field, nodes, parts, brow), trace_ref, bcol)


def write_traces(pieces, trace_ref, bcol):
    for r, piece in enumerate(pieces):
        for c in range(bcol):
            trace_ref[r * bcol + c] = piece


def rim_correction(value, left_ref, right_ref, mass, weight):
    step = weight * penalty
    low = value[:, :RIM] + step * left_ref[...].astype(F32) / mass[:, :RIM]
    last = value.shape[1] - RIM
    high = value[:, last:] + step * right_ref[...].astype(F32) / mass[:, last:]
    return jnp.concatenate([low, value[:, RIM:last], high], axis=1)


def sweep_kernel(
    parts, weight, weight_before, group, coef_ref, field_ref, rhs_ref, mass_ref, keys_ref, matrix_ref,
    *more_refs,
):
    if weight_before is not None:
        left_ref, right_ref, *more_refs = more_refs
    (
        out_ref, field_scr, high_ref, low_ref, hot_ref, found_ref, local_ref, yhigh_ref, ylow_ref, sum_ref,
    ) = more_refs
    columns, count = field_ref.shape
    width = count // parts
    mass = mass_ref[...]
    if weight_before is None:
        field = field_ref[...]
    else:
        field = rim_correction(field_ref[...], left_ref, right_ref, mass, weight_before)
        field_scr[...] = field
    high, low = split_two(field)
    for h in range(parts):
        high_ref[h * columns : (h + 1) * columns] = high[:, h * width : (h + 1) * width]
        low_ref[h * columns : (h + 1) * columns] = low[:, h * width : (h + 1) * width]
    mat_high, mat_low = split_two(matrix_ref[...])
    matrix = jnp.concatenate(
        [
            jnp.concatenate([mat_high, mat_low], axis=1),
            jnp.concatenate([mat_high, jnp.zeros_like(mat_low)], axis=1),
        ],
        axis=0,
    )
    elements = keys_ref.shape[0]
    for start in range(0, elements, group):
        slot = (start // group) % 2
        hot = hot_ref.at[slot]
        found = found_ref.at[slot]
        for e in range(group):
            key = keys_ref[start + e : start + e + 1, :]
            hot[:, e * LANES : (e + 1) * LANES] = one_hot_rows(low_part(key, width), width)
        found[...] = dot(high_ref[...], hot[...]) + dot(low_ref[...], hot[...])
        for e in range(group):
            key = keys_ref[start + e : start + e + 1, :]
            got = pick_part(found[:, e * LANES : (e + 1) * LANES], high_part(key, width), parts)
            got_high, got_low = split_two(got)
            local_ref[e * columns : (e + 1) * columns, :LANES] = got_high
            local_ref[e * columns : (e + 1) * columns, LANES:] = got_low
        product = dot(local_ref[...], matrix)
        for e in range(group):
            key = keys_ref[start + e : start + e + 1, :]
            part = high_part(key, width)
            rows = product[e * columns : (e + 1) * columns]
            value = (rows[:, :LANES] + rows[:, LANES:]) * coef_ref[start + e]
            value_high, value_low = split_two(value)
            for h in range(parts):
                mask = jnp.where(part == h, 1.0, 0.0).astype(BF16)
                span = slice(e * LANES, (e + 1) * LANES)
                yhigh_ref[h * columns : (h + 1) * columns, span] = value_high * mask
                ylow_ref[h * columns : (h + 1) * columns, span] = value_low * mask
        added = dot_nt(yhigh_ref[...], hot[...]) + dot_nt(ylow_ref[...], hot[...])
        if start == 0:
            sum_ref[...] = added
        else:
            sum_ref[...] += added
    for h in range(parts):
        span = slice(h * width, (h + 1) * width)
        before = field_ref[:, span] if weight_before is None else field_scr[:, span]
        stiff = sum_ref[h * columns : (h + 1) * columns]
        out_ref[:, span] = (1.0 - weight) * before + weight * (
            rhs_ref[:, span] - stiff
        ) / mass[:, span]


def loads_kernel(
    parts, brow, weight, nodes_ref, loads_ref, forcing_ref, field_ref, left_ref, right_ref, mass_ref,
    rhs_ref, out_ref, rim_low_ref, rim_high_ref,
):
    nodes = nodes_ref[0:1, :]
    received = loads_ref[...].astype(F32)
    columns, count = field_ref.shape
    span = received.shape[0] // brow
    rows = []
    for r in range(brow):
        piece = received[r * span : (r + 1) * span]
        rows += [piece[:, :columns], piece[:, columns : HALVES * columns]]
    added = scatter_nodes(jnp.transpose(jnp.concatenate(rows, axis=0)), nodes, parts, count)
    rhs_ref[...] = forcing_ref[...] + added
    mass = mass_ref[...]
    field = field_ref[...] + weight * added / mass
    field = rim_correction(field, left_ref, right_ref, mass, weight)
    out_ref[...] = field
    rim_low_ref[...] = field[:, :RIM].astype(BF16)
    rim_high_ref[...] = field[:, count - RIM :].astype(BF16)


def finish_kernel(
    parts, brow, bcol, weight, nodes_ref, field_ref, left_ref, right_ref, mass_ref,
    out_ref, trace_ref, rim_low_ref, rim_high_ref,
):
    field = rim_correction(field_ref[...], left_ref, right_ref, mass_ref[...], weight)
    count = field.shape[1]
    out_ref[...] = field
    rim_low_ref[...] = field[:, :RIM].astype(BF16)
    rim_high_ref[...] = field[:, count - RIM :].astype(BF16)
    write_traces(trace_rows(field, nodes_ref[0:1, :], parts, brow), trace_ref, bcol)


def rim_kernel(
    weight, low_ref, high_ref, left_ref, right_ref, mass_low_ref, mass_high_ref, rim_low_ref, rim_high_ref
):
    step = weight * penalty
    rim_low_ref[...] = (low_ref[...] + step * left_ref[...].astype(F32) / mass_low_ref[...]).astype(BF16)
    rim_high_ref[...] = (
        high_ref[...] + step * right_ref[...].astype(F32) / mass_high_ref[...]
    ).astype(BF16)


def last_kernel(weight, field_ref, left_ref, right_ref, mass_ref, out_ref):
    out_ref[...] = rim_correction(field_ref[...], left_ref, right_ref, mass_ref[...], weight)


def tile_kernel(count_all, source_ref, target_ref, real_ref, imag_ref):
    soften = 0.5 * float(count_all) ** (-1.0 / 3.0)
    rows, cols = real_ref.shape
    step = 16
    for top in range(0, rows, step):
        squared = soften * soften
        for axis in range(3):
            delta = source_ref[top : top + step, axis : axis + 1] - target_ref[axis : axis + 1, :]
            squared = squared + delta * delta
        inverse = lax.rsqrt(squared)
        turns = (squared * inverse) * (wave_number / (2.0 * math.pi))
        turns = turns - jnp.floor(turns + 0.5)
        z = turns * turns
        sine = jnp.full_like(z, SIN_POLY[-1])
        for factor in SIN_POLY[-2::-1]:
            sine = sine * z + factor
        sine = sine * turns
        cosine = jnp.full_like(z, COS_POLY[-1])
        for factor in COS_POLY[-2::-1]:
            cosine = cosine * z + factor
        double = sine * (inverse * (2.0 / math.sqrt(float(count_all))))
        real_ref[top : top + step] = (
            inverse * (1.0 / math.sqrt(float(count_all))) - sine * double
        ).astype(BF16)
        imag_ref[top : top + step] = (cosine * double).astype(BF16)


def potential_kernel(pair, panel_dev, brow, map_ref, trace_ref, real_ref, imag_ref, out_ref, sum_ref):
    step = pl.program_id(0)
    owner, slot = map_ref[0:1, :], map_ref[1:2, :]
    panels = owner.shape[1]
    lane = lax.broadcasted_iota(jnp.int32, (1, panels), 1)
    inside = jnp.where(lane < panel_dev, 0, SLOT_ROWS)
    rows_each = pair * SLOT_ROWS
    key = owner * rows_each + inside + low_part(slot, SLOT_ROWS)
    half = high_part(slot, SLOT_ROWS)
    devices = trace_ref.shape[0]
    rows = trace_ref[...].astype(F32).reshape(devices * rows_each, LANES)
    turned_rows = jnp.transpose(rows).astype(BF16)
    found = dot(turned_rows, one_hot_rows(key, devices * rows_each))
    columns = LANES // HALVES
    density = jnp.where(half == 0, found[:columns], found[columns:])
    turned = jnp.concatenate([-density[columns // 2 :], density[: columns // 2]], axis=0)
    part = dot(density.astype(BF16), real_ref[...]) + dot(turned.astype(BF16), imag_ref[...])

    @pl.when(step == 0)
    def first():
        sum_ref[...] = part

    @pl.when(step > 0)
    def later():
        sum_ref[...] += part

    @pl.when(step == pl.num_programs(0) - 1)
    def write():
        for r in range(brow):
            out_ref[r] = sum_ref[:, r * panel_dev : (r + 1) * panel_dev]


def total(parts_ref):
    value = parts_ref[0]
    for r in range(1, parts_ref.shape[0]):
        value = value + parts_ref[r]
    return value


def send_loads_kernel(devices, own_ref, parts_ref, loads_ref):
    loads_ref[...] = load_rows(total(parts_ref), own_ref[...], devices).astype(BF16)


def sum_kernel(parts_ref, out_ref):
    out_ref[...] = total(parts_ref)


def exchange(rim_low, rim_high):
    count = lax.axis_size("brow") * lax.axis_size("bcol")
    forward = [(i, i + 1) for i in range(count - 1)]
    backward = [(target, source) for source, target in forward]
    low = lax.ppermute(rim_high, AXES, forward)
    high = lax.ppermute(rim_low, AXES, backward)
    return low, high


def swap_all(blocks):
    return lax.all_to_all(blocks, AXES, split_axis=0, concat_axis=0, tiled=True)


def per_device(
    panel_points,
    panel_map,
    element_nodes,
    element_coef,
    element_matrix,
    node_mass,
    forcing,
    field_start,
    potential_start,
):
    columns, panel_dev = potential_start.shape
    count = field_start.shape[1]
    brow, bcol = lax.axis_size("brow"), lax.axis_size("bcol")
    devices = brow * bcol
    count_all = panel_dev * devices
    capacity = max(2, 2 * panel_dev // devices)
    assert capacity <= HALVES * SLOT_ROWS and columns * HALVES == LANES
    parts = 256 // columns
    width = count // parts
    row_panels = bcol * panel_dev
    row_index, col_index = lax.axis_index("brow"), lax.axis_index("bcol")
    self_rank = row_index * bcol + col_index
    slots = HALVES * devices * SLOT_ROWS
    own_map = lax.dynamic_slice_in_dim(panel_map, self_rank * panel_dev, panel_dev, 1)
    row_map = lax.dynamic_slice_in_dim(panel_map, row_index * row_panels, row_panels, 1)
    point_rows = -(-panel_dev // LANES)
    assert 3 * point_rows <= 8
    points = jnp.pad(panel_points, ((0, 0), (0, point_rows * LANES - panel_dev)))
    points = points.reshape(3 * point_rows, LANES)
    points = jnp.pad(points, ((0, 8 - 3 * point_rows), (0, 0)))
    mass = node_mass.reshape(1, count)
    nodes_each, elements = element_nodes.shape
    keys = jnp.pad(element_nodes.T, ((0, 0), (0, LANES - nodes_each)))
    matrix = jnp.pad(element_matrix, ((0, LANES - nodes_each), (0, LANES - nodes_each)))
    smem = pl.BlockSpec(memory_space=pltpu.SMEM)
    vmem = pl.BlockSpec(memory_space=pltpu.VMEM)
    rim_shape = shape_of((columns, RIM), BF16)
    trace_shape = shape_of((devices, bcol * SLOT_ROWS, LANES), BF16)
    field_shape = shape_of((columns, count), F32)

    nodes, small, traces, *rim = call(
        functools.partial(setup_kernel, parts, brow, bcol, panel_dev),
        (shape_of((8, slots), jnp.int32), shape_of((devices, 16, LANES), BF16), trace_shape, rim_shape, rim_shape),
        2_000_000_000,
        in_specs=[smem] + [vmem] * 5,
        out_specs=(vmem,) * 5,
    )(self_rank.reshape(1), panel_map, own_map, field_start, potential_start, points)

    group = 8
    assert elements % group == 0

    def sweep(field, rhs, weight, halo=(), weight_before=None):
        rows = parts * columns
        return call(
            functools.partial(sweep_kernel, parts, weight, weight_before, group),
            field_shape,
            4_000_000_000,
            in_specs=[smem] + [vmem] * (5 + len(halo)),
            out_specs=vmem,
            scratch_shapes=[
                pltpu.VMEM((columns, count), F32),
                pltpu.VMEM((rows, width), BF16),
                pltpu.VMEM((rows, width), BF16),
                pltpu.VMEM((2, width, group * LANES), BF16),
                pltpu.VMEM((2, rows, group * LANES), F32),
                pltpu.VMEM((group * columns, 2 * LANES), BF16),
                pltpu.VMEM((rows, group * LANES), BF16),
                pltpu.VMEM((rows, group * LANES), BF16),
                pltpu.VMEM((rows, width), F32),
            ],
        )(element_coef, field, rhs, mass, keys, matrix, *halo)

    def rims(field, halo, weight):
        low = pl.BlockSpec((columns, RIM), lambda i: (0, 0))
        high = pl.BlockSpec((columns, RIM), lambda i: (0, count // RIM - 1))
        mass_low = pl.BlockSpec((1, RIM), lambda i: (0, 0))
        mass_high = pl.BlockSpec((1, RIM), lambda i: (0, count // RIM - 1))
        whole = pl.BlockSpec((columns, RIM), lambda i: (0, 0))
        return call(
            functools.partial(rim_kernel, weight),
            (rim_shape, rim_shape),
            100_000_000,
            grid=(1,),
            in_specs=[low, high, whole, whole, mass_low, mass_high],
            out_specs=(whole, whole),
        )(field, field, *halo, mass, mass)

    def add_loads(loads, field, halo, weight):
        return call(
            functools.partial(loads_kernel, parts, brow, weight),
            (field_shape, field_shape, rim_shape, rim_shape),
            500_000_000,
            in_specs=[vmem] * 7,
            out_specs=(vmem,) * 4,
        )(nodes, loads, forcing, field, *halo, mass)

    def potential_parts(traces_in, real_tile, imag_tile):
        pair = 2
        rows = pair * panel_dev
        return call(
            functools.partial(potential_kernel, pair, panel_dev, brow),
            shape_of((brow, columns, panel_dev), F32),
            2_000_000_000,
            grid=(bcol // pair,),
            in_specs=[
                pl.BlockSpec((3, rows), lambda i: (0, i)),
                pl.BlockSpec((devices, pair * SLOT_ROWS, LANES), lambda i: (0, i, 0)),
                pl.BlockSpec((rows, brow * panel_dev), lambda i: (i, 0)),
                pl.BlockSpec((rows, brow * panel_dev), lambda i: (i, 0)),
            ],
            out_specs=pl.BlockSpec((brow, columns, panel_dev), lambda i: (0, 0, 0)),
            scratch_shapes=[pltpu.VMEM((columns, brow * panel_dev), F32)],
        )(row_map, traces_in, real_tile, imag_tile)

    weights = [weight_of(sweep_index) for sweep_index in range(SWEEPS)]

    halo = exchange(*rim)
    small_in = swap_all(small)
    traces_in = swap_all(traces)
    field = sweep(field_start, forcing, weights[0])
    loads_in = small_in[:, :SLOT_ROWS].reshape(devices * SLOT_ROWS, LANES)
    all_points = small_in[:, SLOT_ROWS : SLOT_ROWS + 3 * point_rows].astype(F32)
    all_points = all_points.reshape(brow, bcol, 3, point_rows * LANES)[..., :panel_dev]
    source_points = lax.dynamic_index_in_dim(all_points, row_index, 0, keepdims=False)
    source_points = source_points.transpose(0, 2, 1).reshape(row_panels, 3)
    target_points = lax.dynamic_index_in_dim(all_points, col_index, 1, keepdims=False)
    target_points = target_points.transpose(1, 0, 2).reshape(3, brow * panel_dev)
    tile_rows = row_panels // bcol
    tile_shape = shape_of((row_panels, brow * panel_dev), BF16)
    tile_spec = pl.BlockSpec((tile_rows, brow * panel_dev), lambda i: (i, 0))
    real_tile, imag_tile = call(
        functools.partial(tile_kernel, count_all),
        (tile_shape, tile_shape),
        8_000_000_000,
        grid=(bcol,),
        in_specs=[
            pl.BlockSpec((tile_rows, 3), lambda i: (i, 0)),
            pl.BlockSpec((3, brow * panel_dev), lambda i: (0, 0)),
        ],
        out_specs=(tile_spec, tile_spec),
    )(source_points, target_points)
    rhs, field, *rim = add_loads(loads_in, field, halo, weights[0])
    halo = exchange(*rim)
    field = sweep(field, rhs, weights[1])
    parts_out = lax.all_to_all(
        potential_parts(traces_in, real_tile, imag_tile), "brow", split_axis=0, concat_axis=0, tiled=True
    )
    halo_now = exchange(*rims(field, halo, weights[1]))
    field = sweep(field, rhs, weights[2], halo, weights[1])
    loads_out = call(
        functools.partial(send_loads_kernel, devices),
        shape_of((devices * SLOT_ROWS, LANES), BF16),
        100_000_000,
        in_specs=[vmem, vmem],
        out_specs=vmem,
    )(own_map, parts_out)
    loads_in = swap_all(loads_out.reshape(devices, SLOT_ROWS, LANES)).reshape(
        devices * SLOT_ROWS, LANES
    )
    field, traces, *rim = call(
        functools.partial(finish_kernel, parts, brow, bcol, weights[2]),
        (field_shape, trace_shape, rim_shape, rim_shape),
        500_000_000,
        in_specs=[vmem] * 5,
        out_specs=(vmem,) * 4,
    )(nodes, field, *halo_now, mass)

    traces_in = swap_all(traces)
    halo = exchange(*rim)
    field = sweep(field, forcing, weights[0])
    rhs, field, *rim = add_loads(loads_in, field, halo, weights[0])
    halo = exchange(*rim)
    field = sweep(field, rhs, weights[1])
    halo_now = exchange(*rims(field, halo, weights[1]))
    parts_out = lax.all_to_all(
        potential_parts(traces_in, real_tile, imag_tile), "brow", split_axis=0, concat_axis=0, tiled=True
    )
    field = sweep(field, rhs, weights[2], halo, weights[1])
    field = call(
        functools.partial(last_kernel, weights[2]),
        field_shape,
        100_000_000,
        in_specs=[vmem] * 4,
        out_specs=vmem,
    )(field, *halo_now, mass)
    potential = call(
        sum_kernel, shape_of((columns, panel_dev), F32), 1_000_000, in_specs=[vmem], out_specs=vmem
    )(parts_out)
    return (field, potential)


def solution(mesh):
    placed = (
        P(None, AXES),
        P(),
        P(None, AXES),
        P(AXES),
        P(),
        P(AXES),
        P(None, AXES),
        P(None, AXES),
        P(None, AXES),
    )
    return jax.shard_map(
        per_device,
        mesh=mesh,
        in_specs=placed,
        out_specs=(P(None, AXES), P(None, AXES)),
        check_vma=False,
    )
```

```python
import functools
import math

import jax
import jax.numpy as jnp
from jax import lax
from jax.experimental import pallas as pl
from jax.experimental.pallas import tpu as pltpu
from jax.sharding import PartitionSpec as P

RIM = 128
SWEEPS = 3
LANES = 128
LOAD_ROWS = 8
POINT_ROWS = 8
HALVES = 2
GROUP = 8
BLOCKS = 4

wave_number = 20.0
penalty = 0.5

AXES = ("brow", "bcol")
F32 = jnp.float32
BF16 = jnp.bfloat16

SIN_POLY = (3.14159264, -5.16771008, 2.55007752, -0.59829129, 0.07765766)
COS_POLY = (0.99999995, -4.93479283, 4.05841135, -1.33187657, 0.21968961)

MIB = 1024 * 1024


def weight_of(sweep):
    return 1.0 / (1.25 + 0.75 * math.cos(math.pi * (2 * sweep + 1) / (2.0 * SWEEPS)))


def call(kernel, out_shape, cost, limit=16, **more):
    return pl.pallas_call(
        kernel,
        out_shape=out_shape,
        compiler_params=pltpu.CompilerParams(vmem_limit_bytes=limit * MIB),
        cost_estimate=pl.CostEstimate(flops=cost, bytes_accessed=1 << 20, transcendentals=0),
        **more,
    )


def shape_of(shape, dtype):
    return jax.ShapeDtypeStruct(shape, dtype)


def dot(a, b):
    return jnp.dot(a, b, preferred_element_type=F32)


def dot_nt(a, b):
    return lax.dot_general(a, b, (((1,), (1,)), ((), ())), preferred_element_type=F32)


def split_two(value):
    high = value.astype(BF16)
    return high, (value - high.astype(F32)).astype(BF16)


def low_part(value, size):
    return value & (size - 1) if size & (size - 1) == 0 else value % size


def high_part(value, size):
    return value >> (size.bit_length() - 1) if size & (size - 1) == 0 else value // size


def stack_parts(value, parts):
    width = value.shape[1] // parts
    return jnp.concatenate([value[:, i * width : (i + 1) * width] for i in range(parts)], axis=0)


def one_hot_rows(key, rows):
    seen = lax.broadcasted_iota(jnp.int32, (rows, key.shape[1]), 0)
    return jnp.where(seen == key, 1.0, 0.0).astype(BF16)


def pick_part(stacked, part, parts):
    rows = stacked.shape[0] // parts
    picked = stacked[(parts - 1) * rows :]
    for i in reversed(range(parts - 1)):
        picked = jnp.where(part == i, stacked[i * rows : (i + 1) * rows], picked)
    return picked


def gather_nodes(field, nodes, parts):
    width = field.shape[1] // parts
    hot = one_hot_rows(jnp.where(nodes < 0, -1, low_part(nodes, width)), width)
    found = dot(stack_parts(field.astype(BF16), parts), hot)
    return pick_part(found, high_part(nodes, width), parts)


def scatter_nodes(values, nodes, parts, count):
    width = count // parts
    hot = one_hot_rows(jnp.where(nodes < 0, -1, low_part(nodes, width)), width)
    masked = jnp.concatenate(
        [jnp.where(high_part(nodes, width) == i, values, 0.0) for i in range(parts)], axis=0
    ).astype(BF16)
    added = dot_nt(masked, hot)
    rows = values.shape[0]
    return jnp.concatenate([added[i * rows : (i + 1) * rows] for i in range(parts)], axis=1)


def halves_of(slot, rows):
    half = jnp.where(slot >= rows, 1, 0)
    return half, slot - half * rows


def trace_rows(field, nodes, parts, brow, used):
    turned = jnp.transpose(gather_nodes(field, nodes, parts))
    span = turned.shape[0] // brow
    return [
        jnp.concatenate(
            [turned[r * span : r * span + used], turned[r * span + used : r * span + 2 * used]], axis=1
        )
        for r in range(brow)
    ]


def own_panels(map_ref, rank, panel_dev):
    first = rank * panel_dev
    base = (first >> 7) << 7
    window = -(-panel_dev // LANES) * LANES
    near = map_ref[:, pl.ds(pl.multiple_of(base, LANES), window)]
    return jnp.where(first == base, near[:, :panel_dev], near[:, window - panel_dev :])


def load_rows(potential, own_map, devices, slot_rows):
    owner, slot = own_map[0:1], own_map[1:2]
    half, low = halves_of(slot, slot_rows)
    rows = devices * LOAD_ROWS
    key = half * rows + owner * LOAD_ROWS + low
    found = dot_nt(one_hot_rows(key, HALVES * rows), potential.astype(BF16))
    return jnp.concatenate([found[:rows], found[rows:]], axis=1).reshape(devices, LOAD_ROWS, LANES)


def node_tables(map_ref, rank, brow, bcol, panel_dev, slot_rows, stride):
    row_panels = bcol * panel_dev
    row_slots = -(-HALVES * bcol * stride // LANES) * LANES
    lane = lax.broadcasted_iota(jnp.int32, (1, row_panels), 1).astype(F32)
    block = jnp.floor((lane + 0.5) * (1.0 / panel_dev)).astype(jnp.int32)
    row_id = lax.broadcasted_iota(jnp.int32, (8, row_panels), 0)
    tables = []
    for r in range(brow):
        span = slice(r * row_panels, (r + 1) * row_panels)
        owner, slot, node = map_ref[0:1, span], map_ref[1:2, span], map_ref[2:3, span]
        half, low = halves_of(slot, slot_rows)
        key = jnp.where(owner == rank, half * (bcol * stride) + block * stride + low, -1)
        values = jnp.where(
            row_id == 0, high_part(node, 256), jnp.where(row_id == 1, low_part(node, 256), 1)
        ).astype(F32).astype(BF16)
        found = dot_nt(values, one_hot_rows(key, row_slots))
        table = jnp.where(found[2:3] > 0.5, found[0:1] * 256.0 + found[1:2], -1.0)
        tables.append(table.astype(jnp.int32))
    return jnp.concatenate(tables, axis=1)


def point_rows(points):
    row_id = lax.broadcasted_iota(jnp.int32, (POINT_ROWS, LANES), 0)
    each = POINT_ROWS // 3
    width = points.shape[1]
    value = jnp.zeros((POINT_ROWS, LANES), F32)
    for axis in range(3):
        for part in range(-(-width // LANES)):
            piece = points[axis : axis + 1, part * LANES : (part + 1) * LANES]
            short = LANES - piece.shape[1]
            if short:
                piece = jnp.concatenate([piece, jnp.zeros((1, short), F32)], axis=1)
            value = jnp.where(row_id == axis * each + part, piece, value)
    return value


def write_chunks(chunk_ref, pieces, loads, bcol, points=None):
    used = pieces[0].shape[0]
    for r, piece in enumerate(pieces):
        for c in range(bcol):
            device = r * bcol + c
            rows = [piece, loads[device]] + ([] if points is None else [points])
            left = chunk_ref.shape[1] - used - LOAD_ROWS - (0 if points is None else POINT_ROWS)
            if left:
                rows.append(jnp.zeros((left, LANES), F32))
            chunk_ref[device] = jnp.concatenate(rows, axis=0).astype(BF16)


def write_rims(field, even, first_ref, second_ref):
    low = field[:, :RIM]
    high = field[:, field.shape[1] - RIM :]
    first_ref[...] = jnp.where(even, high, low).astype(BF16)
    second_ref[...] = jnp.where(even, low, high).astype(BF16)


def setup_kernel(
    parts, brow, bcol, panel_dev, slot_rows, rank_ref, map_ref, field_ref, potential_ref, points_ref,
    nodes_ref, load_nodes_ref, chunk_ref, rim_first_ref, rim_second_ref,
):
    rank = rank_ref[0]
    tables = functools.partial(node_tables, map_ref, rank, brow, bcol, panel_dev, slot_rows)
    nodes = tables(slot_rows)
    nodes_ref[...] = jnp.broadcast_to(nodes, nodes_ref.shape)
    load_nodes_ref[...] = jnp.broadcast_to(tables(LOAD_ROWS), load_nodes_ref.shape)
    field = field_ref[...]
    write_rims(field, low_part(rank, 2) == 0, rim_first_ref, rim_second_ref)
    loads = load_rows(
        potential_ref[...], own_panels(map_ref, rank, panel_dev), brow * bcol, slot_rows
    )
    pieces = trace_rows(field, nodes, parts, brow, bcol * slot_rows)
    write_chunks(chunk_ref, pieces, loads, bcol, point_rows(points_ref[...].astype(F32)))


def hot_kernel(keys_ref, nodes_hot_ref):
    width = nodes_hot_ref.shape[0]
    for e in range(keys_ref.shape[0]):
        key = keys_ref[e : e + 1, :]
        nodes_hot_ref[:, e * LANES : (e + 1) * LANES] = one_hot_rows(low_part(key, width), width)


def rim_correction(value, even, first_ref, second_ref, mass, weight):
    step = weight * penalty
    first, second = first_ref[...].astype(F32), second_ref[...].astype(F32)
    left, right = jnp.where(even, second, first), jnp.where(even, first, second)
    last = value.shape[1] - RIM
    low = value[:, :RIM] + step * left / mass[:, :RIM]
    high = value[:, last:] + step * right / mass[:, last:]
    return jnp.concatenate([low, value[:, RIM:last], high], axis=1)


def received_loads(chunk_ref, used, brow, columns):
    received = chunk_ref[...].astype(F32)[:, used : used + LOAD_ROWS]
    received = received.reshape(received.shape[0] * LOAD_ROWS, LANES)
    span = received.shape[0] // brow
    rows = []
    for r in range(brow):
        piece = received[r * span : (r + 1) * span]
        rows += [piece[:, :columns], piece[:, columns : HALVES * columns]]
    return jnp.transpose(jnp.concatenate(rows, axis=0))


def sweep_kernel(
    parts, weight, weight_before, brow, used, rank_ref, coef_ref, field_ref, rhs_ref, mass_ref, keys_ref,
    matrix_ref, hot_ref, *more_refs,
):
    if weight_before is not None:
        first_ref, second_ref, out_ref, field_scr, *scratch = more_refs
    else:
        chunk_ref, nodes_ref, out_ref, total_ref, *scratch = more_refs
    high_ref, low_ref, found_ref, local_ref, yhigh_ref, ylow_ref, sum_ref = scratch
    columns, count = field_ref.shape
    width = count // parts
    mass = mass_ref[...]
    if weight_before is None:
        field = field_ref[...]
        loads = received_loads(chunk_ref, used, brow, columns)
        total_ref[...] = rhs_ref[...] + scatter_nodes(loads, nodes_ref[0:1, :], parts, count)
        rhs_now, field_now = total_ref, field_ref
    else:
        even = low_part(rank_ref[0], 2) == 0
        field = rim_correction(field_ref[...], even, first_ref, second_ref, mass, weight_before)
        field_scr[...] = field
        rhs_now, field_now = rhs_ref, field_scr
    high, low = split_two(field)
    for h in range(parts):
        high_ref[h * columns : (h + 1) * columns] = high[:, h * width : (h + 1) * width]
        low_ref[h * columns : (h + 1) * columns] = low[:, h * width : (h + 1) * width]
    mat_high, mat_low = split_two(matrix_ref[...])
    matrix = jnp.concatenate(
        [
            jnp.concatenate([mat_high, mat_low], axis=1),
            jnp.concatenate([mat_high, jnp.zeros_like(mat_low)], axis=1),
        ],
        axis=0,
    )
    groups = keys_ref.shape[0] // GROUP
    lanes = GROUP * LANES

    def gather(group):
        hot = hot_ref[:, group * lanes : (group + 1) * lanes]
        found_ref[group % 2] = dot(high_ref[...], hot) + dot(low_ref[...], hot)

    def multiply(group):
        slot = group % 2
        for e in range(GROUP):
            element = group * GROUP + e
            key = keys_ref[element : element + 1, :]
            got = pick_part(found_ref[slot, :, e * LANES : (e + 1) * LANES], high_part(key, width), parts)
            got_high, got_low = split_two(got)
            local_ref[slot, e * columns : (e + 1) * columns, :LANES] = got_high
            local_ref[slot, e * columns : (e + 1) * columns, LANES:] = got_low
        product = dot(local_ref[slot], matrix)
        for e in range(GROUP):
            element = group * GROUP + e
            part = high_part(keys_ref[element : element + 1, :], width)
            rows = product[e * columns : (e + 1) * columns]
            value = (rows[:, :LANES] + rows[:, LANES:]) * coef_ref[element]
            value_high, value_low = split_two(value)
            span = slice(e * LANES, (e + 1) * LANES)
            for h in range(parts):
                mask = jnp.where(part == h, 1.0, 0.0).astype(BF16)
                yhigh_ref[slot, h * columns : (h + 1) * columns, span] = value_high * mask
                ylow_ref[slot, h * columns : (h + 1) * columns, span] = value_low * mask

    def scatter(group):
        hot = hot_ref[:, group * lanes : (group + 1) * lanes]
        added = dot_nt(yhigh_ref[group % 2], hot) + dot_nt(ylow_ref[group % 2], hot)
        sum_ref[...] = added if group == 0 else sum_ref[...] + added

    gather(0)
    for group in range(groups):
        if group + 1 < groups:
            gather(group + 1)
        multiply(group)
        scatter(group)
    for h in range(parts):
        span = slice(h * width, (h + 1) * width)
        stiff = sum_ref[h * columns : (h + 1) * columns]
        out_ref[:, span] = (1.0 - weight) * field_now[:, span] + weight * (
            rhs_now[:, span] - stiff
        ) / mass[:, span]


def finish_kernel(
    parts, brow, bcol, panel_dev, slot_rows, weight, rank_ref, map_ref, nodes_ref, field_ref,
    first_ref, second_ref, mass_ref, potential_ref, out_ref, chunk_ref, rim_first_ref, rim_second_ref,
):
    rank = rank_ref[0]
    even = low_part(rank, 2) == 0
    field = rim_correction(field_ref[...], even, first_ref, second_ref, mass_ref[...], weight)
    out_ref[...] = field
    write_rims(field, even, rim_first_ref, rim_second_ref)
    loads = load_rows(
        potential_ref[...], own_panels(map_ref, rank, panel_dev), brow * bcol, slot_rows
    )
    pieces = trace_rows(field, nodes_ref[0:1, :], parts, brow, bcol * slot_rows)
    write_chunks(chunk_ref, pieces, loads, bcol)


def last_kernel(weight, rank_ref, field_ref, first_ref, second_ref, mass_ref, out_ref):
    even = low_part(rank_ref[0], 2) == 0
    out_ref[...] = rim_correction(field_ref[...], even, first_ref, second_ref, mass_ref[...], weight)


def tile_kernel(brow, bcol, panel_dev, used, place_ref, chunk_ref, real_ref, imag_ref, target_ref):
    count_all = brow * bcol * panel_dev
    soften = 0.5 * float(count_all) ** (-1.0 / 3.0)
    each = POINT_ROWS // 3
    row_index, col_index = place_ref[0], place_ref[1]
    start = used + LOAD_ROWS

    def points_of(device):
        return chunk_ref[device].astype(F32)[start : start + POINT_ROWS]

    @pl.when(pl.program_id(0) == 0)
    def targets():
        near = [points_of(r * bcol + col_index) for r in range(brow)]
        for axis in range(3):
            rows = []
            for piece in near:
                for part in range(each):
                    width = min(LANES, panel_dev - part * LANES)
                    rows.append(piece[axis * each + part : axis * each + part + 1, :width])
            target_ref[axis : axis + 1, :] = jnp.concatenate(rows, axis=1)

    source = jnp.transpose(points_of(row_index * bcol + pl.program_id(0)))
    step = 16
    for top in range(0, panel_dev, step):
        part, first = top // LANES, top % LANES
        squared = soften * soften
        for axis in range(3):
            column = source[first : first + step, axis * each + part : axis * each + part + 1]
            delta = column - target_ref[axis : axis + 1, :]
            squared = squared + delta * delta
        inverse = lax.rsqrt(squared)
        turns = (squared * inverse) * (wave_number / (2.0 * math.pi))
        turns = turns - jnp.floor(turns + 0.5)
        z = turns * turns
        sine = jnp.full_like(z, SIN_POLY[-1])
        for factor in SIN_POLY[-2::-1]:
            sine = sine * z + factor
        sine = sine * turns
        cosine = jnp.full_like(z, COS_POLY[-1])
        for factor in COS_POLY[-2::-1]:
            cosine = cosine * z + factor
        double = sine * (inverse * (2.0 / math.sqrt(float(count_all))))
        real_ref[top : top + step] = (
            inverse * (1.0 / math.sqrt(float(count_all))) - sine * double
        ).astype(BF16)
        imag_ref[top : top + step] = (cosine * double).astype(BF16)


def potential_kernel(
    brow, bcol, panel_dev, slot_rows, place_ref, map_ref, chunk_ref, real_ref, imag_ref, out_ref,
):
    row_panels = bcol * panel_dev
    base = pl.multiple_of(place_ref[0] * row_panels, LANES)
    devices = brow * bcol
    columns = LANES // HALVES
    rows = BLOCKS * slot_rows
    panels = BLOCKS * panel_dev
    lane = lax.broadcasted_iota(jnp.int32, (1, panels), 1).astype(F32)
    block = jnp.floor((lane + 0.5) * (1.0 / panel_dev)).astype(jnp.int32)
    traces = chunk_ref[...].astype(F32)
    total = None
    for group in range(bcol // BLOCKS):
        span = pl.ds(base + group * panels, panels)
        owner, slot = map_ref[0:1, span], map_ref[1:2, span]
        half, low = halves_of(slot, slot_rows)
        key = owner * rows + block * slot_rows + low
        near = traces[:, group * rows : (group + 1) * rows].reshape(devices * rows, LANES)
        found = dot(jnp.transpose(near).astype(BF16), one_hot_rows(key, devices * rows))
        density = jnp.where(half == 0, found[:columns], found[columns:])
        turned = jnp.concatenate([-density[columns // 2 :], density[: columns // 2]], axis=0)
        here = slice(group * panels, (group + 1) * panels)
        part = dot(density.astype(BF16), real_ref[here]) + dot(turned.astype(BF16), imag_ref[here])
        total = part if total is None else total + part
    for r in range(brow):
        out_ref[r] = total[:, r * panel_dev : (r + 1) * panel_dev]


def per_device(
    panel_points,
    panel_map,
    element_nodes,
    element_coef,
    element_matrix,
    node_mass,
    forcing,
    field_start,
    potential_start,
):
    columns, panel_dev = potential_start.shape
    count = field_start.shape[1]
    brow, bcol = lax.axis_size("brow"), lax.axis_size("bcol")
    devices = brow * bcol
    capacity = max(2, 2 * panel_dev // devices)
    slot_rows = -(-capacity // HALVES)
    used = bcol * slot_rows
    assert slot_rows <= LOAD_ROWS and columns * HALVES == LANES and bcol % BLOCKS == 0
    parts = 256 // columns
    width = count // parts
    row_panels = bcol * panel_dev
    row_index, col_index = lax.axis_index("brow"), lax.axis_index("bcol")
    rank = (row_index * bcol + col_index).reshape(1)
    place = jnp.stack([row_index, col_index])
    mass = node_mass.reshape(1, count)
    nodes_each, elements = element_nodes.shape
    assert elements % GROUP == 0
    keys = jnp.pad(element_nodes.T, ((0, 0), (0, LANES - nodes_each)))
    matrix = jnp.pad(element_matrix, ((0, LANES - nodes_each), (0, LANES - nodes_each)))
    smem = pl.BlockSpec(memory_space=pltpu.SMEM)
    vmem = pl.BlockSpec(memory_space=pltpu.VMEM)
    rim_shape = shape_of((columns, RIM), BF16)
    field_shape = shape_of((columns, count), F32)
    weights = [weight_of(sweep_index) for sweep_index in range(SWEEPS)]
    even_pairs = [(i, i ^ 1) for i in range(devices)]
    odd_pairs = [pair for i in range(1, devices - 1, 2) for pair in ((i, i + 1), (i + 1, i))]
    even = (rank[0] & 1) == 0

    def chunk_shape(rows, unit):
        return shape_of((devices, -(-rows // unit) * unit, LANES), BF16)

    def table_shape(stride):
        return shape_of((8, brow * (-(-HALVES * bcol * stride // LANES) * LANES)), jnp.int32)

    def exchange(first, second):
        return lax.ppermute(first, AXES, even_pairs), lax.ppermute(second, AXES, odd_pairs)

    def rims(field, halo, weight):
        first, second = (piece.astype(F32) for piece in halo)
        left, right = jnp.where(even, second, first), jnp.where(even, first, second)
        last = count - RIM
        low = field[:, :RIM] + (weight * penalty) * left / mass[:, :RIM]
        high = field[:, last:] + (weight * penalty) * right / mass[:, last:]
        return jnp.where(even, high, low).astype(BF16), jnp.where(even, low, high).astype(BF16)

    def swap_all(chunks):
        return lax.all_to_all(chunks, AXES, split_axis=0, concat_axis=0, tiled=True)

    def sweep(field, rhs, weight, more, weight_before=None):
        rows = parts * columns
        lanes = GROUP * LANES
        first = weight_before is None
        return call(
            functools.partial(sweep_kernel, parts, weight, weight_before, brow, used),
            (field_shape, field_shape) if first else field_shape,
            5_000_000_000,
            limit=24,
            in_specs=[smem, smem] + [vmem] * 8,
            out_specs=(vmem, vmem) if first else vmem,
            scratch_shapes=([] if first else [pltpu.VMEM((columns, count), F32)])
            + [
                pltpu.VMEM((rows, width), BF16),
                pltpu.VMEM((rows, width), BF16),
                pltpu.VMEM((2, rows, lanes), F32),
                pltpu.VMEM((2, GROUP * columns, 2 * LANES), BF16),
                pltpu.VMEM((2, rows, lanes), BF16),
                pltpu.VMEM((2, rows, lanes), BF16),
                pltpu.VMEM((rows, width), F32),
            ],
        )(rank, element_coef, field, rhs, mass, keys, matrix, hot, *more)

    def potential_parts(chunks, real_tile, imag_tile):
        tile_mib = -(-(4 * real_tile.size) // MIB)
        parts_out = call(
            functools.partial(potential_kernel, brow, bcol, panel_dev, slot_rows),
            shape_of((brow, columns, panel_dev), F32),
            2_000_000_000,
            limit=12 + tile_mib,
            in_specs=[smem] + [vmem] * 4,
            out_specs=vmem,
        )(place, panel_map, chunks, real_tile, imag_tile)
        return parts_out

    def sum_parts(parts_out):
        return lax.psum_scatter(parts_out, "brow", scatter_dimension=0, tiled=False)

    nodes, load_nodes, chunks, *rim = call(
        functools.partial(setup_kernel, parts, brow, bcol, panel_dev, slot_rows),
        (
            table_shape(slot_rows),
            table_shape(LOAD_ROWS),
            chunk_shape(used + LOAD_ROWS + POINT_ROWS, 16),
            rim_shape,
            rim_shape,
        ),
        2_000_000_000,
        in_specs=[smem] + [vmem] * 4,
        out_specs=(vmem,) * 5,
    )(rank, panel_map, field_start, potential_start, panel_points)
    hot = call(
        hot_kernel,
        shape_of((width, elements * LANES), BF16),
        1_000_000_000,
        in_specs=[vmem],
        out_specs=vmem,
    )(keys)
    halo = exchange(*rim)
    chunks = swap_all(chunks)
    field, rhs = sweep(field_start, forcing, weights[0], (chunks, load_nodes))
    tile_shape = shape_of((row_panels, brow * panel_dev), BF16)
    tile_spec = pl.BlockSpec((panel_dev, brow * panel_dev), lambda i: (i, 0))
    real_tile, imag_tile = call(
        functools.partial(tile_kernel, brow, bcol, panel_dev, used),
        (tile_shape, tile_shape),
        8_000_000_000,
        grid=(bcol,),
        in_specs=[smem, vmem],
        out_specs=(tile_spec, tile_spec),
        scratch_shapes=[pltpu.VMEM((8, brow * panel_dev), F32)],
    )(place, chunks)
    potential = sum_parts(potential_parts(chunks, real_tile, imag_tile))
    halo_next = exchange(*rims(field, halo, weights[0]))
    field = sweep(field, rhs, weights[1], halo, weights[0])
    halo, halo_next = halo_next, exchange(*rims(field, halo_next, weights[1]))
    field = sweep(field, rhs, weights[2], halo, weights[1])
    field, chunks, *rim = call(
        functools.partial(finish_kernel, parts, brow, bcol, panel_dev, slot_rows, weights[2]),
        (field_shape, chunk_shape(used + LOAD_ROWS, 8), rim_shape, rim_shape),
        1_000_000_000,
        in_specs=[smem] + [vmem] * 7,
        out_specs=(vmem,) * 4,
    )(rank, panel_map, nodes, field, *halo_next, mass, potential)

    halo = exchange(*rim)
    chunks = swap_all(chunks)
    parts_out = potential_parts(chunks, real_tile, imag_tile)
    parts_out, field = lax.optimization_barrier((parts_out, field))
    potential = sum_parts(parts_out)
    field, rhs = sweep(field, forcing, weights[0], (chunks, load_nodes))
    halo_next = exchange(*rims(field, halo, weights[0]))
    field = sweep(field, rhs, weights[1], halo, weights[0])
    halo, halo_next = halo_next, exchange(*rims(field, halo_next, weights[1]))
    field = sweep(field, rhs, weights[2], halo, weights[1])
    field = call(
        functools.partial(last_kernel, weights[2]),
        field_shape,
        100_000_000,
        in_specs=[smem] + [vmem] * 4,
        out_specs=vmem,
    )(rank, field, *halo_next, mass)
    return (field, potential)


def solution(mesh):
    placed = (
        P(None, AXES),
        P(),
        P(None, AXES),
        P(AXES),
        P(),
        P(AXES),
        P(None, AXES),
        P(None, AXES),
        P(None, AXES),
    )
    return jax.shard_map(
        per_device,
        mesh=mesh,
        in_specs=placed,
        out_specs=(P(None, AXES), P(None, AXES)),
        check_vma=False,
    )
```

```python
import functools
import math

import jax
import jax.numpy as jnp
from jax import lax
from jax.experimental import pallas as pl
from jax.experimental.pallas import tpu as pltpu
from jax.sharding import PartitionSpec as P

RIM = 128
SWEEPS = 3
LANES = 128
LOAD_ROWS = 8
POINT_ROWS = 8
HALVES = 2
GROUP = 4
BLOCKS = 4

wave_number = 20.0
penalty = 0.5

AXES = ("brow", "bcol")
F32 = jnp.float32
BF16 = jnp.bfloat16

SIN_POLY = (3.14159264, -5.16771008, 2.55007752, -0.59829129, 0.07765766)
COS_POLY = (0.99999995, -4.93479283, 4.05841135, -1.33187657, 0.21968961)

MIB = 1024 * 1024


def weight_of(sweep):
    return 1.0 / (1.25 + 0.75 * math.cos(math.pi * (2 * sweep + 1) / (2.0 * SWEEPS)))


def call(kernel, out_shape, cost, limit=16, **more):
    return pl.pallas_call(
        kernel,
        out_shape=out_shape,
        compiler_params=pltpu.CompilerParams(vmem_limit_bytes=limit * MIB),
        cost_estimate=pl.CostEstimate(flops=cost, bytes_accessed=1 << 20, transcendentals=0),
        **more,
    )


def shape_of(shape, dtype):
    return jax.ShapeDtypeStruct(shape, dtype)


def dot(a, b):
    return jnp.dot(a, b, preferred_element_type=F32)


def dot_nt(a, b):
    return lax.dot_general(a, b, (((1,), (1,)), ((), ())), preferred_element_type=F32)


def split_two(value):
    high = value.astype(BF16)
    return high, (value - high.astype(F32)).astype(BF16)


def low_part(value, size):
    return value & (size - 1) if size & (size - 1) == 0 else value % size


def high_part(value, size):
    return value >> (size.bit_length() - 1) if size & (size - 1) == 0 else value // size


def stack_parts(value, parts):
    width = value.shape[1] // parts
    return jnp.concatenate([value[:, i * width : (i + 1) * width] for i in range(parts)], axis=0)


def one_hot_rows(key, rows):
    seen = lax.broadcasted_iota(jnp.int32, (rows, key.shape[1]), 0)
    return jnp.where(seen == key, 1.0, 0.0).astype(BF16)


def pick_part(stacked, part, parts):
    rows = stacked.shape[0] // parts
    picked = stacked[(parts - 1) * rows :]
    for i in reversed(range(parts - 1)):
        picked = jnp.where(part == i, stacked[i * rows : (i + 1) * rows], picked)
    return picked


def gather_nodes(field, nodes, parts):
    width = field.shape[1] // parts
    hot = one_hot_rows(jnp.where(nodes < 0, -1, low_part(nodes, width)), width)
    found = dot(stack_parts(field.astype(BF16), parts), hot)
    return pick_part(found, high_part(nodes, width), parts)


def scatter_nodes(values, nodes, parts, count):
    width = count // parts
    hot = one_hot_rows(jnp.where(nodes < 0, -1, low_part(nodes, width)), width)
    masked = jnp.concatenate(
        [jnp.where(high_part(nodes, width) == i, values, 0.0) for i in range(parts)], axis=0
    ).astype(BF16)
    added = dot_nt(masked, hot)
    rows = values.shape[0]
    return jnp.concatenate([added[i * rows : (i + 1) * rows] for i in range(parts)], axis=1)


def halves_of(slot, rows):
    half = jnp.where(slot >= rows, 1, 0)
    return half, slot - half * rows


def trace_rows(field, nodes, parts, brow, used):
    turned = jnp.transpose(gather_nodes(field, nodes, parts))
    span = turned.shape[0] // brow
    return [
        jnp.concatenate(
            [turned[r * span : r * span + used], turned[r * span + used : r * span + 2 * used]], axis=1
        )
        for r in range(brow)
    ]


def own_panels(map_ref, rank, panel_dev):
    first = rank * panel_dev
    base = (first >> 7) << 7
    window = -(-panel_dev // LANES) * LANES
    near = map_ref[:, pl.ds(pl.multiple_of(base, LANES), window)]
    return jnp.where(first == base, near[:, :panel_dev], near[:, window - panel_dev :])


def load_rows(potential, own_map, devices, slot_rows):
    owner, slot = own_map[0:1], own_map[1:2]
    half, low = halves_of(slot, slot_rows)
    rows = devices * LOAD_ROWS
    key = half * rows + owner * LOAD_ROWS + low
    found = dot_nt(one_hot_rows(key, HALVES * rows), potential.astype(BF16))
    return jnp.concatenate([found[:rows], found[rows:]], axis=1).reshape(devices, LOAD_ROWS, LANES)


def node_tables(map_ref, rank, brow, bcol, panel_dev, slot_rows, stride):
    row_panels = bcol * panel_dev
    row_slots = -(-HALVES * bcol * stride // LANES) * LANES
    lane = lax.broadcasted_iota(jnp.int32, (1, row_panels), 1).astype(F32)
    block = jnp.floor((lane + 0.5) * (1.0 / panel_dev)).astype(jnp.int32)
    row_id = lax.broadcasted_iota(jnp.int32, (8, row_panels), 0)
    tables = []
    for r in range(brow):
        span = slice(r * row_panels, (r + 1) * row_panels)
        owner, slot, node = map_ref[0:1, span], map_ref[1:2, span], map_ref[2:3, span]
        half, low = halves_of(slot, slot_rows)
        key = jnp.where(owner == rank, half * (bcol * stride) + block * stride + low, -1)
        values = jnp.where(
            row_id == 0, high_part(node, 256), jnp.where(row_id == 1, low_part(node, 256), 1)
        ).astype(F32).astype(BF16)
        found = dot_nt(values, one_hot_rows(key, row_slots))
        table = jnp.where(found[2:3] > 0.5, found[0:1] * 256.0 + found[1:2], -1.0)
        tables.append(table.astype(jnp.int32))
    return jnp.concatenate(tables, axis=1)


def point_rows(points):
    row_id = lax.broadcasted_iota(jnp.int32, (POINT_ROWS, LANES), 0)
    each = POINT_ROWS // 3
    width = points.shape[1]
    value = jnp.zeros((POINT_ROWS, LANES), F32)
    for axis in range(3):
        for part in range(-(-width // LANES)):
            piece = points[axis : axis + 1, part * LANES : (part + 1) * LANES]
            short = LANES - piece.shape[1]
            if short:
                piece = jnp.concatenate([piece, jnp.zeros((1, short), F32)], axis=1)
            value = jnp.where(row_id == axis * each + part, piece, value)
    return value


def write_chunks(chunk_ref, pieces, loads, bcol, points=None):
    used = pieces[0].shape[0]
    for r, piece in enumerate(pieces):
        for c in range(bcol):
            device = r * bcol + c
            rows = [piece, loads[device]] + ([] if points is None else [points])
            left = chunk_ref.shape[1] - used - LOAD_ROWS - (0 if points is None else POINT_ROWS)
            if left:
                rows.append(jnp.zeros((left, LANES), F32))
            chunk_ref[device] = jnp.concatenate(rows, axis=0).astype(BF16)


def write_rims(field, even, first_ref, second_ref):
    low = field[:, :RIM]
    high = field[:, field.shape[1] - RIM :]
    first_ref[...] = jnp.where(even, high, low).astype(BF16)
    second_ref[...] = jnp.where(even, low, high).astype(BF16)


def setup_kernel(
    parts, brow, bcol, panel_dev, slot_rows, rank_ref, map_ref, field_ref, potential_ref, points_ref,
    nodes_ref, load_nodes_ref, chunk_ref, rim_first_ref, rim_second_ref,
):
    rank = rank_ref[0]
    tables = functools.partial(node_tables, map_ref, rank, brow, bcol, panel_dev, slot_rows)
    nodes = tables(slot_rows)
    nodes_ref[...] = jnp.broadcast_to(nodes, nodes_ref.shape)
    load_nodes_ref[...] = jnp.broadcast_to(tables(LOAD_ROWS), load_nodes_ref.shape)
    field = field_ref[...]
    write_rims(field, low_part(rank, 2) == 0, rim_first_ref, rim_second_ref)
    loads = load_rows(
        potential_ref[...], own_panels(map_ref, rank, panel_dev), brow * bcol, slot_rows
    )
    pieces = trace_rows(field, nodes, parts, brow, bcol * slot_rows)
    write_chunks(chunk_ref, pieces, loads, bcol, point_rows(points_ref[...].astype(F32)))


def hot_kernel(keys_ref, hot_ref, built_ref, sems):
    groups, width, _ = built_ref.shape
    copies = []
    for group in range(groups):
        for e in range(GROUP):
            key = keys_ref[group * GROUP + e : group * GROUP + e + 1, :]
            built_ref[group, :, e * LANES : (e + 1) * LANES] = one_hot_rows(low_part(key, width), width)
        copies.append(pltpu.make_async_copy(built_ref.at[group], hot_ref.at[group], sems.at[group]))
        copies[-1].start()
    for copy in copies:
        copy.wait()


def rim_correction(value, even, first_ref, second_ref, mass, weight):
    step = weight * penalty
    first, second = first_ref[...].astype(F32), second_ref[...].astype(F32)
    left, right = jnp.where(even, second, first), jnp.where(even, first, second)
    last = value.shape[1] - RIM
    low = value[:, :RIM] + step * left / mass[:, :RIM]
    high = value[:, last:] + step * right / mass[:, last:]
    return jnp.concatenate([low, value[:, RIM:last], high], axis=1)


def received_loads(chunk_ref, used, brow, columns):
    received = chunk_ref[...].astype(F32)[:, used : used + LOAD_ROWS]
    received = received.reshape(received.shape[0] * LOAD_ROWS, LANES)
    span = received.shape[0] // brow
    rows = []
    for r in range(brow):
        piece = received[r * span : (r + 1) * span]
        rows += [piece[:, :columns], piece[:, columns : HALVES * columns]]
    return jnp.transpose(jnp.concatenate(rows, axis=0))


def sweep_kernel(
    parts, weight, weight_before, rank_ref, coef_ref, field_ref, rhs_ref, mass_ref, keys_ref,
    matrix_ref, hot_ref, *more_refs,
):
    if weight_before is not None:
        first_ref, second_ref, out_ref, field_scr, *scratch = more_refs
    else:
        out_ref, *scratch = more_refs
    held_ref, sems, high_ref, low_ref, found_ref, local_ref, product_ref, yhigh_ref, ylow_ref, sum_ref = scratch
    groups = held_ref.shape[0]
    copies = [
        pltpu.make_async_copy(hot_ref.at[group], held_ref.at[group], sems.at[group])
        for group in range(groups)
    ]
    for copy in copies:
        copy.start()
    columns, count = field_ref.shape
    width = count // parts
    mass = mass_ref[...]
    if weight_before is None:
        field = field_ref[...]
        field_now = field_ref
    else:
        even = low_part(rank_ref[0], 2) == 0
        field = rim_correction(field_ref[...], even, first_ref, second_ref, mass, weight_before)
        field_scr[...] = field
        field_now = field_scr
    high, low = split_two(field)
    for h in range(parts):
        high_ref[h * columns : (h + 1) * columns] = high[:, h * width : (h + 1) * width]
        low_ref[h * columns : (h + 1) * columns] = low[:, h * width : (h + 1) * width]
    mat_high, mat_low = split_two(matrix_ref[...])
    matrix = jnp.concatenate(
        [
            jnp.concatenate([mat_high, mat_low], axis=1),
            jnp.concatenate([mat_high, jnp.zeros_like(mat_low)], axis=1),
        ],
        axis=0,
    )

    def gather(group):
        copies[group].wait()
        hot = held_ref[group]
        found_ref[group % 2] = dot(high_ref[...], hot) + dot(low_ref[...], hot)

    def pick(group):
        slot = group % 2
        for e in range(GROUP):
            element = group * GROUP + e
            key = keys_ref[element : element + 1, :]
            got = pick_part(found_ref[slot, :, e * LANES : (e + 1) * LANES], high_part(key, width), parts)
            got_high, got_low = split_two(got)
            local_ref[slot, e * columns : (e + 1) * columns, :LANES] = got_high
            local_ref[slot, e * columns : (e + 1) * columns, LANES:] = got_low

    def multiply(group):
        product_ref[group % 2] = dot(local_ref[group % 2], matrix)

    def scale(group):
        slot = group % 2
        for e in range(GROUP):
            element = group * GROUP + e
            part = high_part(keys_ref[element : element + 1, :], width)
            rows = product_ref[slot, e * columns : (e + 1) * columns]
            value = (rows[:, :LANES] + rows[:, LANES:]) * coef_ref[element]
            value_high, value_low = split_two(value)
            span = slice(e * LANES, (e + 1) * LANES)
            for h in range(parts):
                mask = jnp.where(part == h, 1.0, 0.0).astype(BF16)
                yhigh_ref[slot, h * columns : (h + 1) * columns, span] = value_high * mask
                ylow_ref[slot, h * columns : (h + 1) * columns, span] = value_low * mask

    def scatter(group):
        hot = held_ref[group]
        added = dot_nt(yhigh_ref[group % 2], hot) + dot_nt(ylow_ref[group % 2], hot)
        sum_ref[...] = added if group == 0 else sum_ref[...] + added

    gather(0)
    for group in range(groups):
        pick(group)
        if group + 1 < groups:
            gather(group + 1)
        multiply(group)
        if group:
            scatter(group - 1)
        scale(group)
    scatter(groups - 1)
    for h in range(parts):
        span = slice(h * width, (h + 1) * width)
        stiff = sum_ref[h * columns : (h + 1) * columns]
        out_ref[:, span] = (1.0 - weight) * field_now[:, span] + weight * (
            rhs_ref[:, span] - stiff
        ) / mass[:, span]


def loads_kernel(
    parts, brow, weight, used, rank_ref, nodes_ref, chunk_ref, forcing_ref, field_ref, first_ref,
    second_ref, mass_ref, rhs_ref, out_ref, rim_first_ref, rim_second_ref,
):
    columns, count = field_ref.shape
    loads = received_loads(chunk_ref, used, brow, columns)
    added = scatter_nodes(loads, nodes_ref[0:1, :], parts, count)
    rhs_ref[...] = forcing_ref[...] + added
    mass = mass_ref[...]
    even = low_part(rank_ref[0], 2) == 0
    field = field_ref[...] + weight * added / mass
    field = rim_correction(field, even, first_ref, second_ref, mass, weight)
    out_ref[...] = field
    write_rims(field, even, rim_first_ref, rim_second_ref)


def finish_kernel(
    parts, brow, bcol, panel_dev, slot_rows, weight, rank_ref, map_ref, nodes_ref, field_ref,
    first_ref, second_ref, mass_ref, potential_ref, out_ref, chunk_ref, rim_first_ref, rim_second_ref,
):
    rank = rank_ref[0]
    even = low_part(rank, 2) == 0
    field = rim_correction(field_ref[...], even, first_ref, second_ref, mass_ref[...], weight)
    out_ref[...] = field
    write_rims(field, even, rim_first_ref, rim_second_ref)
    loads = load_rows(
        potential_ref[...], own_panels(map_ref, rank, panel_dev), brow * bcol, slot_rows
    )
    pieces = trace_rows(field, nodes_ref[0:1, :], parts, brow, bcol * slot_rows)
    write_chunks(chunk_ref, pieces, loads, bcol)


def last_kernel(weight, rank_ref, field_ref, first_ref, second_ref, mass_ref, out_ref):
    even = low_part(rank_ref[0], 2) == 0
    out_ref[...] = rim_correction(field_ref[...], even, first_ref, second_ref, mass_ref[...], weight)


def density_groups(place_ref, map_ref, chunk_ref, brow, bcol, panel_dev, slot_rows):
    base = pl.multiple_of(place_ref[0] * (bcol * panel_dev), LANES)
    devices = brow * bcol
    columns = LANES // HALVES
    rows = BLOCKS * slot_rows
    panels = BLOCKS * panel_dev
    lane = lax.broadcasted_iota(jnp.int32, (1, panels), 1).astype(F32)
    block = jnp.floor((lane + 0.5) * (1.0 / panel_dev)).astype(jnp.int32)
    traces = chunk_ref[...].astype(F32)
    for group in range(bcol // BLOCKS):
        span = pl.ds(base + group * panels, panels)
        owner, slot = map_ref[0:1, span], map_ref[1:2, span]
        half, low = halves_of(slot, slot_rows)
        key = owner * rows + block * slot_rows + low
        near = traces[:, group * rows : (group + 1) * rows].reshape(devices * rows, LANES)
        found = dot(jnp.transpose(near).astype(BF16), one_hot_rows(key, devices * rows))
        density = jnp.where(half == 0, found[:columns], found[columns:])
        turned = jnp.concatenate([-density[columns // 2 :], density[: columns // 2]], axis=0)
        yield density.astype(BF16), turned.astype(BF16)


def write_parts(out_ref, total, panel_dev):
    for r in range(out_ref.shape[0]):
        out_ref[r] = total[:, r * panel_dev : (r + 1) * panel_dev]


def tile_kernel(
    brow, bcol, panel_dev, slot_rows, place_ref, map_ref, chunk_ref, out_ref, real_ref, imag_ref,
    target_ref, density_ref, turned_ref, built_real_ref, built_imag_ref, sum_ref, sems,
):
    count_all = brow * bcol * panel_dev
    soften = 0.5 * float(count_all) ** (-1.0 / 3.0)
    each = POINT_ROWS // 3
    row_index, col_index = place_ref[0], place_ref[1]
    start = bcol * slot_rows + LOAD_ROWS
    block = pl.program_id(0)

    def points_of(device):
        return chunk_ref[device].astype(F32)[start : start + POINT_ROWS]

    def copies(index):
        return (
            pltpu.make_async_copy(built_real_ref.at[index], real_ref.at[index], sems.at[0, index]),
            pltpu.make_async_copy(built_imag_ref.at[index], imag_ref.at[index], sems.at[1, index]),
        )

    @pl.when(block == 0)
    def prepare():
        near = [points_of(r * bcol + col_index) for r in range(brow)]
        for axis in range(3):
            rows = []
            for piece in near:
                for part in range(each):
                    wide = min(LANES, panel_dev - part * LANES)
                    rows.append(piece[axis * each + part : axis * each + part + 1, :wide])
            target_ref[axis : axis + 1, :] = jnp.concatenate(rows, axis=1)
        sum_ref[...] = jnp.zeros_like(sum_ref)
        groups = density_groups(place_ref, map_ref, chunk_ref, brow, bcol, panel_dev, slot_rows)
        for group, (density, turned) in enumerate(groups):
            for k in range(BLOCKS):
                span = slice(k * panel_dev, (k + 1) * panel_dev)
                density_ref[group * BLOCKS + k] = density[:, span]
                turned_ref[group * BLOCKS + k] = turned[:, span]

    source = jnp.transpose(points_of(row_index * bcol + block))
    step = 16
    for top in range(0, panel_dev, step):
        part, first = top // LANES, top % LANES
        squared = soften * soften
        for axis in range(3):
            column = source[first : first + step, axis * each + part : axis * each + part + 1]
            delta = column - target_ref[axis : axis + 1, :]
            squared = squared + delta * delta
        inverse = lax.rsqrt(squared)
        turns = (squared * inverse) * (wave_number / (2.0 * math.pi))
        turns = turns - jnp.floor(turns + 0.5)
        z = turns * turns
        sine = jnp.full_like(z, SIN_POLY[-1])
        for factor in SIN_POLY[-2::-1]:
            sine = sine * z + factor
        sine = sine * turns
        cosine = jnp.full_like(z, COS_POLY[-1])
        for factor in COS_POLY[-2::-1]:
            cosine = cosine * z + factor
        double = sine * (inverse * (2.0 / math.sqrt(float(count_all))))
        built_real_ref[block, top : top + step] = (
            inverse * (1.0 / math.sqrt(float(count_all))) - sine * double
        ).astype(BF16)
        built_imag_ref[block, top : top + step] = (cosine * double).astype(BF16)
    for copy in copies(block):
        copy.start()
    sum_ref[...] += dot(density_ref[block], built_real_ref[block]) + dot(
        turned_ref[block], built_imag_ref[block]
    )

    @pl.when(block == bcol - 1)
    def end():
        write_parts(out_ref, sum_ref[...], panel_dev)
        for index in range(bcol):
            for copy in copies(index):
                copy.wait()


def potential_kernel(
    brow, bcol, panel_dev, slot_rows, place_ref, map_ref, chunk_ref, real_ref, imag_ref, out_ref,
    held_real_ref, held_imag_ref, sems,
):
    copies = (
        pltpu.make_async_copy(real_ref, held_real_ref, sems.at[0]),
        pltpu.make_async_copy(imag_ref, held_imag_ref, sems.at[1]),
    )
    for copy in copies:
        copy.start()
    groups = list(density_groups(place_ref, map_ref, chunk_ref, brow, bcol, panel_dev, slot_rows))
    for copy in copies:
        copy.wait()
    total = None
    for group, (density, turned) in enumerate(groups):
        here = slice(group * BLOCKS, (group + 1) * BLOCKS)
        shape = (BLOCKS * panel_dev, brow * panel_dev)
        part = dot(density, held_real_ref[here].reshape(shape)) + dot(
            turned, held_imag_ref[here].reshape(shape)
        )
        total = part if total is None else total + part
    write_parts(out_ref, total, panel_dev)


def per_device(
    panel_points,
    panel_map,
    element_nodes,
    element_coef,
    element_matrix,
    node_mass,
    forcing,
    field_start,
    potential_start,
):
    columns, panel_dev = potential_start.shape
    count = field_start.shape[1]
    brow, bcol = lax.axis_size("brow"), lax.axis_size("bcol")
    devices = brow * bcol
    capacity = max(2, 2 * panel_dev // devices)
    slot_rows = -(-capacity // HALVES)
    used = bcol * slot_rows
    assert slot_rows <= LOAD_ROWS and columns * HALVES == LANES and bcol % BLOCKS == 0
    parts = 256 // columns
    width = count // parts
    row_panels = bcol * panel_dev
    row_index, col_index = lax.axis_index("brow"), lax.axis_index("bcol")
    rank = (row_index * bcol + col_index).reshape(1)
    place = jnp.stack([row_index, col_index])
    mass = node_mass.reshape(1, count)
    nodes_each, elements = element_nodes.shape
    assert elements % GROUP == 0
    keys = jnp.pad(element_nodes.T, ((0, 0), (0, LANES - nodes_each)))
    matrix = jnp.pad(element_matrix, ((0, LANES - nodes_each), (0, LANES - nodes_each)))
    smem = pl.BlockSpec(memory_space=pltpu.SMEM)
    vmem = pl.BlockSpec(memory_space=pltpu.VMEM)
    rim_shape = shape_of((columns, RIM), BF16)
    field_shape = shape_of((columns, count), F32)
    weights = [weight_of(sweep_index) for sweep_index in range(SWEEPS)]
    even_pairs = [(i, i ^ 1) for i in range(devices)]
    odd_pairs = [pair for i in range(1, devices - 1, 2) for pair in ((i, i + 1), (i + 1, i))]
    even = (rank[0] & 1) == 0

    def chunk_shape(rows, unit):
        return shape_of((devices, -(-rows // unit) * unit, LANES), BF16)

    def table_shape(stride):
        return shape_of((8, brow * (-(-HALVES * bcol * stride // LANES) * LANES)), jnp.int32)

    def exchange(first, second):
        return lax.ppermute(first, AXES, even_pairs), lax.ppermute(second, AXES, odd_pairs)

    def rims(field, halo, weight):
        first, second = (piece.astype(F32) for piece in halo)
        left, right = jnp.where(even, second, first), jnp.where(even, first, second)
        last = count - RIM
        low = field[:, :RIM] + (weight * penalty) * left / mass[:, :RIM]
        high = field[:, last:] + (weight * penalty) * right / mass[:, last:]
        return jnp.where(even, high, low).astype(BF16), jnp.where(even, low, high).astype(BF16)

    def swap_all(chunks):
        return lax.all_to_all(chunks, AXES, split_axis=0, concat_axis=0, tiled=True)

    hbm = pl.BlockSpec(memory_space=pltpu.HBM)
    hot_shape = (elements // GROUP, width, GROUP * LANES)
    hot_blocks = max(hot_shape[0], -(-48 * MIB // (2 * width * GROUP * LANES)))

    def sweep(field, rhs, weight, halo=(), weight_before=None):
        rows = parts * columns
        lanes = GROUP * LANES
        first = weight_before is None
        return call(
            functools.partial(sweep_kernel, parts, weight, weight_before),
            field_shape,
            5_000_000_000,
            limit=24,
            in_specs=[smem, smem] + [vmem] * 5 + [hbm] + [vmem] * len(halo),
            out_specs=vmem,
            scratch_shapes=([] if first else [pltpu.VMEM((columns, count), F32)])
            + [
                pltpu.VMEM(hot_shape, BF16),
                pltpu.SemaphoreType.DMA((elements // GROUP,)),
                pltpu.VMEM((rows, width), BF16),
                pltpu.VMEM((rows, width), BF16),
                pltpu.VMEM((2, rows, lanes), F32),
                pltpu.VMEM((2, GROUP * columns, 2 * LANES), BF16),
                pltpu.VMEM((2, GROUP * columns, 2 * LANES), F32),
                pltpu.VMEM((2, rows, lanes), BF16),
                pltpu.VMEM((2, rows, lanes), BF16),
                pltpu.VMEM((rows, width), F32),
            ],
        )(rank, element_coef, field, rhs, mass, keys, matrix, hot, *halo)

    def add_loads(chunks, field, halo, weight):
        return call(
            functools.partial(loads_kernel, parts, brow, weight, used),
            (field_shape, field_shape, rim_shape, rim_shape),
            500_000_000,
            in_specs=[smem] + [vmem] * 7,
            out_specs=(vmem,) * 4,
        )(rank, load_nodes, chunks, forcing, field, *halo, mass)

    tile_shape = (bcol, panel_dev, brow * panel_dev)
    parts_shape = shape_of((brow, columns, panel_dev), F32)
    sizes = (brow, bcol, panel_dev, slot_rows)

    def sum_parts(parts_out):
        return lax.psum_scatter(parts_out, "brow", scatter_dimension=0, tiled=False)

    nodes, load_nodes, chunks, *rim = call(
        functools.partial(setup_kernel, parts, brow, bcol, panel_dev, slot_rows),
        (
            table_shape(slot_rows),
            table_shape(LOAD_ROWS),
            chunk_shape(used + LOAD_ROWS + POINT_ROWS, 16),
            rim_shape,
            rim_shape,
        ),
        2_000_000_000,
        limit=56,
        in_specs=[smem] + [vmem] * 4,
        out_specs=(vmem,) * 5,
    )(rank, panel_map, field_start, potential_start, panel_points)
    hot = call(
        hot_kernel,
        shape_of((hot_blocks,) + hot_shape[1:], BF16),
        1_000_000_000,
        in_specs=[vmem],
        out_specs=hbm,
        scratch_shapes=[pltpu.VMEM(hot_shape, BF16), pltpu.SemaphoreType.DMA((hot_shape[0],))],
    )(keys)
    halo = exchange(*rim)
    chunks = swap_all(chunks)
    field = sweep(field_start, forcing, weights[0])
    parts_out, real_tile, imag_tile = call(
        functools.partial(tile_kernel, *sizes),
        (parts_shape, shape_of(tile_shape, BF16), shape_of(tile_shape, BF16)),
        8_000_000_000,
        limit=58,
        grid=(bcol,),
        in_specs=[smem, vmem, vmem],
        out_specs=(vmem, hbm, hbm),
        scratch_shapes=[
            pltpu.VMEM((8, brow * panel_dev), F32),
            pltpu.VMEM((bcol, columns, panel_dev), BF16),
            pltpu.VMEM((bcol, columns, panel_dev), BF16),
            pltpu.VMEM(tile_shape, BF16),
            pltpu.VMEM(tile_shape, BF16),
            pltpu.VMEM((columns, brow * panel_dev), F32),
            pltpu.SemaphoreType.DMA((2, bcol)),
        ],
    )(place, panel_map, chunks)
    potential = sum_parts(parts_out)
    rhs, field, *rim = add_loads(chunks, field, halo, weights[0])
    halo = exchange(*rim)
    field = sweep(field, rhs, weights[1])
    halo_next = exchange(*rims(field, halo, weights[1]))
    field = sweep(field, rhs, weights[2], halo, weights[1])
    field, chunks, *rim = call(
        functools.partial(finish_kernel, parts, brow, bcol, panel_dev, slot_rows, weights[2]),
        (field_shape, chunk_shape(used + LOAD_ROWS, 8), rim_shape, rim_shape),
        1_000_000_000,
        in_specs=[smem] + [vmem] * 7,
        out_specs=(vmem,) * 4,
    )(rank, panel_map, nodes, field, *halo_next, mass, potential)

    halo = exchange(*rim)
    chunks = swap_all(chunks)
    field = sweep(field, forcing, weights[0])
    parts_out = call(
        functools.partial(potential_kernel, *sizes),
        parts_shape,
        2_000_000_000,
        limit=58,
        in_specs=[smem, vmem, vmem, hbm, hbm],
        out_specs=vmem,
        scratch_shapes=[
            pltpu.VMEM(tile_shape, BF16),
            pltpu.VMEM(tile_shape, BF16),
            pltpu.SemaphoreType.DMA((2,)),
        ],
    )(place, panel_map, chunks, real_tile, imag_tile)
    parts_out, field = lax.optimization_barrier((parts_out, field))
    potential = sum_parts(parts_out)
    rhs, field, *rim = add_loads(chunks, field, halo, weights[0])
    halo = exchange(*rim)
    field = sweep(field, rhs, weights[1])
    halo_next = exchange(*rims(field, halo, weights[1]))
    field = sweep(field, rhs, weights[2], halo, weights[1])
    field = call(
        functools.partial(last_kernel, weights[2]),
        field_shape,
        100_000_000,
        in_specs=[smem] + [vmem] * 4,
        out_specs=vmem,
    )(rank, field, *halo_next, mass)
    return (field, potential)


def solution(mesh):
    placed = (
        P(None, AXES),
        P(),
        P(None, AXES),
        P(AXES),
        P(),
        P(AXES),
        P(None, AXES),
        P(None, AXES),
        P(None, AXES),
    )
    return jax.shard_map(
        per_device,
        mesh=mesh,
        in_specs=placed,
        out_specs=(P(None, AXES), P(None, AXES)),
        check_vma=False,
    )
```

```python
import functools
import math

import jax
import jax.numpy as jnp
from jax import lax
from jax.experimental import pallas as pl
from jax.experimental.pallas import tpu as pltpu
from jax.sharding import PartitionSpec as P

RIM = 128
SWEEPS = 3
LANES = 128
LOAD_ROWS = 8
POINT_ROWS = 8
HALVES = 2
GROUP = 8
BLOCKS = 4

wave_number = 20.0
penalty = 0.5

AXES = ("brow", "bcol")
F32 = jnp.float32
BF16 = jnp.bfloat16

SIN_POLY = (3.14159264, -5.16771008, 2.55007752, -0.59829129, 0.07765766)
COS_POLY = (0.99999995, -4.93479283, 4.05841135, -1.33187657, 0.21968961)

MIB = 1024 * 1024


def weight_of(sweep):
    return 1.0 / (1.25 + 0.75 * math.cos(math.pi * (2 * sweep + 1) / (2.0 * SWEEPS)))


def call(kernel, out_shape, cost, limit=16, **more):
    return pl.pallas_call(
        kernel,
        out_shape=out_shape,
        compiler_params=pltpu.CompilerParams(vmem_limit_bytes=limit * MIB),
        cost_estimate=pl.CostEstimate(flops=cost, bytes_accessed=1 << 20, transcendentals=0),
        **more,
    )


def shape_of(shape, dtype):
    return jax.ShapeDtypeStruct(shape, dtype)


def dot(a, b):
    return jnp.dot(a, b, preferred_element_type=F32)


def dot_nt(a, b):
    return lax.dot_general(a, b, (((1,), (1,)), ((), ())), preferred_element_type=F32)


def split_two(value):
    high = value.astype(BF16)
    return high, (value - high.astype(F32)).astype(BF16)


def low_part(value, size):
    return value & (size - 1) if size & (size - 1) == 0 else value % size


def high_part(value, size):
    return value >> (size.bit_length() - 1) if size & (size - 1) == 0 else value // size


def stack_parts(value, parts):
    width = value.shape[1] // parts
    return jnp.concatenate([value[:, i * width : (i + 1) * width] for i in range(parts)], axis=0)


def one_hot_rows(key, rows):
    seen = lax.broadcasted_iota(jnp.int32, (rows, key.shape[1]), 0)
    return jnp.where(seen == key, 1.0, 0.0).astype(BF16)


def pick_part(stacked, part, parts):
    rows = stacked.shape[0] // parts
    picked = stacked[(parts - 1) * rows :]
    for i in reversed(range(parts - 1)):
        picked = jnp.where(part == i, stacked[i * rows : (i + 1) * rows], picked)
    return picked


def gather_nodes(field, nodes, parts):
    width = field.shape[1] // parts
    hot = one_hot_rows(jnp.where(nodes < 0, -1, low_part(nodes, width)), width)
    found = dot(stack_parts(field.astype(BF16), parts), hot)
    return pick_part(found, high_part(nodes, width), parts)


def scatter_nodes(values, nodes, parts, count):
    width = count // parts
    hot = one_hot_rows(jnp.where(nodes < 0, -1, low_part(nodes, width)), width)
    masked = jnp.concatenate(
        [jnp.where(high_part(nodes, width) == i, values, 0.0) for i in range(parts)], axis=0
    ).astype(BF16)
    added = dot_nt(masked, hot)
    rows = values.shape[0]
    return jnp.concatenate([added[i * rows : (i + 1) * rows] for i in range(parts)], axis=1)


def halves_of(slot, rows):
    half = jnp.where(slot >= rows, 1, 0)
    return half, slot - half * rows


def trace_rows(field, nodes, parts, brow, used):
    turned = jnp.transpose(gather_nodes(field, nodes, parts))
    span = turned.shape[0] // brow
    return [
        jnp.concatenate(
            [turned[r * span : r * span + used], turned[r * span + used : r * span + 2 * used]], axis=1
        )
        for r in range(brow)
    ]


def own_panels(map_ref, rank, panel_dev):
    first = rank * panel_dev
    base = (first >> 7) << 7
    window = -(-panel_dev // LANES) * LANES
    near = map_ref[:, pl.ds(pl.multiple_of(base, LANES), window)]
    return jnp.where(first == base, near[:, :panel_dev], near[:, window - panel_dev :])


def load_rows(potential, own_map, devices, slot_rows):
    owner, slot = own_map[0:1], own_map[1:2]
    half, low = halves_of(slot, slot_rows)
    rows = devices * LOAD_ROWS
    key = half * rows + owner * LOAD_ROWS + low
    found = dot_nt(one_hot_rows(key, HALVES * rows), potential.astype(BF16))
    return jnp.concatenate([found[:rows], found[rows:]], axis=1).reshape(devices, LOAD_ROWS, LANES)


def node_tables(map_ref, rank, brow, bcol, panel_dev, slot_rows, stride):
    row_panels = bcol * panel_dev
    row_slots = -(-HALVES * bcol * stride // LANES) * LANES
    lane = lax.broadcasted_iota(jnp.int32, (1, row_panels), 1).astype(F32)
    block = jnp.floor((lane + 0.5) * (1.0 / panel_dev)).astype(jnp.int32)
    row_id = lax.broadcasted_iota(jnp.int32, (8, row_panels), 0)
    tables = []
    for r in range(brow):
        span = slice(r * row_panels, (r + 1) * row_panels)
        owner, slot, node = map_ref[0:1, span], map_ref[1:2, span], map_ref[2:3, span]
        half, low = halves_of(slot, slot_rows)
        key = jnp.where(owner == rank, half * (bcol * stride) + block * stride + low, -1)
        values = jnp.where(
            row_id == 0, high_part(node, 256), jnp.where(row_id == 1, low_part(node, 256), 1)
        ).astype(F32).astype(BF16)
        found = dot_nt(values, one_hot_rows(key, row_slots))
        table = jnp.where(found[2:3] > 0.5, found[0:1] * 256.0 + found[1:2], -1.0)
        tables.append(table.astype(jnp.int32))
    return jnp.concatenate(tables, axis=1)


def point_rows(points):
    row_id = lax.broadcasted_iota(jnp.int32, (POINT_ROWS, LANES), 0)
    each = POINT_ROWS // 3
    width = points.shape[1]
    value = jnp.zeros((POINT_ROWS, LANES), F32)
    for axis in range(3):
        for part in range(-(-width // LANES)):
            piece = points[axis : axis + 1, part * LANES : (part + 1) * LANES]
            short = LANES - piece.shape[1]
            if short:
                piece = jnp.concatenate([piece, jnp.zeros((1, short), F32)], axis=1)
            value = jnp.where(row_id == axis * each + part, piece, value)
    return value


def write_chunks(chunk_ref, pieces, loads, bcol, points=None):
    used = pieces[0].shape[0]
    for r, piece in enumerate(pieces):
        for c in range(bcol):
            device = r * bcol + c
            rows = [piece, loads[device]] + ([] if points is None else [points])
            left = chunk_ref.shape[1] - used - LOAD_ROWS - (0 if points is None else POINT_ROWS)
            if left:
                rows.append(jnp.zeros((left, LANES), F32))
            chunk_ref[device] = jnp.concatenate(rows, axis=0).astype(BF16)


def write_rims(field, even, first_ref, second_ref):
    low = field[:, :RIM]
    high = field[:, field.shape[1] - RIM :]
    first_ref[...] = jnp.where(even, high, low).astype(BF16)
    second_ref[...] = jnp.where(even, low, high).astype(BF16)


def setup_kernel(
    parts, brow, bcol, panel_dev, slot_rows, rank_ref, map_ref, field_ref, potential_ref, points_ref,
    nodes_ref, load_nodes_ref, chunk_ref, rim_first_ref, rim_second_ref,
):
    rank = rank_ref[0]
    tables = functools.partial(node_tables, map_ref, rank, brow, bcol, panel_dev, slot_rows)
    nodes = tables(slot_rows)
    nodes_ref[...] = jnp.broadcast_to(nodes, nodes_ref.shape)
    load_nodes_ref[...] = jnp.broadcast_to(tables(LOAD_ROWS), load_nodes_ref.shape)
    field = field_ref[...]
    write_rims(field, low_part(rank, 2) == 0, rim_first_ref, rim_second_ref)
    loads = load_rows(
        potential_ref[...], own_panels(map_ref, rank, panel_dev), brow * bcol, slot_rows
    )
    pieces = trace_rows(field, nodes, parts, brow, bcol * slot_rows)
    write_chunks(chunk_ref, pieces, loads, bcol, point_rows(points_ref[...].astype(F32)))


def rim_correction(value, even, first_ref, second_ref, mass, weight):
    step = weight * penalty
    first, second = first_ref[...].astype(F32), second_ref[...].astype(F32)
    left, right = jnp.where(even, second, first), jnp.where(even, first, second)
    last = value.shape[1] - RIM
    low = value[:, :RIM] + step * left / mass[:, :RIM]
    high = value[:, last:] + step * right / mass[:, last:]
    return jnp.concatenate([low, value[:, RIM:last], high], axis=1)


def received_loads(chunk_ref, used, brow, columns):
    received = chunk_ref[...].astype(F32)[:, used : used + LOAD_ROWS]
    received = received.reshape(received.shape[0] * LOAD_ROWS, LANES)
    span = received.shape[0] // brow
    rows = []
    for r in range(brow):
        piece = received[r * span : (r + 1) * span]
        rows += [piece[:, :columns], piece[:, columns : HALVES * columns]]
    return jnp.transpose(jnp.concatenate(rows, axis=0))


def sweep_kernel(
    parts, weight, weight_before, build, rank_ref, coef_ref, field_ref, rhs_ref, mass_ref, keys_ref,
    matrix_ref, *more_refs,
):
    if build:
        out_ref, hot_ref, *scratch = more_refs
    elif weight_before is None:
        hot_ref, out_ref, *scratch = more_refs
    else:
        hot_ref, first_ref, second_ref, out_ref, field_scr, *scratch = more_refs
    held_ref, sems, high_ref, low_ref, found_ref, local_ref, yhigh_ref, ylow_ref, sum_ref = scratch
    groups = held_ref.shape[0]
    copies = []
    for group in range(groups):
        ends = (held_ref.at[group], hot_ref.at[group])
        copies.append(pltpu.make_async_copy(*(ends if build else ends[::-1]), sems.at[group]))
        if not build:
            copies[-1].start()
    columns, count = field_ref.shape
    width = count // parts
    mass = mass_ref[...]
    if weight_before is None:
        field = field_ref[...]
        field_now = field_ref
    else:
        even = low_part(rank_ref[0], 2) == 0
        field = rim_correction(field_ref[...], even, first_ref, second_ref, mass, weight_before)
        field_scr[...] = field
        field_now = field_scr
    high, low = split_two(field)
    for h in range(parts):
        high_ref[h * columns : (h + 1) * columns] = high[:, h * width : (h + 1) * width]
        low_ref[h * columns : (h + 1) * columns] = low[:, h * width : (h + 1) * width]
    mat_high, mat_low = split_two(matrix_ref[...])
    matrix = jnp.concatenate(
        [
            jnp.concatenate([mat_high, mat_low], axis=1),
            jnp.concatenate([mat_high, jnp.zeros_like(mat_low)], axis=1),
        ],
        axis=0,
    )

    def gather(group):
        if build:
            for e in range(GROUP):
                key = keys_ref[group * GROUP + e : group * GROUP + e + 1, :]
                held_ref[group, :, e * LANES : (e + 1) * LANES] = one_hot_rows(low_part(key, width), width)
            copies[group].start()
        else:
            copies[group].wait()
        hot = held_ref[group]
        found_ref[group % 2] = dot(high_ref[...], hot) + dot(low_ref[...], hot)

    def multiply(group):
        slot = group % 2
        for e in range(GROUP):
            element = group * GROUP + e
            key = keys_ref[element : element + 1, :]
            got = pick_part(found_ref[slot, :, e * LANES : (e + 1) * LANES], high_part(key, width), parts)
            got_high, got_low = split_two(got)
            local_ref[slot, e * columns : (e + 1) * columns, :LANES] = got_high
            local_ref[slot, e * columns : (e + 1) * columns, LANES:] = got_low

        product = dot(local_ref[slot], matrix)
        for e in range(GROUP):
            element = group * GROUP + e
            part = high_part(keys_ref[element : element + 1, :], width)
            rows = product[e * columns : (e + 1) * columns]
            value = (rows[:, :LANES] + rows[:, LANES:]) * coef_ref[element]
            value_high, value_low = split_two(value)
            span = slice(e * LANES, (e + 1) * LANES)
            for h in range(parts):
                mask = jnp.where(part == h, 1.0, 0.0).astype(BF16)
                yhigh_ref[slot, h * columns : (h + 1) * columns, span] = value_high * mask
                ylow_ref[slot, h * columns : (h + 1) * columns, span] = value_low * mask

    def scatter(group):
        hot = held_ref[group]
        added = dot_nt(yhigh_ref[group % 2], hot) + dot_nt(ylow_ref[group % 2], hot)
        sum_ref[...] = added if group == 0 else sum_ref[...] + added

    gather(0)
    for group in range(groups):
        if group + 1 < groups:
            gather(group + 1)
        multiply(group)
        scatter(group)
    if build:
        for copy in copies:
            copy.wait()
    for h in range(parts):
        span = slice(h * width, (h + 1) * width)
        stiff = sum_ref[h * columns : (h + 1) * columns]
        out_ref[:, span] = (1.0 - weight) * field_now[:, span] + weight * (
            rhs_ref[:, span] - stiff
        ) / mass[:, span]


def loads_kernel(
    parts, brow, weight, used, rank_ref, nodes_ref, chunk_ref, forcing_ref, field_ref, first_ref,
    second_ref, mass_ref, rhs_ref, out_ref, rim_first_ref, rim_second_ref,
):
    columns, count = field_ref.shape
    loads = received_loads(chunk_ref, used, brow, columns)
    added = scatter_nodes(loads, nodes_ref[0:1, :], parts, count)
    rhs_ref[...] = forcing_ref[...] + added
    mass = mass_ref[...]
    even = low_part(rank_ref[0], 2) == 0
    field = field_ref[...] + weight * added / mass
    field = rim_correction(field, even, first_ref, second_ref, mass, weight)
    out_ref[...] = field
    write_rims(field, even, rim_first_ref, rim_second_ref)


def total(parts_ref):
    value = parts_ref[0]
    for r in range(1, parts_ref.shape[0]):
        value = value + parts_ref[r]
    return value


def finish_kernel(
    parts, brow, bcol, panel_dev, slot_rows, weight, rank_ref, map_ref, nodes_ref, field_ref,
    first_ref, second_ref, mass_ref, parts_ref, out_ref, chunk_ref, rim_first_ref, rim_second_ref,
):
    rank = rank_ref[0]
    even = low_part(rank, 2) == 0
    field = rim_correction(field_ref[...], even, first_ref, second_ref, mass_ref[...], weight)
    out_ref[...] = field
    write_rims(field, even, rim_first_ref, rim_second_ref)
    loads = load_rows(
        total(parts_ref), own_panels(map_ref, rank, panel_dev), brow * bcol, slot_rows
    )
    pieces = trace_rows(field, nodes_ref[0:1, :], parts, brow, bcol * slot_rows)
    write_chunks(chunk_ref, pieces, loads, bcol)


def last_kernel(
    weight, rank_ref, field_ref, first_ref, second_ref, mass_ref, parts_ref, out_ref, potential_ref
):
    even = low_part(rank_ref[0], 2) == 0
    out_ref[...] = rim_correction(field_ref[...], even, first_ref, second_ref, mass_ref[...], weight)
    potential_ref[...] = total(parts_ref)


def density_groups(rank_ref, map_ref, chunk_ref, brow, bcol, panel_dev, slot_rows):
    base = pl.multiple_of(high_part(rank_ref[0], bcol) * (bcol * panel_dev), LANES)
    devices = brow * bcol
    columns = LANES // HALVES
    rows = BLOCKS * slot_rows
    panels = BLOCKS * panel_dev
    lane = lax.broadcasted_iota(jnp.int32, (1, panels), 1).astype(F32)
    block = jnp.floor((lane + 0.5) * (1.0 / panel_dev)).astype(jnp.int32)
    traces = chunk_ref[...].astype(F32)
    for group in range(bcol // BLOCKS):
        span = pl.ds(base + group * panels, panels)
        owner, slot = map_ref[0:1, span], map_ref[1:2, span]
        half, low = halves_of(slot, slot_rows)
        key = owner * rows + block * slot_rows + low
        near = traces[:, group * rows : (group + 1) * rows].reshape(devices * rows, LANES)
        found = dot(jnp.transpose(near).astype(BF16), one_hot_rows(key, devices * rows))
        density = jnp.where(half == 0, found[:columns], found[columns:])
        turned = jnp.concatenate([-density[columns // 2 :], density[: columns // 2]], axis=0)
        yield density.astype(BF16), turned.astype(BF16)


def write_parts(out_ref, total, panel_dev):
    for r in range(out_ref.shape[0]):
        out_ref[r] = total[:, r * panel_dev : (r + 1) * panel_dev]


def split_three(value):
    high = value.astype(BF16).astype(F32)
    middle = (value - high).astype(BF16).astype(F32)
    return [high, middle, value - high - middle]


def squares(axes):
    return sum(row * row for row in axes[1:]) + axes[0] * axes[0]


def rows_of(rows, dtype=BF16):
    row_id = lax.broadcasted_iota(jnp.int32, (16, rows[0].shape[1]), 0)
    value = jnp.zeros(row_id.shape, F32)
    for index, row in enumerate(rows):
        value = jnp.where(row_id == index, row, value)
    return value.astype(dtype)


def tile_kernel(
    brow, bcol, panel_dev, slot_rows, rank_ref, map_ref, chunk_ref, out_ref, tile_ref,
    target_ref, density_ref, turned_ref, distance_ref, built_ref, sum_ref, sems,
):
    count_all = brow * bcol * panel_dev
    soften = 0.5 * float(count_all) ** (-1.0 / 3.0)
    each = POINT_ROWS // 3
    row_index, col_index = high_part(rank_ref[0], bcol), low_part(rank_ref[0], bcol)
    start = bcol * slot_rows + LOAD_ROWS
    block = pl.program_id(0)

    def points_of(device):
        return chunk_ref[device].astype(F32)[start : start + POINT_ROWS]

    def copy_of(index):
        return pltpu.make_async_copy(built_ref.at[index], tile_ref.at[index], sems.at[index])

    @pl.when(block == 0)
    def prepare():
        near = [points_of(r * bcol + col_index) for r in range(brow)]
        axes = []
        for axis in range(3):
            rows = []
            for piece in near:
                for part in range(each):
                    wide = min(LANES, panel_dev - part * LANES)
                    rows.append(piece[axis * each + part : axis * each + part + 1, :wide])
            axes.append(jnp.concatenate(rows, axis=1))
        norms = split_three(squares(axes) + soften * soften)
        target_ref[...] = rows_of([-2.0 * row for row in axes] + [jnp.ones_like(axes[0])] * 3 + norms)
        sum_ref[...] = jnp.zeros_like(sum_ref)
        groups = density_groups(rank_ref, map_ref, chunk_ref, brow, bcol, panel_dev, slot_rows)
        for group, (density, turned) in enumerate(groups):
            for k in range(BLOCKS):
                span = slice(k * panel_dev, (k + 1) * panel_dev)
                density_ref[group * BLOCKS + k] = density[:, span]
                turned_ref[group * BLOCKS + k] = turned[:, span]

    piece = points_of(row_index * bcol + block)
    axes = [
        jnp.concatenate([piece[axis * each + part : axis * each + part + 1] for part in range(each)], axis=1)
        for axis in range(3)
    ]
    norms = split_three(squares(axes))
    source = jnp.transpose(rows_of(axes + norms + [jnp.ones_like(axes[0])] * 3, F32)).astype(BF16)
    distance_ref[...] = dot(source[:panel_dev], target_ref[...])
    step = 16
    for top in range(0, panel_dev, step):
        squared = distance_ref[top : top + step]
        inverse = lax.rsqrt(squared)
        turns = (squared * inverse) * (wave_number / (2.0 * math.pi))
        turns = turns - jnp.floor(turns + 0.5)
        z = turns * turns
        sine = jnp.full_like(z, SIN_POLY[-1])
        for factor in SIN_POLY[-2::-1]:
            sine = sine * z + factor
        sine = sine * turns
        cosine = jnp.full_like(z, COS_POLY[-1])
        for factor in COS_POLY[-2::-1]:
            cosine = cosine * z + factor
        double = sine * (inverse * (2.0 / math.sqrt(float(count_all))))
        built_ref[block, 0, top : top + step] = (
            inverse * (1.0 / math.sqrt(float(count_all))) - sine * double
        ).astype(BF16)
        built_ref[block, 1, top : top + step] = (cosine * double).astype(BF16)
    copy_of(block).start()
    sum_ref[...] += dot(density_ref[block], built_ref[block, 0]) + dot(
        turned_ref[block], built_ref[block, 1]
    )

    @pl.when(block == bcol - 1)
    def end():
        write_parts(out_ref, sum_ref[...], panel_dev)
        for index in range(bcol):
            copy_of(index).wait()


def potential_kernel(
    brow, bcol, panel_dev, slot_rows, rank_ref, map_ref, chunk_ref, tile_ref, out_ref, held_ref, sems,
):
    copies = [
        pltpu.make_async_copy(tile_ref.at[block], held_ref.at[block], sems.at[block])
        for block in range(bcol)
    ]
    for copy in copies:
        copy.start()
    whole = None
    groups = density_groups(rank_ref, map_ref, chunk_ref, brow, bcol, panel_dev, slot_rows)
    for group, (density, turned) in enumerate(groups):
        for k in range(BLOCKS):
            block = group * BLOCKS + k
            copies[block].wait()
            span = slice(k * panel_dev, (k + 1) * panel_dev)
            part = dot(density[:, span], held_ref[block, 0]) + dot(turned[:, span], held_ref[block, 1])
            whole = part if whole is None else whole + part
    write_parts(out_ref, whole, panel_dev)


def per_device(
    panel_points,
    panel_map,
    element_nodes,
    element_coef,
    element_matrix,
    node_mass,
    forcing,
    field_start,
    potential_start,
):
    columns, panel_dev = potential_start.shape
    count = field_start.shape[1]
    brow, bcol = lax.axis_size("brow"), lax.axis_size("bcol")
    devices = brow * bcol
    capacity = max(2, 2 * panel_dev // devices)
    slot_rows = -(-capacity // HALVES)
    used = bcol * slot_rows
    assert slot_rows <= LOAD_ROWS and columns * HALVES == LANES and bcol % BLOCKS == 0
    parts = 256 // columns
    width = count // parts
    row_panels = bcol * panel_dev
    row_index, col_index = lax.axis_index("brow"), lax.axis_index("bcol")
    rank = (row_index * bcol + col_index).reshape(1)
    mass = node_mass.reshape(1, count)
    nodes_each, elements = element_nodes.shape
    assert elements % GROUP == 0
    keys = jnp.pad(element_nodes.T, ((0, 0), (0, LANES - nodes_each)))
    matrix = jnp.pad(element_matrix, ((0, LANES - nodes_each), (0, LANES - nodes_each)))
    smem = pl.BlockSpec(memory_space=pltpu.SMEM)
    vmem = pl.BlockSpec(memory_space=pltpu.VMEM)
    rim_shape = shape_of((columns, RIM), BF16)
    field_shape = shape_of((columns, count), F32)
    weights = [weight_of(sweep_index) for sweep_index in range(SWEEPS)]
    even_pairs = [(i, i ^ 1) for i in range(devices)]
    odd_pairs = [pair for i in range(1, devices - 1, 2) for pair in ((i, i + 1), (i + 1, i))]
    even = (rank[0] & 1) == 0

    def chunk_shape(rows, unit):
        return shape_of((devices, -(-rows // unit) * unit, LANES), BF16)

    def table_shape(stride):
        return shape_of((8, brow * (-(-HALVES * bcol * stride // LANES) * LANES)), jnp.int32)

    def exchange(first, second):
        return lax.ppermute(first, AXES, even_pairs), lax.ppermute(second, AXES, odd_pairs)

    def rims(field, halo, weight):
        first, second = (piece.astype(F32) for piece in halo)
        left, right = jnp.where(even, second, first), jnp.where(even, first, second)
        last = count - RIM
        low = field[:, :RIM] + (weight * penalty) * left / mass[:, :RIM]
        high = field[:, last:] + (weight * penalty) * right / mass[:, last:]
        return jnp.where(even, high, low).astype(BF16), jnp.where(even, low, high).astype(BF16)

    def swap_all(chunks):
        return lax.all_to_all(chunks, AXES, split_axis=0, concat_axis=0, tiled=True)

    hbm = pl.BlockSpec(memory_space=pltpu.HBM)
    hot_shape = (elements // GROUP, width, GROUP * LANES)
    tile_shape = (bcol, HALVES, panel_dev, brow * panel_dev)

    def padded_shape(shape):
        blocks = max(shape[0], -(-48 * MIB // (2 * math.prod(shape[1:]))))
        return shape_of((blocks,) + shape[1:], BF16)

    def sweep(field, rhs, weight, halo=(), weight_before=None, hot=None):
        rows = parts * columns
        lanes = GROUP * LANES
        build = hot is None
        more = () if build else (hot, *halo)
        return call(
            functools.partial(sweep_kernel, parts, weight, weight_before, build),
            (field_shape, padded_shape(hot_shape)) if build else field_shape,
            5_000_000_000,
            limit=24,
            in_specs=[smem, smem] + [vmem] * 5 + [hbm] * (not build) + [vmem] * len(halo),
            out_specs=(vmem, hbm) if build else vmem,
            scratch_shapes=[pltpu.VMEM((columns, count), F32)] * bool(halo)
            + [
                pltpu.VMEM(hot_shape, BF16),
                pltpu.SemaphoreType.DMA((hot_shape[0],)),
                pltpu.VMEM((rows, width), BF16),
                pltpu.VMEM((rows, width), BF16),
                pltpu.VMEM((2, rows, lanes), F32),
                pltpu.VMEM((2, GROUP * columns, 2 * LANES), BF16),
                pltpu.VMEM((2, rows, lanes), BF16),
                pltpu.VMEM((2, rows, lanes), BF16),
                pltpu.VMEM((rows, width), F32),
            ],
        )(rank, element_coef, field, rhs, mass, keys, matrix, *more)

    def add_loads(chunks, field, halo, weight):
        return call(
            functools.partial(loads_kernel, parts, brow, weight, used),
            (field_shape, field_shape, rim_shape, rim_shape),
            500_000_000,
            in_specs=[smem] + [vmem] * 7,
            out_specs=(vmem,) * 4,
        )(rank, load_nodes, chunks, forcing, field, *halo, mass)

    parts_shape = shape_of((brow, columns, panel_dev), F32)
    sizes = (brow, bcol, panel_dev, slot_rows)
    tile_mib = -(-(2 * math.prod(tile_shape)) // MIB)

    def swap_parts(parts_out):
        return lax.all_to_all(parts_out, "brow", split_axis=0, concat_axis=0, tiled=True)

    nodes, load_nodes, chunks, *rim = call(
        functools.partial(setup_kernel, parts, brow, bcol, panel_dev, slot_rows),
        (
            table_shape(slot_rows),
            table_shape(LOAD_ROWS),
            chunk_shape(used + LOAD_ROWS + POINT_ROWS, 16),
            rim_shape,
            rim_shape,
        ),
        2_000_000_000,
        limit=56,
        in_specs=[smem] + [vmem] * 4,
        out_specs=(vmem,) * 5,
    )(rank, panel_map, field_start, potential_start, panel_points)
    halo = exchange(*rim)
    chunks = swap_all(chunks)
    field, hot = sweep(field_start, forcing, weights[0])
    parts_out, tiles = call(
        functools.partial(tile_kernel, *sizes),
        (parts_shape, padded_shape(tile_shape)),
        8_000_000_000,
        limit=16 + tile_mib,
        grid=(bcol,),
        in_specs=[smem, vmem, vmem],
        out_specs=(vmem, hbm),
        scratch_shapes=[
            pltpu.VMEM((16, brow * panel_dev), BF16),
            pltpu.VMEM((bcol, columns, panel_dev), BF16),
            pltpu.VMEM((bcol, columns, panel_dev), BF16),
            pltpu.VMEM((panel_dev, brow * panel_dev), F32),
            pltpu.VMEM(tile_shape, BF16),
            pltpu.VMEM((columns, brow * panel_dev), F32),
            pltpu.SemaphoreType.DMA((bcol,)),
        ],
    )(rank, panel_map, chunks)
    parts_in = swap_parts(parts_out)
    rhs, field, *rim = add_loads(chunks, field, halo, weights[0])
    halo = exchange(*rim)
    field = sweep(field, rhs, weights[1], hot=hot)
    halo_next = exchange(*rims(field, halo, weights[1]))
    field = sweep(field, rhs, weights[2], halo, weights[1], hot)
    field, chunks, *rim = call(
        functools.partial(finish_kernel, parts, brow, bcol, panel_dev, slot_rows, weights[2]),
        (field_shape, chunk_shape(used + LOAD_ROWS, 8), rim_shape, rim_shape),
        1_000_000_000,
        in_specs=[smem] + [vmem] * 7,
        out_specs=(vmem,) * 4,
    )(rank, panel_map, nodes, field, *halo_next, mass, parts_in)

    halo = exchange(*rim)
    chunks = swap_all(chunks)
    field = sweep(field, forcing, weights[0], hot=hot)
    parts_out = call(
        functools.partial(potential_kernel, *sizes),
        parts_shape,
        2_000_000_000,
        limit=16 + tile_mib,
        in_specs=[smem, vmem, vmem, hbm],
        out_specs=vmem,
        scratch_shapes=[pltpu.VMEM(tile_shape, BF16), pltpu.SemaphoreType.DMA((bcol,))],
    )(rank, panel_map, chunks, tiles)
    parts_in = swap_parts(parts_out)
    rhs, field, *rim = add_loads(chunks, field, halo, weights[0])
    halo = exchange(*rim)
    field = sweep(field, rhs, weights[1], hot=hot)
    halo_next = exchange(*rims(field, halo, weights[1]))
    field = sweep(field, rhs, weights[2], halo, weights[1], hot)
    return call(
        functools.partial(last_kernel, weights[2]),
        (field_shape, shape_of((columns, panel_dev), F32)),
        100_000_000,
        in_specs=[smem] + [vmem] * 5,
        out_specs=(vmem, vmem),
    )(rank, field, *halo_next, mass, parts_in)


def solution(mesh):
    placed = (
        P(None, AXES),
        P(),
        P(None, AXES),
        P(AXES),
        P(),
        P(AXES),
        P(None, AXES),
        P(None, AXES),
        P(None, AXES),
    )
    return jax.shard_map(
        per_device,
        mesh=mesh,
        in_specs=placed,
        out_specs=(P(None, AXES), P(None, AXES)),
        check_vma=False,
    )
```

```python
import functools
import math

import jax
import jax.numpy as jnp
from jax import lax
from jax.experimental import pallas as pl
from jax.experimental.pallas import tpu as pltpu
from jax.sharding import PartitionSpec as P

RIM = 128
SWEEPS = 3
LANES = 128
LOAD_ROWS = 8
POINT_ROWS = 8
HALVES = 2
GROUP = 8
BLOCKS = 4

wave_number = 20.0
penalty = 0.5

AXES = ("brow", "bcol")
F32 = jnp.float32
BF16 = jnp.bfloat16

SIN_POLY = (3.14159264, -5.16771008, 2.55007752, -0.59829129, 0.07765766)
COS_POLY = (0.99999995, -4.93479283, 4.05841135, -1.33187657, 0.21968961)

MIB = 1024 * 1024


def weight_of(sweep):
    return 1.0 / (1.25 + 0.75 * math.cos(math.pi * (2 * sweep + 1) / (2.0 * SWEEPS)))


def call(kernel, out_shape, cost, limit=28, **more):
    return pl.pallas_call(
        kernel,
        out_shape=out_shape,
        compiler_params=pltpu.CompilerParams(vmem_limit_bytes=limit * MIB),
        cost_estimate=pl.CostEstimate(flops=cost, bytes_accessed=1 << 20, transcendentals=0),
        **more,
    )


def shape_of(shape, dtype):
    return jax.ShapeDtypeStruct(shape, dtype)


def kept(shape, dtype):
    return pltpu.VMEM(shape, dtype)


def in_hbm(*arrays):
    return tuple(pltpu.with_memory_space_constraint(array, pltpu.HBM) for array in arrays)


def in_vmem(*arrays):
    return tuple(pltpu.with_memory_space_constraint(array, pltpu.VMEM) for array in arrays)


def dot(a, b):
    return jnp.dot(a, b, preferred_element_type=F32)


def dot_nt(a, b):
    return lax.dot_general(a, b, (((1,), (1,)), ((), ())), preferred_element_type=F32)


def split_two(value):
    high = value.astype(BF16)
    return high, (value - high.astype(F32)).astype(BF16)


def low_part(value, size):
    return value & (size - 1) if size & (size - 1) == 0 else value % size


def high_part(value, size):
    return value >> (size.bit_length() - 1) if size & (size - 1) == 0 else value // size


def stack_parts(value, parts):
    width = value.shape[1] // parts
    return jnp.concatenate([value[:, i * width : (i + 1) * width] for i in range(parts)], axis=0)


def one_hot_rows(key, rows):
    seen = lax.broadcasted_iota(jnp.int16, (rows, key.shape[1]), 0)
    return jnp.where(seen == key.astype(jnp.int16), BF16(1), BF16(0))


def pick_part(stacked, part, parts):
    rows = stacked.shape[0] // parts
    picked = stacked[(parts - 1) * rows :]
    for i in reversed(range(parts - 1)):
        picked = jnp.where(part == i, stacked[i * rows : (i + 1) * rows], picked)
    return picked


def gather_nodes(field, nodes, parts):
    width = field.shape[1] // parts
    hot = one_hot_rows(jnp.where(nodes < 0, -1, low_part(nodes, width)), width)
    found = dot(stack_parts(field.astype(BF16), parts), hot)
    return pick_part(found, high_part(nodes, width), parts)


def scatter_nodes(values, nodes, parts, count):
    width = count // parts
    hot = one_hot_rows(jnp.where(nodes < 0, -1, low_part(nodes, width)), width)
    masked = jnp.concatenate(
        [jnp.where(high_part(nodes, width) == i, values, 0.0) for i in range(parts)], axis=0
    ).astype(BF16)
    added = dot_nt(masked, hot)
    rows = values.shape[0]
    return jnp.concatenate([added[i * rows : (i + 1) * rows] for i in range(parts)], axis=1)


def halves_of(slot, rows):
    half = jnp.where(slot >= rows, 1, 0)
    return half, slot - half * rows


def trace_rows(field, nodes, parts, brow, used):
    turned = jnp.transpose(gather_nodes(field, nodes, parts))
    span = turned.shape[0] // brow
    return [
        jnp.concatenate(
            [turned[r * span : r * span + used], turned[r * span + used : r * span + 2 * used]], axis=1
        )
        for r in range(brow)
    ]


def own_panels(map_ref, rank, panel_dev):
    first = rank * panel_dev
    base = (first >> 7) << 7
    window = -(-panel_dev // LANES) * LANES
    near = map_ref[:, pl.ds(pl.multiple_of(base, LANES), window)]
    return jnp.where(first == base, near[:, :panel_dev], near[:, window - panel_dev :])


def load_rows(potential, own_map, devices, slot_rows):
    owner, slot = own_map[0:1], own_map[1:2]
    half, low = halves_of(slot, slot_rows)
    rows = devices * LOAD_ROWS
    key = half * rows + owner * LOAD_ROWS + low
    found = dot_nt(one_hot_rows(key, HALVES * rows), potential.astype(BF16))
    return jnp.concatenate([found[:rows], found[rows:]], axis=1).reshape(devices, LOAD_ROWS, LANES)


def node_tables(map_ref, rank, brow, bcol, panel_dev, slot_rows, stride):
    row_panels = bcol * panel_dev
    row_slots = -(-HALVES * bcol * stride // LANES) * LANES
    lane = lax.broadcasted_iota(jnp.int32, (1, row_panels), 1).astype(F32)
    block = jnp.floor((lane + 0.5) * (1.0 / panel_dev)).astype(jnp.int32)
    row_id = lax.broadcasted_iota(jnp.int32, (8, row_panels), 0)
    tables = []
    for r in range(brow):
        span = slice(r * row_panels, (r + 1) * row_panels)
        owner, slot, node = map_ref[0:1, span], map_ref[1:2, span], map_ref[2:3, span]
        half, low = halves_of(slot, slot_rows)
        key = jnp.where(owner == rank, half * (bcol * stride) + block * stride + low, -1)
        values = jnp.where(
            row_id == 0, high_part(node, 256), jnp.where(row_id == 1, low_part(node, 256), 1)
        ).astype(F32).astype(BF16)
        found = dot_nt(values, one_hot_rows(key, row_slots))
        table = jnp.where(found[2:3] > 0.5, found[0:1] * 256.0 + found[1:2], -1.0)
        tables.append(table.astype(jnp.int32))
    return jnp.concatenate(tables, axis=1)


def point_rows(points):
    row_id = lax.broadcasted_iota(jnp.int32, (POINT_ROWS, LANES), 0)
    each = POINT_ROWS // 3
    width = points.shape[1]
    value = jnp.zeros((POINT_ROWS, LANES), F32)
    for axis in range(3):
        for part in range(-(-width // LANES)):
            piece = points[axis : axis + 1, part * LANES : (part + 1) * LANES]
            short = LANES - piece.shape[1]
            if short:
                piece = jnp.concatenate([piece, jnp.zeros((1, short), F32)], axis=1)
            value = jnp.where(row_id == axis * each + part, piece, value)
    return value


def write_chunks(chunk_ref, pieces, loads, bcol, points=None):
    used = pieces[0].shape[0]
    for r, piece in enumerate(pieces):
        for c in range(bcol):
            device = r * bcol + c
            rows = [piece, loads[device]] + ([] if points is None else [points])
            left = chunk_ref.shape[1] - used - LOAD_ROWS - (0 if points is None else POINT_ROWS)
            if left:
                rows.append(jnp.zeros((left, LANES), F32))
            chunk_ref[device] = jnp.concatenate(rows, axis=0).astype(BF16)


def write_rims(field, even, first_ref, second_ref):
    low = field[:, :RIM]
    high = field[:, field.shape[1] - RIM :]
    first_ref[...] = jnp.where(even, high, low).astype(BF16)
    second_ref[...] = jnp.where(even, low, high).astype(BF16)


def setup_kernel(
    parts, brow, bcol, panel_dev, slot_rows, rank_ref, map_ref, field_ref, potential_ref, points_ref,
    element_nodes_ref, element_matrix_ref, node_mass_ref,
    nodes_ref, load_nodes_ref, row_map_ref, own_map_ref, keys_ref, matrix_ref, mass_ref,
    chunk_ref, rim_first_ref, rim_second_ref,
):
    rank = rank_ref[0]
    row_panels = bcol * panel_dev
    base = pl.multiple_of(high_part(rank, bcol) * row_panels, LANES)
    row_map_ref[...] = map_ref[:, pl.ds(base, row_panels)]
    own_map = own_panels(map_ref, rank, panel_dev)
    own_map_ref[...] = own_map
    keys_ref[...] = jnp.zeros_like(keys_ref)
    keys_ref[:, : element_nodes_ref.shape[1]] = element_nodes_ref[...]
    matrix_ref[...] = jnp.zeros_like(matrix_ref)
    matrix_ref[: element_matrix_ref.shape[0], : element_matrix_ref.shape[1]] = element_matrix_ref[...]
    mass_ref[...] = node_mass_ref[...]
    tables = functools.partial(node_tables, map_ref, rank, brow, bcol, panel_dev, slot_rows)
    nodes = tables(slot_rows)
    nodes_ref[...] = jnp.broadcast_to(nodes, nodes_ref.shape)
    load_nodes_ref[...] = jnp.broadcast_to(tables(LOAD_ROWS), load_nodes_ref.shape)
    field = field_ref[...]
    write_rims(field, low_part(rank, 2) == 0, rim_first_ref, rim_second_ref)
    loads = load_rows(potential_ref[...], own_map, brow * bcol, slot_rows)
    pieces = trace_rows(field, nodes, parts, brow, bcol * slot_rows)
    write_chunks(chunk_ref, pieces, loads, bcol, point_rows(points_ref[...].astype(F32)))


def rim_correction(value, even, first_ref, second_ref, mass, weight):
    step = weight * penalty
    first, second = first_ref[...].astype(F32), second_ref[...].astype(F32)
    left, right = jnp.where(even, second, first), jnp.where(even, first, second)
    last = value.shape[1] - RIM
    low = value[:, :RIM] + step * left / mass[:, :RIM]
    high = value[:, last:] + step * right / mass[:, last:]
    return jnp.concatenate([low, value[:, RIM:last], high], axis=1)


def received_loads(chunk_ref, used, brow, columns):
    received = chunk_ref[...].astype(F32)[:, used : used + LOAD_ROWS]
    received = received.reshape(received.shape[0] * LOAD_ROWS, LANES)
    span = received.shape[0] // brow
    rows = []
    for r in range(brow):
        piece = received[r * span : (r + 1) * span]
        rows += [piece[:, :columns], piece[:, columns : HALVES * columns]]
    return jnp.transpose(jnp.concatenate(rows, axis=0))


def sweep_kernel(
    parts, weight, weight_before, build, rank_ref, coef_ref, field_ref, rhs_ref, mass_ref, keys_ref,
    matrix_ref, *more_refs,
):
    if build:
        out_ref, hot_ref, total_ref, sem, *scratch = more_refs
        copy = pltpu.make_async_copy(rhs_ref, total_ref, sem)
        copy.start()
        rhs_ref = total_ref
    elif weight_before is None:
        hot_ref, out_ref, *scratch = more_refs
    else:
        hot_ref, first_ref, second_ref, out_ref, field_scr, *scratch = more_refs
    high_ref, low_ref, found_ref, local_ref, yhigh_ref, ylow_ref, sum_ref = scratch
    groups = hot_ref.shape[0]
    columns, count = field_ref.shape
    width = count // parts
    mass = mass_ref[...]
    if weight_before is None:
        field = field_ref[...]
        field_now = field_ref
    else:
        even = low_part(rank_ref[0], 2) == 0
        field = rim_correction(field_ref[...], even, first_ref, second_ref, mass, weight_before)
        field_scr[...] = field
        field_now = field_scr
    high, low = split_two(field)
    for h in range(parts):
        high_ref[h * columns : (h + 1) * columns] = high[:, h * width : (h + 1) * width]
        low_ref[h * columns : (h + 1) * columns] = low[:, h * width : (h + 1) * width]
    mat_high, mat_low = split_two(matrix_ref[...])
    matrix = jnp.concatenate(
        [
            jnp.concatenate([mat_high, mat_low], axis=1),
            jnp.concatenate([mat_high, jnp.zeros_like(mat_low)], axis=1),
        ],
        axis=0,
    )

    def gather(group):
        if build:
            for e in range(GROUP):
                key = keys_ref[group * GROUP + e : group * GROUP + e + 1, :]
                hot_ref[group, :, e * LANES : (e + 1) * LANES] = one_hot_rows(low_part(key, width), width)
        hot = hot_ref[group]
        found_ref[group % 2] = dot(high_ref[...], hot) + dot(low_ref[...], hot)

    def multiply(group):
        slot = group % 2
        for e in range(GROUP):
            element = group * GROUP + e
            key = keys_ref[element : element + 1, :]
            got = pick_part(found_ref[slot, :, e * LANES : (e + 1) * LANES], high_part(key, width), parts)
            got_high, got_low = split_two(got)
            local_ref[slot, e * columns : (e + 1) * columns, :LANES] = got_high
            local_ref[slot, e * columns : (e + 1) * columns, LANES:] = got_low

        product = dot(local_ref[slot], matrix)
        for e in range(GROUP):
            element = group * GROUP + e
            part = high_part(keys_ref[element : element + 1, :], width)
            rows = product[e * columns : (e + 1) * columns]
            value = (rows[:, :LANES] + rows[:, LANES:]) * coef_ref[element]
            value_high, value_low = split_two(value)
            span = slice(e * LANES, (e + 1) * LANES)
            for h in range(parts):
                mask = jnp.where(part == h, 1.0, 0.0).astype(BF16)
                yhigh_ref[slot, h * columns : (h + 1) * columns, span] = value_high * mask
                ylow_ref[slot, h * columns : (h + 1) * columns, span] = value_low * mask

    def scatter(group):
        hot = hot_ref[group]
        added = dot_nt(yhigh_ref[group % 2], hot) + dot_nt(ylow_ref[group % 2], hot)
        sum_ref[...] = added if group == 0 else sum_ref[...] + added

    gather(0)
    for group in range(groups):
        if group + 1 < groups:
            gather(group + 1)
        multiply(group)
        scatter(group)
    if build:
        copy.wait()
    for h in range(parts):
        span = slice(h * width, (h + 1) * width)
        stiff = sum_ref[h * columns : (h + 1) * columns]
        out_ref[:, span] = (1.0 - weight) * field_now[:, span] + weight * (
            rhs_ref[:, span] - stiff
        ) / mass[:, span]


def loads_kernel(
    parts, brow, weight, used, rank_ref, nodes_ref, chunk_ref, forcing_ref, field_ref, first_ref,
    second_ref, mass_ref, rhs_ref, out_ref, rim_first_ref, rim_second_ref,
):
    columns, count = field_ref.shape
    loads = received_loads(chunk_ref, used, brow, columns)
    added = scatter_nodes(loads, nodes_ref[0:1, :], parts, count)
    rhs_ref[...] = forcing_ref[...] + added
    mass = mass_ref[...]
    even = low_part(rank_ref[0], 2) == 0
    field = field_ref[...] + weight * added / mass
    field = rim_correction(field, even, first_ref, second_ref, mass, weight)
    out_ref[...] = field
    write_rims(field, even, rim_first_ref, rim_second_ref)


def total(parts_ref):
    value = parts_ref[0]
    for r in range(1, parts_ref.shape[0]):
        value = value + parts_ref[r]
    return value


def finish_kernel(
    parts, brow, bcol, panel_dev, slot_rows, weight, rank_ref, own_map_ref, nodes_ref, field_ref,
    first_ref, second_ref, mass_ref, parts_ref, out_ref, chunk_ref, rim_first_ref, rim_second_ref,
):
    rank = rank_ref[0]
    even = low_part(rank, 2) == 0
    field = rim_correction(field_ref[...], even, first_ref, second_ref, mass_ref[...], weight)
    out_ref[...] = field
    write_rims(field, even, rim_first_ref, rim_second_ref)
    loads = load_rows(total(parts_ref), own_map_ref[...], brow * bcol, slot_rows)
    pieces = trace_rows(field, nodes_ref[0:1, :], parts, brow, bcol * slot_rows)
    write_chunks(chunk_ref, pieces, loads, bcol)


def last_kernel(
    weight, rank_ref, field_ref, first_ref, second_ref, mass_ref, parts_ref, out_ref, potential_ref
):
    even = low_part(rank_ref[0], 2) == 0
    out_ref[...] = rim_correction(field_ref[...], even, first_ref, second_ref, mass_ref[...], weight)
    potential_ref[...] = total(parts_ref)


def density_groups(map_ref, chunk_ref, brow, bcol, panel_dev, slot_rows):
    devices = brow * bcol
    columns = LANES // HALVES
    rows = BLOCKS * slot_rows
    panels = BLOCKS * panel_dev
    lane = lax.broadcasted_iota(jnp.int32, (1, panels), 1).astype(F32)
    block = jnp.floor((lane + 0.5) * (1.0 / panel_dev)).astype(jnp.int32)
    traces = chunk_ref[...].astype(F32)
    for group in range(bcol // BLOCKS):
        span = slice(group * panels, (group + 1) * panels)
        owner, slot = map_ref[0:1, span], map_ref[1:2, span]
        half, low = halves_of(slot, slot_rows)
        key = owner * rows + block * slot_rows + low
        near = traces[:, group * rows : (group + 1) * rows].reshape(devices * rows, LANES)
        found = dot(jnp.transpose(near).astype(BF16), one_hot_rows(key, devices * rows))
        density = jnp.where(half == 0, found[:columns], found[columns:])
        turned = jnp.concatenate([-density[columns // 2 :], density[: columns // 2]], axis=0)
        yield density.astype(BF16), turned.astype(BF16)


def write_parts(out_ref, total, panel_dev):
    for r in range(out_ref.shape[0]):
        out_ref[r] = total[:, r * panel_dev : (r + 1) * panel_dev]


def split_three(value):
    high = value.astype(BF16).astype(F32)
    middle = (value - high).astype(BF16).astype(F32)
    return [high, middle, value - high - middle]


def squares(axes):
    return sum(row * row for row in axes[1:]) + axes[0] * axes[0]


def rows_of(rows, dtype=BF16):
    row_id = lax.broadcasted_iota(jnp.int32, (16, rows[0].shape[1]), 0)
    value = jnp.zeros(row_id.shape, F32)
    for index, row in enumerate(rows):
        value = jnp.where(row_id == index, row, value)
    return value.astype(dtype)


def tile_kernel(
    brow, bcol, panel_dev, slot_rows, rank_ref, map_ref, chunk_ref, out_ref, tile_ref,
    target_ref, density_ref, turned_ref, distance_ref, sum_ref,
):
    count_all = brow * bcol * panel_dev
    soften = 0.5 * float(count_all) ** (-1.0 / 3.0)
    each = POINT_ROWS // 3
    row_index, col_index = high_part(rank_ref[0], bcol), low_part(rank_ref[0], bcol)
    start = bcol * slot_rows + LOAD_ROWS
    block = pl.program_id(0)

    def points_of(device):
        return chunk_ref[device].astype(F32)[start : start + POINT_ROWS]

    @pl.when(block == 0)
    def prepare():
        near = [points_of(r * bcol + col_index) for r in range(brow)]
        axes = []
        for axis in range(3):
            rows = []
            for piece in near:
                for part in range(each):
                    wide = min(LANES, panel_dev - part * LANES)
                    rows.append(piece[axis * each + part : axis * each + part + 1, :wide])
            axes.append(jnp.concatenate(rows, axis=1))
        norms = split_three(squares(axes) + soften * soften)
        target_ref[...] = rows_of([-2.0 * row for row in axes] + [jnp.ones_like(axes[0])] * 3 + norms)
        sum_ref[...] = jnp.zeros_like(sum_ref)
        groups = density_groups(map_ref, chunk_ref, brow, bcol, panel_dev, slot_rows)
        for group, (density, turned) in enumerate(groups):
            for k in range(BLOCKS):
                span = slice(k * panel_dev, (k + 1) * panel_dev)
                density_ref[group * BLOCKS + k] = density[:, span]
                turned_ref[group * BLOCKS + k] = turned[:, span]

    piece = points_of(row_index * bcol + block)
    axes = [
        jnp.concatenate([piece[axis * each + part : axis * each + part + 1] for part in range(each)], axis=1)
        for axis in range(3)
    ]
    norms = split_three(squares(axes))
    source = jnp.transpose(rows_of(axes + norms + [jnp.ones_like(axes[0])] * 3, F32)).astype(BF16)
    distance_ref[...] = dot(source[:panel_dev], target_ref[...])
    step = 16
    for top in range(0, panel_dev, step):
        squared = distance_ref[top : top + step]
        inverse = lax.rsqrt(squared)
        turns = (squared * inverse) * (wave_number / (2.0 * math.pi))
        turns = turns - jnp.floor(turns + 0.5)
        z = turns * turns
        sine = jnp.full_like(z, SIN_POLY[-1])
        for factor in SIN_POLY[-2::-1]:
            sine = sine * z + factor
        sine = sine * turns
        cosine = jnp.full_like(z, COS_POLY[-1])
        for factor in COS_POLY[-2::-1]:
            cosine = cosine * z + factor
        double = sine * (inverse * (2.0 / math.sqrt(float(count_all))))
        tile_ref[block, 0, top : top + step] = (
            inverse * (1.0 / math.sqrt(float(count_all))) - sine * double
        ).astype(BF16)
        tile_ref[block, 1, top : top + step] = (cosine * double).astype(BF16)
    sum_ref[...] += dot(density_ref[block], tile_ref[block, 0]) + dot(
        turned_ref[block], tile_ref[block, 1]
    )

    @pl.when(block == bcol - 1)
    def end():
        write_parts(out_ref, sum_ref[...], panel_dev)


def potential_kernel(
    brow, bcol, panel_dev, slot_rows, map_ref, chunk_ref, tile_ref, out_ref,
):
    whole = None
    groups = density_groups(map_ref, chunk_ref, brow, bcol, panel_dev, slot_rows)
    for group, (density, turned) in enumerate(groups):
        for k in range(BLOCKS):
            block = group * BLOCKS + k
            span = slice(k * panel_dev, (k + 1) * panel_dev)
            part = dot(density[:, span], tile_ref[block, 0]) + dot(turned[:, span], tile_ref[block, 1])
            whole = part if whole is None else whole + part
    write_parts(out_ref, whole, panel_dev)


def per_device(
    panel_points,
    panel_map,
    element_nodes,
    element_coef,
    element_matrix,
    node_mass,
    forcing,
    field_start,
    potential_start,
):
    columns, panel_dev = potential_start.shape
    count = field_start.shape[1]
    brow, bcol = lax.axis_size("brow"), lax.axis_size("bcol")
    devices = brow * bcol
    capacity = max(2, 2 * panel_dev // devices)
    slot_rows = -(-capacity // HALVES)
    used = bcol * slot_rows
    assert slot_rows <= LOAD_ROWS and columns * HALVES == LANES and bcol % BLOCKS == 0
    parts = 256 // columns
    width = count // parts
    row_panels = bcol * panel_dev
    row_index, col_index = lax.axis_index("brow"), lax.axis_index("bcol")
    rank = (row_index * bcol + col_index).reshape(1)
    nodes_each, elements = element_nodes.shape
    assert elements % GROUP == 0
    smem = pl.BlockSpec(memory_space=pltpu.SMEM)
    vmem = pl.BlockSpec(memory_space=pltpu.VMEM)
    rim_shape = shape_of((columns, RIM), BF16)
    field_shape = shape_of((columns, count), F32)
    weights = [weight_of(sweep_index) for sweep_index in range(SWEEPS)]
    even_pairs = [(i, i ^ 1) for i in range(devices)]
    odd_pairs = [pair for i in range(1, devices - 1, 2) for pair in ((i, i + 1), (i + 1, i))]
    even = (rank[0] & 1) == 0

    def chunk_shape(rows, unit):
        return shape_of((devices, -(-rows // unit) * unit, LANES), BF16)

    def table_shape(stride):
        return 8, brow * (-(-HALVES * bcol * stride // LANES) * LANES)

    def exchange(first, second):
        return lax.ppermute(first, AXES, even_pairs), lax.ppermute(second, AXES, odd_pairs)

    def rims(field, halo, weight):
        first, second = (piece.astype(F32) for piece in halo)
        left, right = jnp.where(even, second, first), jnp.where(even, first, second)
        last = count - RIM
        low = field[:, :RIM] + (weight * penalty) * left / node_mass[:RIM]
        high = field[:, last:] + (weight * penalty) * right / node_mass[last:]
        return jnp.where(even, high, low).astype(BF16), jnp.where(even, low, high).astype(BF16)

    def swap_all(chunks):
        return lax.all_to_all(chunks, AXES, split_axis=0, concat_axis=0, tiled=True)

    hbm = pl.BlockSpec(memory_space=pltpu.HBM)
    hot_shape = (elements // GROUP, width, GROUP * LANES)
    tile_shape = (bcol, HALVES, panel_dev, brow * panel_dev)

    def sweep(field, rhs, weight, halo=(), weight_before=None, hot=None):
        rows = parts * columns
        lanes = GROUP * LANES
        build = hot is None
        if build:
            given = (rank, *in_hbm(element_coef, field, rhs), *in_vmem(mass, keys, matrix))
        else:
            given = (rank, *in_hbm(element_coef), field, rhs, *in_vmem(mass, keys, matrix, hot), *halo)
        return call(
            functools.partial(sweep_kernel, parts, weight, weight_before, build),
            (field_shape, kept(hot_shape, BF16), kept((columns, count), F32)) if build else field_shape,
            5_000_000_000,
            in_specs=[smem, smem, vmem, hbm if build else vmem] + [vmem] * (len(given) - 4),
            out_specs=(vmem,) * 3 if build else vmem,
            scratch_shapes=[pltpu.SemaphoreType.DMA] * build
            + [pltpu.VMEM((columns, count), F32)] * bool(halo)
            + [
                pltpu.VMEM((rows, width), BF16),
                pltpu.VMEM((rows, width), BF16),
                pltpu.VMEM((2, rows, lanes), F32),
                pltpu.VMEM((2, GROUP * columns, 2 * LANES), BF16),
                pltpu.VMEM((2, rows, lanes), BF16),
                pltpu.VMEM((2, rows, lanes), BF16),
                pltpu.VMEM((rows, width), F32),
            ],
        )(*given)

    def add_loads(chunks, field, halo, weight):
        return call(
            functools.partial(loads_kernel, parts, brow, weight, used),
            (field_shape, field_shape, rim_shape, rim_shape),
            500_000_000,
            in_specs=[smem] + [vmem] * 7,
            out_specs=(vmem,) * 4,
        )(rank, *in_vmem(load_nodes), chunks, *in_vmem(forcing_kept), field, *halo, *in_vmem(mass))

    parts_shape = shape_of((brow, columns, panel_dev), F32)
    sizes = (brow, bcol, panel_dev, slot_rows)

    def swap_parts(parts_out):
        return lax.all_to_all(parts_out, "brow", split_axis=0, concat_axis=0, tiled=True)

    (nodes, load_nodes, row_map, own_map, keys, matrix, mass, chunks, *rim) = call(
        functools.partial(setup_kernel, parts, brow, bcol, panel_dev, slot_rows),
        (
            kept(table_shape(slot_rows), jnp.int32),
            kept(table_shape(LOAD_ROWS), jnp.int32),
            kept((3, row_panels), jnp.int32),
            kept((3, panel_dev), jnp.int32),
            kept((elements, LANES), jnp.int32),
            kept((LANES, LANES), F32),
            kept((1, count), F32),
            chunk_shape(used + LOAD_ROWS + POINT_ROWS, 16),
            kept(rim_shape.shape, BF16),
            kept(rim_shape.shape, BF16),
        ),
        2_000_000_000,
        in_specs=[smem] + [vmem] * 7,
        out_specs=(vmem,) * 10,
    )(
        rank,
        *in_hbm(
            panel_map, field_start, potential_start, panel_points, element_nodes.T, element_matrix,
            node_mass.reshape(1, count),
        ),
    )
    halo = exchange(*rim)
    chunks = swap_all(chunks)
    field, hot, forcing_kept = sweep(field_start, forcing, weights[0])
    parts_out, tiles = call(
        functools.partial(tile_kernel, *sizes),
        (parts_shape, kept(tile_shape, BF16)),
        8_000_000_000,
        grid=(bcol,),
        in_specs=[smem, vmem, vmem],
        out_specs=(vmem, vmem),
        scratch_shapes=[
            pltpu.VMEM((16, brow * panel_dev), BF16),
            pltpu.VMEM((bcol, columns, panel_dev), BF16),
            pltpu.VMEM((bcol, columns, panel_dev), BF16),
            pltpu.VMEM((panel_dev, brow * panel_dev), F32),
            pltpu.VMEM((columns, brow * panel_dev), F32),
        ],
    )(rank, *in_vmem(row_map), chunks)
    parts_in = swap_parts(parts_out)
    rhs, field, *rim = add_loads(chunks, field, halo, weights[0])
    halo = exchange(*rim)
    field = sweep(field, rhs, weights[1], hot=hot)
    halo_next = exchange(*rims(field, halo, weights[1]))
    field = sweep(field, rhs, weights[2], halo, weights[1], hot)
    field, chunks, *rim = call(
        functools.partial(finish_kernel, parts, brow, bcol, panel_dev, slot_rows, weights[2]),
        (field_shape, chunk_shape(used + LOAD_ROWS, 8), rim_shape, rim_shape),
        1_000_000_000,
        in_specs=[smem] + [vmem] * 7,
        out_specs=(vmem,) * 4,
    )(rank, *in_vmem(own_map, nodes), field, *halo_next, *in_vmem(mass), parts_in)

    halo = exchange(*rim)
    chunks = swap_all(chunks)
    field = sweep(field, *in_vmem(forcing_kept), weights[0], hot=hot)
    parts_out = call(
        functools.partial(potential_kernel, *sizes),
        parts_shape,
        2_000_000_000,
        in_specs=[vmem] * 3,
        out_specs=vmem,
    )(*in_vmem(row_map), chunks, *in_vmem(tiles))
    parts_in = swap_parts(parts_out)
    rhs, field, *rim = add_loads(chunks, field, halo, weights[0])
    halo = exchange(*rim)
    field = sweep(field, rhs, weights[1], hot=hot)
    halo_next = exchange(*rims(field, halo, weights[1]))
    field = sweep(field, rhs, weights[2], halo, weights[1], hot)
    return call(
        functools.partial(last_kernel, weights[2]),
        (field_shape, shape_of((columns, panel_dev), F32)),
        100_000_000,
        in_specs=[smem] + [vmem] * 5,
        out_specs=(vmem, vmem),
    )(rank, field, *halo_next, *in_vmem(mass), parts_in)


def solution(mesh):
    placed = (
        P(None, AXES),
        P(),
        P(None, AXES),
        P(AXES),
        P(),
        P(AXES),
        P(None, AXES),
        P(None, AXES),
        P(None, AXES),
    )
    return jax.shard_map(
        per_device,
        mesh=mesh,
        in_specs=placed,
        out_specs=(P(None, AXES), P(None, AXES)),
        check_vma=False,
    )
```

```python
import functools
import math

import jax
import jax.numpy as jnp
from jax import lax
from jax.experimental import pallas as pl
from jax.experimental.pallas import tpu as pltpu
from jax.sharding import PartitionSpec as P

RIM = 128
SWEEPS = 3
LANES = 128
LOAD_ROWS = 8
POINT_ROWS = 8
HALVES = 2
GROUP = 4
BLOCKS = 4

wave_number = 20.0
penalty = 0.5

AXES = ("brow", "bcol")
F32 = jnp.float32
BF16 = jnp.bfloat16

SIN_POLY = (3.14159264, -5.16771008, 2.55007752, -0.59829129, 0.07765766)
COS_POLY = (0.99999995, -4.93479283, 4.05841135, -1.33187657, 0.21968961)

ROUNDER = 1.5 * 2.0**23
MIB = 1024 * 1024


def weight_of(sweep):
    return 1.0 / (1.25 + 0.75 * math.cos(math.pi * (2 * sweep + 1) / (2.0 * SWEEPS)))


def call(kernel, out_shape, cost, limit=28, **more):
    return pl.pallas_call(
        kernel,
        out_shape=out_shape,
        compiler_params=pltpu.CompilerParams(vmem_limit_bytes=limit * MIB),
        cost_estimate=pl.CostEstimate(flops=cost, bytes_accessed=1 << 20, transcendentals=0),
        **more,
    )


def shape_of(shape, dtype):
    return jax.ShapeDtypeStruct(shape, dtype)


def kept(shape, dtype):
    return pltpu.VMEM(shape, dtype)


def in_hbm(*arrays):
    return tuple(pltpu.with_memory_space_constraint(array, pltpu.HBM) for array in arrays)


def in_vmem(*arrays):
    return tuple(pltpu.with_memory_space_constraint(array, pltpu.VMEM) for array in arrays)


def dot(a, b):
    return jnp.dot(a, b, preferred_element_type=F32)


def dot_nt(a, b):
    return lax.dot_general(a, b, (((1,), (1,)), ((), ())), preferred_element_type=F32)


def split_two(value):
    high = value.astype(BF16)
    return high, (value - high.astype(F32)).astype(BF16)


def low_part(value, size):
    return value & (size - 1) if size & (size - 1) == 0 else value % size


def high_part(value, size):
    return value >> (size.bit_length() - 1) if size & (size - 1) == 0 else value // size


def stack_parts(value, parts):
    width = value.shape[1] // parts
    return jnp.concatenate([value[:, i * width : (i + 1) * width] for i in range(parts)], axis=0)


def one_hot_rows(key, rows):
    seen = lax.broadcasted_iota(jnp.int16, (rows, key.shape[1]), 0)
    return jnp.where(seen == key.astype(jnp.int16), BF16(1), BF16(0))


def pick_part(stacked, part, parts):
    rows = stacked.shape[0] // parts
    picked = stacked[(parts - 1) * rows :]
    for i in reversed(range(parts - 1)):
        picked = jnp.where(part == i, stacked[i * rows : (i + 1) * rows], picked)
    return picked


def gather_nodes(field, nodes, parts):
    width = field.shape[1] // parts
    hot = one_hot_rows(jnp.where(nodes < 0, -1, low_part(nodes, width)), width)
    found = dot(stack_parts(field.astype(BF16), parts), hot)
    return pick_part(found, high_part(nodes, width), parts)


def scatter_nodes(values, nodes, parts, count):
    width = count // parts
    hot = one_hot_rows(jnp.where(nodes < 0, -1, low_part(nodes, width)), width)
    masked = jnp.concatenate(
        [jnp.where(high_part(nodes, width) == i, values, 0.0) for i in range(parts)], axis=0
    ).astype(BF16)
    added = dot_nt(masked, hot)
    rows = values.shape[0]
    return jnp.concatenate([added[i * rows : (i + 1) * rows] for i in range(parts)], axis=1)


def halves_of(slot, rows):
    half = jnp.where(slot >= rows, 1, 0)
    return half, slot - half * rows


def trace_rows(field, nodes, parts, brow, used):
    turned = jnp.transpose(gather_nodes(field, nodes, parts))
    span = turned.shape[0] // brow
    return [
        jnp.concatenate(
            [turned[r * span : r * span + used], turned[r * span + used : r * span + 2 * used]], axis=1
        )
        for r in range(brow)
    ]


def own_panels(map_ref, rank, panel_dev):
    first = rank * panel_dev
    base = (first >> 7) << 7
    window = -(-panel_dev // LANES) * LANES
    near = map_ref[:, pl.ds(pl.multiple_of(base, LANES), window)]
    return jnp.where(first == base, near[:, :panel_dev], near[:, window - panel_dev :])


def load_rows(potential, own_map, devices, slot_rows):
    owner, slot = own_map[0:1], own_map[1:2]
    half, low = halves_of(slot, slot_rows)
    rows = devices * LOAD_ROWS
    key = half * rows + owner * LOAD_ROWS + low
    found = dot_nt(one_hot_rows(key, HALVES * rows), potential.astype(BF16))
    return jnp.concatenate([found[:rows], found[rows:]], axis=1).reshape(devices, LOAD_ROWS, LANES)


def node_tables(map_ref, rank, brow, bcol, panel_dev, slot_rows, stride):
    row_panels = bcol * panel_dev
    row_slots = -(-HALVES * bcol * stride // LANES) * LANES
    lane = lax.broadcasted_iota(jnp.int32, (1, row_panels), 1).astype(F32)
    block = jnp.floor((lane + 0.5) * (1.0 / panel_dev)).astype(jnp.int32)
    row_id = lax.broadcasted_iota(jnp.int32, (8, row_panels), 0)
    tables = []
    for r in range(brow):
        span = slice(r * row_panels, (r + 1) * row_panels)
        owner, slot, node = map_ref[0:1, span], map_ref[1:2, span], map_ref[2:3, span]
        half, low = halves_of(slot, slot_rows)
        key = jnp.where(owner == rank, half * (bcol * stride) + block * stride + low, -1)
        values = jnp.where(
            row_id == 0, high_part(node, 256), jnp.where(row_id == 1, low_part(node, 256), 1)
        ).astype(F32).astype(BF16)
        found = dot_nt(values, one_hot_rows(key, row_slots))
        table = jnp.where(found[2:3] > 0.5, found[0:1] * 256.0 + found[1:2], -1.0)
        tables.append(table.astype(jnp.int32))
    return jnp.concatenate(tables, axis=1)


def point_rows(points):
    row_id = lax.broadcasted_iota(jnp.int32, (POINT_ROWS, LANES), 0)
    each = POINT_ROWS // 3
    width = points.shape[1]
    value = jnp.zeros((POINT_ROWS, LANES), F32)
    for axis in range(3):
        for part in range(-(-width // LANES)):
            piece = points[axis : axis + 1, part * LANES : (part + 1) * LANES]
            short = LANES - piece.shape[1]
            if short:
                piece = jnp.concatenate([piece, jnp.zeros((1, short), F32)], axis=1)
            value = jnp.where(row_id == axis * each + part, piece, value)
    return value


def write_chunks(chunk_ref, pieces, loads, bcol, points=None):
    used = pieces[0].shape[0]
    for r, piece in enumerate(pieces):
        for c in range(bcol):
            device = r * bcol + c
            rows = [piece, loads[device]] + ([] if points is None else [points])
            left = chunk_ref.shape[1] - used - LOAD_ROWS - (0 if points is None else POINT_ROWS)
            if left:
                rows.append(jnp.zeros((left, LANES), F32))
            chunk_ref[device] = jnp.concatenate(rows, axis=0).astype(BF16)


def write_rims(field, even, first_ref, second_ref):
    low = field[:, :RIM]
    high = field[:, field.shape[1] - RIM :]
    first_ref[...] = jnp.where(even, high, low).astype(BF16)
    second_ref[...] = jnp.where(even, low, high).astype(BF16)


def setup_kernel(
    parts, brow, bcol, panel_dev, slot_rows, rank_ref, map_ref, field_ref, potential_ref, points_ref,
    element_nodes_ref, element_matrix_ref, node_mass_ref,
    nodes_ref, load_nodes_ref, row_map_ref, own_map_ref, keys_ref, matrix_ref, mass_ref,
    chunk_ref, rim_first_ref, rim_second_ref,
):
    rank = rank_ref[0]
    row_panels = bcol * panel_dev
    base = pl.multiple_of(high_part(rank, bcol) * row_panels, LANES)
    row_map_ref[...] = map_ref[:, pl.ds(base, row_panels)]
    own_map = own_panels(map_ref, rank, panel_dev)
    own_map_ref[...] = own_map
    keys_ref[...] = jnp.zeros_like(keys_ref)
    keys_ref[:, : element_nodes_ref.shape[1]] = element_nodes_ref[...]
    matrix_ref[...] = jnp.zeros_like(matrix_ref)
    matrix_ref[: element_matrix_ref.shape[0], : element_matrix_ref.shape[1]] = element_matrix_ref[...]
    mass_ref[...] = node_mass_ref[...]
    tables = functools.partial(node_tables, map_ref, rank, brow, bcol, panel_dev, slot_rows)
    nodes = tables(slot_rows)
    nodes_ref[...] = jnp.broadcast_to(nodes, nodes_ref.shape)
    load_nodes_ref[...] = jnp.broadcast_to(tables(LOAD_ROWS), load_nodes_ref.shape)
    field = field_ref[...]
    write_rims(field, low_part(rank, 2) == 0, rim_first_ref, rim_second_ref)
    loads = load_rows(potential_ref[...], own_map, brow * bcol, slot_rows)
    pieces = trace_rows(field, nodes, parts, brow, bcol * slot_rows)
    write_chunks(chunk_ref, pieces, loads, bcol, point_rows(points_ref[...].astype(F32)))


def rim_correction(value, even, first_ref, second_ref, mass, weight):
    step = weight * penalty
    first, second = first_ref[...].astype(F32), second_ref[...].astype(F32)
    left, right = jnp.where(even, second, first), jnp.where(even, first, second)
    last = value.shape[1] - RIM
    low = value[:, :RIM] + step * left / mass[:, :RIM]
    high = value[:, last:] + step * right / mass[:, last:]
    return jnp.concatenate([low, value[:, RIM:last], high], axis=1)


def received_loads(chunk_ref, used, brow, columns):
    received = chunk_ref[...].astype(F32)[:, used : used + LOAD_ROWS]
    received = received.reshape(received.shape[0] * LOAD_ROWS, LANES)
    span = received.shape[0] // brow
    rows = []
    for r in range(brow):
        piece = received[r * span : (r + 1) * span]
        rows += [piece[:, :columns], piece[:, columns : HALVES * columns]]
    return jnp.transpose(jnp.concatenate(rows, axis=0))


def sweep_kernel(
    parts, weight, weight_before, keep, rank_ref, coef_ref, field_ref, rhs_ref, mass_ref, keys_ref,
    matrix_ref, *more_refs,
):
    if keep:
        out_ref, kept_ref, sem, *scratch = more_refs
        copy = pltpu.make_async_copy(rhs_ref, kept_ref, sem)
        copy.start()
        rhs_ref = kept_ref
    elif weight_before is None:
        out_ref, *scratch = more_refs
    else:
        first_ref, second_ref, out_ref, field_scr, *scratch = more_refs
    hot_ref, high_ref, low_ref, found_ref, local_ref, product_ref, yhigh_ref, ylow_ref, sum_ref = scratch
    groups = hot_ref.shape[0]
    columns, count = field_ref.shape
    width = count // parts
    mass = mass_ref[...]
    if weight_before is None:
        field = field_ref[...]
        field_now = field_ref
    else:
        even = low_part(rank_ref[0], 2) == 0
        field = rim_correction(field_ref[...], even, first_ref, second_ref, mass, weight_before)
        field_scr[...] = field
        field_now = field_scr
    high, low = split_two(field)
    for h in range(parts):
        high_ref[h * columns : (h + 1) * columns] = high[:, h * width : (h + 1) * width]
        low_ref[h * columns : (h + 1) * columns] = low[:, h * width : (h + 1) * width]
    mat_high, mat_low = split_two(matrix_ref[...])
    matrix = jnp.concatenate(
        [
            jnp.concatenate([mat_high, mat_low], axis=1),
            jnp.concatenate([mat_high, jnp.zeros_like(mat_low)], axis=1),
        ],
        axis=0,
    )

    def build(group):
        for e in range(GROUP):
            key = keys_ref[group * GROUP + e : group * GROUP + e + 1, :]
            hot_ref[group, :, e * LANES : (e + 1) * LANES] = one_hot_rows(low_part(key, width), width)

    def gather(group):
        hot = hot_ref[group]
        found_ref[group % 2] = dot(high_ref[...], hot) + dot(low_ref[...], hot)

    def pick(group):
        slot = group % 2
        for e in range(GROUP):
            element = group * GROUP + e
            key = keys_ref[element : element + 1, :]
            got = pick_part(found_ref[slot, :, e * LANES : (e + 1) * LANES], high_part(key, width), parts)
            got_high, got_low = split_two(got)
            local_ref[slot, e * columns : (e + 1) * columns, :LANES] = got_high
            local_ref[slot, e * columns : (e + 1) * columns, LANES:] = got_low


    def multiply(group):
        product_ref[group % 2] = dot(local_ref[group % 2], matrix)

    def scale(group):
        slot = group % 2
        for e in range(GROUP):
            element = group * GROUP + e
            part = high_part(keys_ref[element : element + 1, :], width)
            rows = product_ref[slot, e * columns : (e + 1) * columns]
            value = (rows[:, :LANES] + rows[:, LANES:]) * coef_ref[element]
            value_high, value_low = split_two(value)
            span = slice(e * LANES, (e + 1) * LANES)
            for h in range(parts):
                mask = jnp.where(part == h, 1.0, 0.0).astype(BF16)
                yhigh_ref[slot, h * columns : (h + 1) * columns, span] = value_high * mask
                ylow_ref[slot, h * columns : (h + 1) * columns, span] = value_low * mask

    def scatter(group):
        hot = hot_ref[group]
        added = dot_nt(yhigh_ref[group % 2], hot) + dot_nt(ylow_ref[group % 2], hot)
        sum_ref[...] = added if group == 0 else sum_ref[...] + added

    build(0)
    gather(0)
    build(1)
    for group in range(groups):
        pick(group)
        if group + 1 < groups:
            gather(group + 1)
        if group + 2 < groups:
            build(group + 2)
        multiply(group)
        if group:
            scatter(group - 1)
        scale(group)
    scatter(groups - 1)
    if keep:
        copy.wait()
    for h in range(parts):
        span = slice(h * width, (h + 1) * width)
        stiff = sum_ref[h * columns : (h + 1) * columns]
        out_ref[:, span] = (1.0 - weight) * field_now[:, span] + weight * (
            rhs_ref[:, span] - stiff
        ) / mass[:, span]


def loads_kernel(
    parts, brow, weight, used, rank_ref, nodes_ref, chunk_ref, forcing_ref, field_ref, first_ref,
    second_ref, mass_ref, rhs_ref, out_ref, rim_first_ref, rim_second_ref,
):
    columns, count = field_ref.shape
    loads = received_loads(chunk_ref, used, brow, columns)
    added = scatter_nodes(loads, nodes_ref[0:1, :], parts, count)
    rhs_ref[...] = forcing_ref[...] + added
    mass = mass_ref[...]
    even = low_part(rank_ref[0], 2) == 0
    field = field_ref[...] + weight * added / mass
    field = rim_correction(field, even, first_ref, second_ref, mass, weight)
    out_ref[...] = field
    write_rims(field, even, rim_first_ref, rim_second_ref)


def total(parts_ref):
    value = parts_ref[0]
    for r in range(1, parts_ref.shape[0]):
        value = value + parts_ref[r]
    return value


def finish_kernel(
    parts, brow, bcol, panel_dev, slot_rows, weight, rank_ref, own_map_ref, nodes_ref, field_ref,
    first_ref, second_ref, mass_ref, parts_ref, out_ref, chunk_ref, rim_first_ref, rim_second_ref,
):
    rank = rank_ref[0]
    even = low_part(rank, 2) == 0
    field = rim_correction(field_ref[...], even, first_ref, second_ref, mass_ref[...], weight)
    out_ref[...] = field
    write_rims(field, even, rim_first_ref, rim_second_ref)
    loads = load_rows(total(parts_ref), own_map_ref[...], brow * bcol, slot_rows)
    pieces = trace_rows(field, nodes_ref[0:1, :], parts, brow, bcol * slot_rows)
    write_chunks(chunk_ref, pieces, loads, bcol)


def last_kernel(
    weight, rank_ref, field_ref, first_ref, second_ref, mass_ref, parts_ref, out_ref, potential_ref
):
    even = low_part(rank_ref[0], 2) == 0
    out_ref[...] = rim_correction(field_ref[...], even, first_ref, second_ref, mass_ref[...], weight)
    potential_ref[...] = total(parts_ref)


def density_groups(map_ref, chunk_ref, brow, bcol, panel_dev, slot_rows):
    devices = brow * bcol
    columns = LANES // HALVES
    rows = BLOCKS * slot_rows
    panels = BLOCKS * panel_dev
    lane = lax.broadcasted_iota(jnp.int32, (1, panels), 1).astype(F32)
    block = jnp.floor((lane + 0.5) * (1.0 / panel_dev)).astype(jnp.int32)
    traces = chunk_ref[...].astype(F32)
    for group in range(bcol // BLOCKS):
        span = slice(group * panels, (group + 1) * panels)
        owner, slot = map_ref[0:1, span], map_ref[1:2, span]
        half, low = halves_of(slot, slot_rows)
        key = owner * rows + block * slot_rows + low
        near = traces[:, group * rows : (group + 1) * rows].reshape(devices * rows, LANES)
        found = dot(jnp.transpose(near).astype(BF16), one_hot_rows(key, devices * rows))
        density = jnp.where(half == 0, found[:columns], found[columns:])
        turned = jnp.concatenate([-density[columns // 2 :], density[: columns // 2]], axis=0)
        yield density.astype(BF16), turned.astype(BF16)


def write_parts(out_ref, total, panel_dev):
    for r in range(out_ref.shape[0]):
        out_ref[r] = total[:, r * panel_dev : (r + 1) * panel_dev]


def split_three(value):
    high = value.astype(BF16).astype(F32)
    middle = (value - high).astype(BF16).astype(F32)
    return [high, middle, value - high - middle]


def squares(axes):
    return sum(row * row for row in axes[1:]) + axes[0] * axes[0]


def rows_of(rows, dtype=BF16):
    row_id = lax.broadcasted_iota(jnp.int32, (16, rows[0].shape[1]), 0)
    value = jnp.zeros(row_id.shape, F32)
    for index, row in enumerate(rows):
        value = jnp.where(row_id == index, row, value)
    return value.astype(dtype)


def tile_kernel(
    brow, bcol, panel_dev, slot_rows, rank_ref, map_ref, chunk_ref, out_ref, tile_ref,
    target_ref, density_ref, turned_ref, distance_ref, built_ref, sum_ref, sems,
):
    count_all = brow * bcol * panel_dev
    soften = 0.5 * float(count_all) ** (-1.0 / 3.0)
    each = POINT_ROWS // 3
    row_index, col_index = high_part(rank_ref[0], bcol), low_part(rank_ref[0], bcol)
    start = bcol * slot_rows + LOAD_ROWS
    block = pl.program_id(0)

    def points_of(device):
        return chunk_ref[device].astype(F32)[start : start + POINT_ROWS]

    def copy_of(index):
        return pltpu.make_async_copy(built_ref.at[index], tile_ref.at[index], sems.at[index])

    @pl.when(block == 0)
    def prepare():
        near = [points_of(r * bcol + col_index) for r in range(brow)]
        axes = []
        for axis in range(3):
            rows = []
            for piece in near:
                for part in range(each):
                    wide = min(LANES, panel_dev - part * LANES)
                    rows.append(piece[axis * each + part : axis * each + part + 1, :wide])
            axes.append(jnp.concatenate(rows, axis=1))
        norms = split_three(squares(axes) + soften * soften)
        target_ref[...] = rows_of([-2.0 * row for row in axes] + [jnp.ones_like(axes[0])] * 3 + norms)
        sum_ref[...] = jnp.zeros_like(sum_ref)
        groups = density_groups(map_ref, chunk_ref, brow, bcol, panel_dev, slot_rows)
        for group, (density, turned) in enumerate(groups):
            for k in range(BLOCKS):
                span = slice(k * panel_dev, (k + 1) * panel_dev)
                density_ref[group * BLOCKS + k] = density[:, span]
                turned_ref[group * BLOCKS + k] = turned[:, span]

    piece = points_of(row_index * bcol + block)
    axes = [
        jnp.concatenate([piece[axis * each + part : axis * each + part + 1] for part in range(each)], axis=1)
        for axis in range(3)
    ]
    norms = split_three(squares(axes))
    source = jnp.transpose(rows_of(axes + norms + [jnp.ones_like(axes[0])] * 3, F32)).astype(BF16)
    distance_ref[...] = dot(source[:panel_dev], target_ref[...])
    step = 16
    for top in range(0, panel_dev, step):
        squared = distance_ref[top : top + step]
        inverse = lax.rsqrt(squared)
        turns = (squared * inverse) * (wave_number / (2.0 * math.pi))
        turns = turns - ((turns + ROUNDER) - ROUNDER)
        z = turns * turns
        sine = jnp.full_like(z, SIN_POLY[-1])
        for factor in SIN_POLY[-2::-1]:
            sine = sine * z + factor
        sine = sine * turns
        cosine = jnp.full_like(z, COS_POLY[-1])
        for factor in COS_POLY[-2::-1]:
            cosine = cosine * z + factor
        double = sine * (inverse * (2.0 / math.sqrt(float(count_all))))
        built_ref[block, 0, top : top + step] = (
            inverse * (1.0 / math.sqrt(float(count_all))) - sine * double
        ).astype(BF16)
        built_ref[block, 1, top : top + step] = (cosine * double).astype(BF16)
    copy_of(block).start()
    sum_ref[...] += dot(density_ref[block], built_ref[block, 0]) + dot(
        turned_ref[block], built_ref[block, 1]
    )

    @pl.when(block == bcol - 1)
    def end():
        write_parts(out_ref, sum_ref[...], panel_dev)
        for index in range(bcol):
            copy_of(index).wait()


def potential_kernel(
    brow, bcol, panel_dev, slot_rows, map_ref, chunk_ref, tile_ref, out_ref, held_ref, sems,
):
    copies = [
        pltpu.make_async_copy(tile_ref.at[block], held_ref.at[block], sems.at[block])
        for block in range(bcol)
    ]
    for copy in copies:
        copy.start()
    whole = None
    groups = density_groups(map_ref, chunk_ref, brow, bcol, panel_dev, slot_rows)
    for group, (density, turned) in enumerate(groups):
        for k in range(BLOCKS):
            block = group * BLOCKS + k
            copies[block].wait()
            span = slice(k * panel_dev, (k + 1) * panel_dev)
            part = dot(density[:, span], held_ref[block, 0]) + dot(turned[:, span], held_ref[block, 1])
            whole = part if whole is None else whole + part
    write_parts(out_ref, whole, panel_dev)


def per_device(
    panel_points,
    panel_map,
    element_nodes,
    element_coef,
    element_matrix,
    node_mass,
    forcing,
    field_start,
    potential_start,
):
    columns, panel_dev = potential_start.shape
    count = field_start.shape[1]
    brow, bcol = lax.axis_size("brow"), lax.axis_size("bcol")
    devices = brow * bcol
    capacity = max(2, 2 * panel_dev // devices)
    slot_rows = -(-capacity // HALVES)
    used = bcol * slot_rows
    assert slot_rows <= LOAD_ROWS and columns * HALVES == LANES and bcol % BLOCKS == 0
    parts = 256 // columns
    width = count // parts
    row_panels = bcol * panel_dev
    row_index, col_index = lax.axis_index("brow"), lax.axis_index("bcol")
    rank = (row_index * bcol + col_index).reshape(1)
    nodes_each, elements = element_nodes.shape
    assert elements % GROUP == 0
    smem = pl.BlockSpec(memory_space=pltpu.SMEM)
    vmem = pl.BlockSpec(memory_space=pltpu.VMEM)
    rim_shape = shape_of((columns, RIM), BF16)
    field_shape = shape_of((columns, count), F32)
    weights = [weight_of(sweep_index) for sweep_index in range(SWEEPS)]
    even_pairs = [(i, i ^ 1) for i in range(devices)]
    odd_pairs = [pair for i in range(1, devices - 1, 2) for pair in ((i, i + 1), (i + 1, i))]
    even = (rank[0] & 1) == 0

    def chunk_shape(rows, unit):
        return shape_of((devices, -(-rows // unit) * unit, LANES), BF16)

    def table_shape(stride):
        return 8, brow * (-(-HALVES * bcol * stride // LANES) * LANES)

    def exchange(first, second):
        return lax.ppermute(first, AXES, even_pairs), lax.ppermute(second, AXES, odd_pairs)

    def rims(field, halo, weight):
        first, second = (piece.astype(F32) for piece in halo)
        left, right = jnp.where(even, second, first), jnp.where(even, first, second)
        last = count - RIM
        low = field[:, :RIM] + (weight * penalty) * left / mass[:, :RIM]
        high = field[:, last:] + (weight * penalty) * right / mass[:, last:]
        return jnp.where(even, high, low).astype(BF16), jnp.where(even, low, high).astype(BF16)

    def swap_all(chunks):
        return lax.all_to_all(chunks, AXES, split_axis=0, concat_axis=0, tiled=True)

    hbm = pl.BlockSpec(memory_space=pltpu.HBM)
    hot_shape = (elements // GROUP, width, GROUP * LANES)
    tile_shape = (bcol, HALVES, panel_dev, brow * panel_dev)

    def sweep(field, rhs, weight, halo=(), weight_before=None, keep=False):
        rows = parts * columns
        lanes = GROUP * LANES
        large = in_hbm(field, rhs) if keep else (field, rhs)
        given = (rank, *in_hbm(element_coef), *large, *in_vmem(mass, keys, matrix), *halo)
        return call(
            functools.partial(sweep_kernel, parts, weight, weight_before, keep),
            (field_shape, kept((columns, count), F32)) if keep else field_shape,
            5_000_000_000,
            in_specs=[smem, smem, vmem, hbm if keep else vmem] + [vmem] * (len(given) - 4),
            out_specs=(vmem, vmem) if keep else vmem,
            scratch_shapes=[pltpu.SemaphoreType.DMA] * keep
            + [pltpu.VMEM((columns, count), F32)] * bool(halo)
            + [
                pltpu.VMEM(hot_shape, BF16),
                pltpu.VMEM((rows, width), BF16),
                pltpu.VMEM((rows, width), BF16),
                pltpu.VMEM((2, rows, lanes), F32),
                pltpu.VMEM((2, GROUP * columns, 2 * LANES), BF16),
                pltpu.VMEM((2, GROUP * columns, 2 * LANES), F32),
                pltpu.VMEM((2, rows, lanes), BF16),
                pltpu.VMEM((2, rows, lanes), BF16),
                pltpu.VMEM((rows, width), F32),
            ],
        )(*given)

    def add_loads(chunks, field, halo, weight):
        return call(
            functools.partial(loads_kernel, parts, brow, weight, used),
            (field_shape, field_shape, rim_shape, rim_shape),
            500_000_000,
            in_specs=[smem] + [vmem] * 7,
            out_specs=(vmem,) * 4,
        )(rank, *in_vmem(load_nodes), chunks, *in_vmem(forcing_kept), field, *halo, *in_vmem(mass))

    parts_shape = shape_of((brow, columns, panel_dev), F32)
    sizes = (brow, bcol, panel_dev, slot_rows)
    tile_mib = -(-(2 * math.prod(tile_shape)) // MIB)

    def swap_parts(parts_out):
        return lax.all_to_all(parts_out, "brow", split_axis=0, concat_axis=0, tiled=True)

    (nodes, load_nodes, row_map, own_map, keys, matrix, mass, chunks, *rim) = call(
        functools.partial(setup_kernel, parts, brow, bcol, panel_dev, slot_rows),
        (
            kept(table_shape(slot_rows), jnp.int32),
            kept(table_shape(LOAD_ROWS), jnp.int32),
            kept((3, row_panels), jnp.int32),
            kept((3, panel_dev), jnp.int32),
            kept((elements, LANES), jnp.int32),
            kept((LANES, LANES), F32),
            kept((1, count), F32),
            chunk_shape(used + LOAD_ROWS + POINT_ROWS, 16),
            kept(rim_shape.shape, BF16),
            kept(rim_shape.shape, BF16),
        ),
        2_000_000_000,
        in_specs=[smem] + [vmem] * 7,
        out_specs=(vmem,) * 10,
    )(
        rank,
        *in_hbm(
            panel_map, field_start, potential_start, panel_points, element_nodes.T, element_matrix,
            node_mass.reshape(1, count),
        ),
    )
    halo = exchange(*rim)
    chunks = swap_all(chunks)
    field, forcing_kept = sweep(field_start, forcing, weights[0], keep=True)
    parts_out, tiles = call(
        functools.partial(tile_kernel, *sizes),
        (parts_shape, pltpu.HBM(tile_shape, BF16)),
        8_000_000_000,
        grid=(bcol,),
        limit=16 + tile_mib,
        in_specs=[smem, vmem, vmem],
        out_specs=(vmem, hbm),
        scratch_shapes=[
            pltpu.VMEM((16, brow * panel_dev), BF16),
            pltpu.VMEM((bcol, columns, panel_dev), BF16),
            pltpu.VMEM((bcol, columns, panel_dev), BF16),
            pltpu.VMEM((panel_dev, brow * panel_dev), F32),
            pltpu.VMEM(tile_shape, BF16),
            pltpu.VMEM((columns, brow * panel_dev), F32),
            pltpu.SemaphoreType.DMA((bcol,)),
        ],
    )(rank, *in_vmem(row_map), chunks)
    parts_in = swap_parts(parts_out)
    rhs, field, *rim = add_loads(chunks, field, halo, weights[0])
    halo = exchange(*rim)
    field = sweep(field, rhs, weights[1])
    halo_next = exchange(*rims(field, halo, weights[1]))
    field = sweep(field, rhs, weights[2], halo, weights[1])
    field, chunks, *rim = call(
        functools.partial(finish_kernel, parts, brow, bcol, panel_dev, slot_rows, weights[2]),
        (field_shape, chunk_shape(used + LOAD_ROWS, 8), rim_shape, rim_shape),
        1_000_000_000,
        in_specs=[smem] + [vmem] * 7,
        out_specs=(vmem,) * 4,
    )(rank, *in_vmem(own_map, nodes), field, *halo_next, *in_vmem(mass), parts_in)

    halo = exchange(*rim)
    chunks = swap_all(chunks)
    field = sweep(field, *in_vmem(forcing_kept), weights[0])
    parts_out = call(
        functools.partial(potential_kernel, *sizes),
        parts_shape,
        2_000_000_000,
        limit=16 + tile_mib,
        in_specs=[vmem, vmem, hbm],
        out_specs=vmem,
        scratch_shapes=[pltpu.VMEM(tile_shape, BF16), pltpu.SemaphoreType.DMA((bcol,))],
    )(*in_vmem(row_map), chunks, *in_hbm(tiles))
    parts_in = swap_parts(parts_out)
    rhs, field, *rim = add_loads(chunks, field, halo, weights[0])
    halo = exchange(*rim)
    field = sweep(field, rhs, weights[1])
    halo_next = exchange(*rims(field, halo, weights[1]))
    field = sweep(field, rhs, weights[2], halo, weights[1])
    return call(
        functools.partial(last_kernel, weights[2]),
        (field_shape, shape_of((columns, panel_dev), F32)),
        100_000_000,
        in_specs=[smem] + [vmem] * 5,
        out_specs=(vmem, vmem),
    )(rank, field, *halo_next, *in_vmem(mass), parts_in)


def solution(mesh):
    placed = (
        P(None, AXES),
        P(),
        P(None, AXES),
        P(AXES),
        P(),
        P(AXES),
        P(None, AXES),
        P(None, AXES),
        P(None, AXES),
    )
    return jax.shard_map(
        per_device,
        mesh=mesh,
        in_specs=placed,
        out_specs=(P(None, AXES), P(None, AXES)),
        check_vma=False,
    )
```

```python
import functools
import math

import jax
import jax.numpy as jnp
from jax import lax
from jax.experimental import pallas as pl
from jax.experimental.pallas import tpu as pltpu
from jax.sharding import PartitionSpec as P

RIM = 128
SWEEPS = 3
LANES = 128
LOAD_ROWS = 8
POINT_ROWS = 8
HALVES = 2
GROUP = 4
BLOCKS = 4

wave_number = 20.0
penalty = 0.5

AXES = ("brow", "bcol")
F32 = jnp.float32
BF16 = jnp.bfloat16

SIN_POLY = (3.14159264, -5.16771008, 2.55007752, -0.59829129, 0.07765766)

ROUNDER = 1.5 * 2.0**23
MIB = 1024 * 1024


def weight_of(sweep):
    return 1.0 / (1.25 + 0.75 * math.cos(math.pi * (2 * sweep + 1) / (2.0 * SWEEPS)))


def call(kernel, out_shape, cost, limit=28, **more):
    return pl.pallas_call(
        kernel,
        out_shape=out_shape,
        compiler_params=pltpu.CompilerParams(vmem_limit_bytes=limit * MIB),
        cost_estimate=pl.CostEstimate(flops=cost, bytes_accessed=1 << 20, transcendentals=0),
        **more,
    )


def shape_of(shape, dtype):
    return jax.ShapeDtypeStruct(shape, dtype)


def kept(shape, dtype):
    return pltpu.VMEM(shape, dtype)


def in_hbm(*arrays):
    return tuple(pltpu.with_memory_space_constraint(array, pltpu.HBM) for array in arrays)


def in_vmem(*arrays):
    return tuple(pltpu.with_memory_space_constraint(array, pltpu.VMEM) for array in arrays)


def dot(a, b):
    return jnp.dot(a, b, preferred_element_type=F32)


def dot_nt(a, b):
    return lax.dot_general(a, b, (((1,), (1,)), ((), ())), preferred_element_type=F32)


def split_two(value):
    high = value.astype(BF16)
    return high, (value - high.astype(F32)).astype(BF16)


def low_part(value, size):
    return value & (size - 1) if size & (size - 1) == 0 else value % size


def high_part(value, size):
    return value >> (size.bit_length() - 1) if size & (size - 1) == 0 else value // size


def stack_parts(value, parts):
    width = value.shape[1] // parts
    return jnp.concatenate([value[:, i * width : (i + 1) * width] for i in range(parts)], axis=0)


def one_hot_rows(key, rows):
    seen = lax.broadcasted_iota(jnp.int16, (rows, key.shape[1]), 0)
    return jnp.where(seen == key.astype(jnp.int16), BF16(1), BF16(0))


def pick_part(stacked, part, parts):
    rows = stacked.shape[0] // parts
    picked = stacked[(parts - 1) * rows :]
    for i in reversed(range(parts - 1)):
        picked = jnp.where(part == i, stacked[i * rows : (i + 1) * rows], picked)
    return picked


def gather_nodes(field, nodes, parts):
    width = field.shape[1] // parts
    hot = one_hot_rows(jnp.where(nodes < 0, -1, low_part(nodes, width)), width)
    found = dot(stack_parts(field.astype(BF16), parts), hot)
    return pick_part(found, high_part(nodes, width), parts)


def scatter_nodes(values, nodes, parts, count):
    width = count // parts
    hot = one_hot_rows(jnp.where(nodes < 0, -1, low_part(nodes, width)), width)
    masked = jnp.concatenate(
        [jnp.where(high_part(nodes, width) == i, values, 0.0) for i in range(parts)], axis=0
    ).astype(BF16)
    added = dot_nt(masked, hot)
    rows = values.shape[0]
    return jnp.concatenate([added[i * rows : (i + 1) * rows] for i in range(parts)], axis=1)


def halves_of(slot, rows):
    half = jnp.where(slot >= rows, 1, 0)
    return half, slot - half * rows


def trace_rows(field, nodes, parts, groups, used):
    turned = jnp.transpose(gather_nodes(field, nodes, parts))
    pieces = []
    for group in range(groups):
        base = group * HALVES * used
        pieces.append(
            jnp.concatenate([turned[base : base + used], turned[base + used : base + 2 * used]], axis=1)
        )
    return pieces


def own_panels(map_ref, rank, panel_dev):
    first = rank * panel_dev
    base = (first >> 7) << 7
    window = -(-panel_dev // LANES) * LANES
    near = map_ref[:, pl.ds(pl.multiple_of(base, LANES), window)]
    return jnp.where(first == base, near[:, :panel_dev], near[:, window - panel_dev :])


def load_rows(potential, own_map, devices, slot_rows):
    owner, slot = own_map[0:1], own_map[1:2]
    half, low = halves_of(slot, slot_rows)
    rows = devices * LOAD_ROWS
    key = half * rows + owner * LOAD_ROWS + low
    found = dot_nt(one_hot_rows(key, HALVES * rows), potential.astype(BF16))
    return jnp.concatenate([found[:rows], found[rows:]], axis=1).reshape(devices, LOAD_ROWS, LANES)


def node_tables(map_ref, rank, brow, bcol, panel_dev, slot_rows):
    row_panels = bcol * panel_dev
    trace_slots, load_slots = table_lanes(brow, bcol, slot_rows)
    lane = lax.broadcasted_iota(jnp.int32, (1, row_panels), 1).astype(F32)
    block = jnp.floor((lane + 0.5) * (1.0 / panel_dev)).astype(jnp.int32)
    row_id = lax.broadcasted_iota(jnp.int32, (8, row_panels), 0)
    traces = None
    loads = []
    for r in range(brow):
        span = slice(r * row_panels, (r + 1) * row_panels)
        owner, slot, node = map_ref[0:1, span], map_ref[1:2, span], map_ref[2:3, span]
        half, low = halves_of(slot, slot_rows)
        own = owner == rank
        values = jnp.where(
            row_id == 0, high_part(node, 256), jnp.where(row_id == 1, low_part(node, 256), 1)
        ).astype(F32).astype(BF16)
        key = ((block * HALVES + half) * brow + r) * slot_rows + low
        found = dot_nt(values, one_hot_rows(jnp.where(own, key, -1), trace_slots))
        traces = found if traces is None else traces + found
        key = (half * bcol + block) * LOAD_ROWS + low
        loads.append(dot_nt(values, one_hot_rows(jnp.where(own, key, -1), load_slots // brow)))
    tables = []
    for found in (traces, jnp.concatenate(loads, axis=1)):
        table = jnp.where(found[2:3] > 0.5, found[0:1] * 256.0 + found[1:2], -1.0)
        tables.append(table.astype(jnp.int32))
    return tables


def table_lanes(brow, bcol, slot_rows):
    trace_slots = -(-HALVES * brow * bcol * slot_rows // LANES) * LANES
    return trace_slots, brow * (-(-HALVES * bcol * LOAD_ROWS // LANES) * LANES)


def point_rows(points):
    row_id = lax.broadcasted_iota(jnp.int32, (POINT_ROWS, LANES), 0)
    each = POINT_ROWS // 3
    width = points.shape[1]
    value = jnp.zeros((POINT_ROWS, LANES), F32)
    for axis in range(3):
        for part in range(-(-width // LANES)):
            piece = points[axis : axis + 1, part * LANES : (part + 1) * LANES]
            short = LANES - piece.shape[1]
            if short:
                piece = jnp.concatenate([piece, jnp.zeros((1, short), F32)], axis=1)
            value = jnp.where(row_id == axis * each + part, piece, value)
    return value


def write_chunks(chunk_ref, pieces, loads, points=None):
    used = pieces[0].shape[0]
    for device in range(chunk_ref.shape[0]):
        rows = [pieces[device % len(pieces)], loads[device]] + ([] if points is None else [points])
        left = chunk_ref.shape[1] - sum(piece.shape[0] for piece in rows)
        if left:
            rows.append(jnp.zeros((left, LANES), F32))
        chunk_ref[device] = jnp.concatenate(rows, axis=0).astype(BF16)


def write_rims(field, even, first_ref, second_ref):
    low = field[:, :RIM]
    high = field[:, field.shape[1] - RIM :]
    first_ref[...] = jnp.where(even, high, low).astype(BF16)
    second_ref[...] = jnp.where(even, low, high).astype(BF16)


def setup_kernel(
    parts, brow, bcol, panel_dev, slot_rows, rank_ref, map_ref, field_ref, potential_ref, points_ref,
    element_nodes_ref, element_matrix_ref, node_mass_ref,
    nodes_ref, load_nodes_ref, source_map_ref, own_map_ref, keys_ref, matrix_ref, mass_ref,
    chunk_ref, rim_first_ref, rim_second_ref,
):
    rank = rank_ref[0]
    source_map_ref[...] = jnp.concatenate(
        [
            own_panels(map_ref, r * bcol + low_part(rank, bcol), panel_dev)
            for r in range(brow)
        ],
        axis=1,
    )
    own_map = own_panels(map_ref, rank, panel_dev)
    own_map_ref[...] = own_map
    keys_ref[...] = jnp.zeros_like(keys_ref)
    keys_ref[:, : element_nodes_ref.shape[1]] = element_nodes_ref[...]
    matrix_ref[...] = jnp.zeros_like(matrix_ref)
    matrix_ref[: element_matrix_ref.shape[0], : element_matrix_ref.shape[1]] = element_matrix_ref[...]
    mass_ref[...] = node_mass_ref[...]
    nodes, load_nodes = node_tables(map_ref, rank, brow, bcol, panel_dev, slot_rows)
    nodes_ref[...] = jnp.broadcast_to(nodes, nodes_ref.shape)
    load_nodes_ref[...] = jnp.broadcast_to(load_nodes, load_nodes_ref.shape)
    field = field_ref[...]
    write_rims(field, low_part(rank, 2) == 0, rim_first_ref, rim_second_ref)
    loads = load_rows(potential_ref[...], own_map, brow * bcol, slot_rows)
    pieces = trace_rows(field, nodes, parts, bcol, brow * slot_rows)
    write_chunks(chunk_ref, pieces, loads, point_rows(points_ref[...].astype(F32)))


def rim_correction(value, even, first_ref, second_ref, mass, weight):
    step = weight * penalty
    first, second = first_ref[...].astype(F32), second_ref[...].astype(F32)
    left, right = jnp.where(even, second, first), jnp.where(even, first, second)
    last = value.shape[1] - RIM
    low = value[:, :RIM] + step * left / mass[:, :RIM]
    high = value[:, last:] + step * right / mass[:, last:]
    return jnp.concatenate([low, value[:, RIM:last], high], axis=1)


def received_loads(chunk_ref, used, brow, columns):
    received = chunk_ref[...].astype(F32)[:, used : used + LOAD_ROWS]
    received = received.reshape(received.shape[0] * LOAD_ROWS, LANES)
    span = received.shape[0] // brow
    rows = []
    for r in range(brow):
        piece = received[r * span : (r + 1) * span]
        rows += [piece[:, :columns], piece[:, columns : HALVES * columns]]
    return jnp.transpose(jnp.concatenate(rows, axis=0))


def sweep_kernel(
    parts, weight, weight_before, keep, rank_ref, coef_ref, field_ref, rhs_ref, mass_ref, keys_ref,
    matrix_ref, *more_refs,
):
    if keep:
        out_ref, kept_ref, sem, *scratch = more_refs
        copy = pltpu.make_async_copy(rhs_ref, kept_ref, sem)
        copy.start()
        rhs_ref = kept_ref
    elif weight_before is None:
        out_ref, *scratch = more_refs
    else:
        first_ref, second_ref, out_ref, field_scr, *scratch = more_refs
    hot_ref, high_ref, low_ref, found_ref, local_ref, product_ref, yhigh_ref, ylow_ref, sum_ref = scratch
    groups = hot_ref.shape[0]
    columns, count = field_ref.shape
    width = count // parts
    mass = mass_ref[...]
    if weight_before is None:
        field = field_ref[...]
        field_now = field_ref
    else:
        even = low_part(rank_ref[0], 2) == 0
        field = rim_correction(field_ref[...], even, first_ref, second_ref, mass, weight_before)
        field_scr[...] = field
        field_now = field_scr
    high, low = split_two(field)
    for h in range(parts):
        high_ref[h * columns : (h + 1) * columns] = high[:, h * width : (h + 1) * width]
        low_ref[h * columns : (h + 1) * columns] = low[:, h * width : (h + 1) * width]
    mat_high, mat_low = split_two(matrix_ref[...])
    matrix = jnp.concatenate(
        [
            jnp.concatenate([mat_high, mat_low], axis=1),
            jnp.concatenate([mat_high, jnp.zeros_like(mat_low)], axis=1),
        ],
        axis=0,
    )

    def build(group):
        for e in range(GROUP):
            key = keys_ref[group * GROUP + e : group * GROUP + e + 1, :]
            hot_ref[group, :, e * LANES : (e + 1) * LANES] = one_hot_rows(low_part(key, width), width)

    def gather(group):
        hot = hot_ref[group]
        found_ref[group % 2] = dot(high_ref[...], hot) + dot(low_ref[...], hot)

    def pick(group):
        slot = group % 2
        for e in range(GROUP):
            element = group * GROUP + e
            key = keys_ref[element : element + 1, :]
            got = pick_part(found_ref[slot, :, e * LANES : (e + 1) * LANES], high_part(key, width), parts)
            got_high, got_low = split_two(got)
            local_ref[slot, e * columns : (e + 1) * columns, :LANES] = got_high
            local_ref[slot, e * columns : (e + 1) * columns, LANES:] = got_low


    def multiply(group):
        product_ref[group % 2] = dot(local_ref[group % 2], matrix)

    def scale(group):
        slot = group % 2
        for e in range(GROUP):
            element = group * GROUP + e
            part = high_part(keys_ref[element : element + 1, :], width)
            rows = product_ref[slot, e * columns : (e + 1) * columns]
            value = (rows[:, :LANES] + rows[:, LANES:]) * coef_ref[element]
            value_high, value_low = split_two(value)
            span = slice(e * LANES, (e + 1) * LANES)
            for h in range(parts):
                mask = jnp.where(part == h, 1.0, 0.0).astype(BF16)
                yhigh_ref[slot, h * columns : (h + 1) * columns, span] = value_high * mask
                ylow_ref[slot, h * columns : (h + 1) * columns, span] = value_low * mask

    def scatter(group):
        hot = hot_ref[group]
        added = dot_nt(yhigh_ref[group % 2], hot) + dot_nt(ylow_ref[group % 2], hot)
        sum_ref[...] = added if group == 0 else sum_ref[...] + added

    build(0)
    gather(0)
    build(1)
    for group in range(groups):
        pick(group)
        if group + 1 < groups:
            gather(group + 1)
        if group + 2 < groups:
            build(group + 2)
        multiply(group)
        if group:
            scatter(group - 1)
        scale(group)
    scatter(groups - 1)
    if keep:
        copy.wait()
    for h in range(parts):
        span = slice(h * width, (h + 1) * width)
        stiff = sum_ref[h * columns : (h + 1) * columns]
        out_ref[:, span] = (1.0 - weight) * field_now[:, span] + weight * (
            rhs_ref[:, span] - stiff
        ) / mass[:, span]


def loads_kernel(
    parts, brow, weight, used, rank_ref, nodes_ref, chunk_ref, forcing_ref, field_ref, first_ref,
    second_ref, mass_ref, rhs_ref, out_ref, rim_first_ref, rim_second_ref,
):
    columns, count = field_ref.shape
    loads = received_loads(chunk_ref, used, brow, columns)
    added = scatter_nodes(loads, nodes_ref[0:1, :], parts, count)
    rhs_ref[...] = forcing_ref[...] + added
    mass = mass_ref[...]
    even = low_part(rank_ref[0], 2) == 0
    field = field_ref[...] + weight * added / mass
    field = rim_correction(field, even, first_ref, second_ref, mass, weight)
    out_ref[...] = field
    write_rims(field, even, rim_first_ref, rim_second_ref)


def total(parts_ref):
    value = parts_ref[0]
    for r in range(1, parts_ref.shape[0]):
        value = value + parts_ref[r]
    return value


def finish_kernel(
    parts, brow, bcol, panel_dev, slot_rows, weight, rank_ref, own_map_ref, nodes_ref, field_ref,
    first_ref, second_ref, mass_ref, parts_ref, out_ref, chunk_ref, rim_first_ref, rim_second_ref,
):
    rank = rank_ref[0]
    even = low_part(rank, 2) == 0
    field = rim_correction(field_ref[...], even, first_ref, second_ref, mass_ref[...], weight)
    out_ref[...] = field
    write_rims(field, even, rim_first_ref, rim_second_ref)
    loads = load_rows(total(parts_ref), own_map_ref[...], brow * bcol, slot_rows)
    pieces = trace_rows(field, nodes_ref[0:1, :], parts, bcol, brow * slot_rows)
    write_chunks(chunk_ref, pieces, loads)


def last_kernel(
    weight, rank_ref, field_ref, first_ref, second_ref, mass_ref, parts_ref, out_ref, potential_ref
):
    even = low_part(rank_ref[0], 2) == 0
    out_ref[...] = rim_correction(field_ref[...], even, first_ref, second_ref, mass_ref[...], weight)
    potential_ref[...] = total(parts_ref)


def density_groups(map_ref, chunk_ref, brow, bcol, panel_dev, slot_rows):
    devices = brow * bcol
    columns = LANES // HALVES
    rows = BLOCKS * slot_rows
    panels = BLOCKS * panel_dev
    lane = lax.broadcasted_iota(jnp.int32, (1, panels), 1).astype(F32)
    block = jnp.floor((lane + 0.5) * (1.0 / panel_dev)).astype(jnp.int32)
    traces = chunk_ref[...].astype(F32)
    for group in range(brow // BLOCKS):
        span = slice(group * panels, (group + 1) * panels)
        owner, slot = map_ref[0:1, span], map_ref[1:2, span]
        half, low = halves_of(slot, slot_rows)
        key = owner * rows + block * slot_rows + low
        near = traces[:, group * rows : (group + 1) * rows].reshape(devices * rows, LANES)
        found = dot(jnp.transpose(near).astype(BF16), one_hot_rows(key, devices * rows))
        density = jnp.where(half == 0, found[:columns], found[columns:])
        turned = jnp.concatenate([-density[columns // 2 :], density[: columns // 2]], axis=0)
        yield density.astype(BF16), turned.astype(BF16)


def write_parts(out_ref, total, panel_dev):
    for r in range(out_ref.shape[0]):
        out_ref[r] = total[:, r * panel_dev : (r + 1) * panel_dev]


def split_three(value):
    high = value.astype(BF16).astype(F32)
    middle = (value - high).astype(BF16).astype(F32)
    return [high, middle, value - high - middle]


def squares(axes):
    return sum(row * row for row in axes[1:]) + axes[0] * axes[0]


def rows_of(rows, dtype=BF16):
    row_id = lax.broadcasted_iota(jnp.int32, (16, rows[0].shape[1]), 0)
    value = jnp.zeros(row_id.shape, F32)
    for index, row in enumerate(rows):
        value = jnp.where(row_id == index, row, value)
    return value.astype(dtype)


def tile_kernel(
    brow, bcol, panel_dev, slot_rows, rank_ref, map_ref, chunk_ref, out_ref, tile_ref,
    target_ref, density_ref, turned_ref, distance_ref, built_ref, sum_ref, sems,
):
    count_all = brow * bcol * panel_dev
    soften = 0.5 * float(count_all) ** (-1.0 / 3.0)
    each = POINT_ROWS // 3
    row_index, col_index = high_part(rank_ref[0], bcol), low_part(rank_ref[0], bcol)
    start = brow * slot_rows + LOAD_ROWS
    block = pl.program_id(0)

    def points_of(device):
        return chunk_ref[device].astype(F32)[start : start + POINT_ROWS]

    def copy_of(index):
        return pltpu.make_async_copy(built_ref.at[index], tile_ref.at[index], sems.at[index])

    @pl.when(block == 0)
    def prepare():
        near = [points_of(row_index * bcol + c) for c in range(bcol)]
        axes = []
        for axis in range(3):
            rows = []
            for piece in near:
                for part in range(each):
                    wide = min(LANES, panel_dev - part * LANES)
                    rows.append(piece[axis * each + part : axis * each + part + 1, :wide])
            axes.append(jnp.concatenate(rows, axis=1))
        norms = split_three(squares(axes) + soften * soften)
        target_ref[...] = rows_of([-2.0 * row for row in axes] + [jnp.ones_like(axes[0])] * 3 + norms)
        sum_ref[...] = jnp.zeros_like(sum_ref)
        groups = density_groups(map_ref, chunk_ref, brow, bcol, panel_dev, slot_rows)
        for group, (density, turned) in enumerate(groups):
            for k in range(BLOCKS):
                span = slice(k * panel_dev, (k + 1) * panel_dev)
                density_ref[group * BLOCKS + k] = density[:, span]
                turned_ref[group * BLOCKS + k] = turned[:, span]

    piece = points_of(block * bcol + col_index)
    axes = [
        jnp.concatenate([piece[axis * each + part : axis * each + part + 1] for part in range(each)], axis=1)
        for axis in range(3)
    ]
    norms = split_three(squares(axes))
    source = jnp.transpose(rows_of(axes + norms + [jnp.ones_like(axes[0])] * 3, F32)).astype(BF16)
    distance_ref[...] = dot(source[:panel_dev], target_ref[...])
    step = 16
    for top in range(0, panel_dev, step):
        squared = distance_ref[top : top + step]
        inverse = lax.rsqrt(squared)
        turns = (squared * inverse) * (wave_number / (2.0 * math.pi))
        turns = turns - ((turns + ROUNDER) - ROUNDER)
        z = turns * turns
        sine = jnp.full_like(z, SIN_POLY[-1])
        for factor in SIN_POLY[-2::-1]:
            sine = sine * z + factor
        sine = sine * turns
        rest = 1.0 - sine * sine
        safe = jnp.maximum(rest, 1e-12)
        cosine = safe * lax.rsqrt(safe)
        double = inverse * (2.0 / math.sqrt(float(count_all)))
        built_ref[block, 0, top : top + step] = ((rest - 0.5) * double).astype(BF16)
        built_ref[block, 1, top : top + step] = (sine * cosine * double).astype(BF16)
    copy_of(block).start()
    sum_ref[...] += dot(density_ref[block], built_ref[block, 0]) + dot(
        turned_ref[block], built_ref[block, 1]
    )

    @pl.when(block == brow - 1)
    def end():
        write_parts(out_ref, sum_ref[...], panel_dev)
        for index in range(brow):
            copy_of(index).wait()


def potential_kernel(
    brow, bcol, panel_dev, slot_rows, map_ref, chunk_ref, tile_ref, out_ref, held_ref, sems,
):
    copies = [
        pltpu.make_async_copy(tile_ref.at[block], held_ref.at[block], sems.at[block])
        for block in range(brow)
    ]
    for copy in copies:
        copy.start()
    whole = None
    groups = density_groups(map_ref, chunk_ref, brow, bcol, panel_dev, slot_rows)
    for group, (density, turned) in enumerate(groups):
        for k in range(BLOCKS):
            block = group * BLOCKS + k
            copies[block].wait()
            span = slice(k * panel_dev, (k + 1) * panel_dev)
            part = dot(density[:, span], held_ref[block, 0]) + dot(turned[:, span], held_ref[block, 1])
            whole = part if whole is None else whole + part
    write_parts(out_ref, whole, panel_dev)


def per_device(
    panel_points,
    panel_map,
    element_nodes,
    element_coef,
    element_matrix,
    node_mass,
    forcing,
    field_start,
    potential_start,
):
    columns, panel_dev = potential_start.shape
    count = field_start.shape[1]
    brow, bcol = lax.axis_size("brow"), lax.axis_size("bcol")
    devices = brow * bcol
    capacity = max(2, 2 * panel_dev // devices)
    slot_rows = -(-capacity // HALVES)
    used = brow * slot_rows
    assert slot_rows <= LOAD_ROWS and columns * HALVES == LANES and brow % BLOCKS == 0
    parts = 256 // columns
    width = count // parts
    row_panels = bcol * panel_dev
    row_index, col_index = lax.axis_index("brow"), lax.axis_index("bcol")
    rank = (row_index * bcol + col_index).reshape(1)
    nodes_each, elements = element_nodes.shape
    assert elements % GROUP == 0
    smem = pl.BlockSpec(memory_space=pltpu.SMEM)
    vmem = pl.BlockSpec(memory_space=pltpu.VMEM)
    rim_shape = shape_of((columns, RIM), BF16)
    field_shape = shape_of((columns, count), F32)
    weights = [weight_of(sweep_index) for sweep_index in range(SWEEPS)]
    even_pairs = [(i, i ^ 1) for i in range(devices)]
    odd_pairs = [pair for i in range(1, devices - 1, 2) for pair in ((i, i + 1), (i + 1, i))]
    even = (rank[0] & 1) == 0

    def chunk_shape(rows, unit):
        return shape_of((devices, -(-rows // unit) * unit, LANES), BF16)

    def exchange(first, second):
        return lax.ppermute(first, AXES, even_pairs), lax.ppermute(second, AXES, odd_pairs)

    def rims(field, halo, weight):
        first, second = (piece.astype(F32) for piece in halo)
        left, right = jnp.where(even, second, first), jnp.where(even, first, second)
        last = count - RIM
        low = field[:, :RIM] + (weight * penalty) * left / mass[:, :RIM]
        high = field[:, last:] + (weight * penalty) * right / mass[:, last:]
        return jnp.where(even, high, low).astype(BF16), jnp.where(even, low, high).astype(BF16)

    def swap_all(chunks):
        return lax.all_to_all(chunks, AXES, split_axis=0, concat_axis=0, tiled=True)

    hbm = pl.BlockSpec(memory_space=pltpu.HBM)
    hot_shape = (elements // GROUP, width, GROUP * LANES)
    tile_shape = (brow, HALVES, panel_dev, bcol * panel_dev)

    def sweep(field, rhs, weight, halo=(), weight_before=None, keep=False):
        rows = parts * columns
        lanes = GROUP * LANES
        large = in_hbm(field, rhs) if keep else (field, rhs)
        given = (rank, *in_hbm(element_coef), *large, *in_vmem(mass, keys, matrix), *halo)
        return call(
            functools.partial(sweep_kernel, parts, weight, weight_before, keep),
            (field_shape, kept((columns, count), F32)) if keep else field_shape,
            5_000_000_000,
            in_specs=[smem, smem, vmem, hbm if keep else vmem] + [vmem] * (len(given) - 4),
            out_specs=(vmem, vmem) if keep else vmem,
            scratch_shapes=[pltpu.SemaphoreType.DMA] * keep
            + [pltpu.VMEM((columns, count), F32)] * bool(halo)
            + [
                pltpu.VMEM(hot_shape, BF16),
                pltpu.VMEM((rows, width), BF16),
                pltpu.VMEM((rows, width), BF16),
                pltpu.VMEM((2, rows, lanes), F32),
                pltpu.VMEM((2, GROUP * columns, 2 * LANES), BF16),
                pltpu.VMEM((2, GROUP * columns, 2 * LANES), F32),
                pltpu.VMEM((2, rows, lanes), BF16),
                pltpu.VMEM((2, rows, lanes), BF16),
                pltpu.VMEM((rows, width), F32),
            ],
        )(*given)

    def add_loads(chunks, field, halo, weight):
        return call(
            functools.partial(loads_kernel, parts, brow, weight, used),
            (field_shape, field_shape, rim_shape, rim_shape),
            500_000_000,
            in_specs=[smem] + [vmem] * 7,
            out_specs=(vmem,) * 4,
        )(rank, *in_vmem(load_nodes), chunks, *in_vmem(forcing_kept), field, *halo, *in_vmem(mass))

    parts_shape = shape_of((bcol, columns, panel_dev), F32)
    sizes = (brow, bcol, panel_dev, slot_rows)
    tile_mib = -(-(2 * math.prod(tile_shape)) // MIB)

    def swap_parts(parts_out):
        return lax.all_to_all(parts_out, "bcol", split_axis=0, concat_axis=0, tiled=True)

    trace_slots, load_slots = table_lanes(brow, bcol, slot_rows)
    (nodes, load_nodes, source_map, own_map, keys, matrix, mass, chunks, *rim) = call(
        functools.partial(setup_kernel, parts, brow, bcol, panel_dev, slot_rows),
        (
            kept((8, trace_slots), jnp.int32),
            kept((8, load_slots), jnp.int32),
            kept((3, brow * panel_dev), jnp.int32),
            kept((3, panel_dev), jnp.int32),
            kept((elements, LANES), jnp.int32),
            kept((LANES, LANES), F32),
            kept((1, count), F32),
            chunk_shape(used + LOAD_ROWS + POINT_ROWS, 8),
            kept(rim_shape.shape, BF16),
            kept(rim_shape.shape, BF16),
        ),
        2_000_000_000,
        in_specs=[smem] + [vmem] * 7,
        out_specs=(vmem,) * 10,
    )(
        rank,
        *in_hbm(
            panel_map, field_start, potential_start, panel_points, element_nodes.T, element_matrix,
            node_mass.reshape(1, count),
        ),
    )
    halo = exchange(*rim)
    chunks = swap_all(chunks)
    field, forcing_kept = sweep(field_start, forcing, weights[0], keep=True)
    parts_out, tiles = call(
        functools.partial(tile_kernel, *sizes),
        (parts_shape, pltpu.HBM(tile_shape, BF16)),
        8_000_000_000,
        grid=(brow,),
        limit=16 + tile_mib,
        in_specs=[smem, vmem, vmem],
        out_specs=(vmem, hbm),
        scratch_shapes=[
            pltpu.VMEM((16, bcol * panel_dev), BF16),
            pltpu.VMEM((brow, columns, panel_dev), BF16),
            pltpu.VMEM((brow, columns, panel_dev), BF16),
            pltpu.VMEM((panel_dev, bcol * panel_dev), F32),
            pltpu.VMEM(tile_shape, BF16),
            pltpu.VMEM((columns, bcol * panel_dev), F32),
            pltpu.SemaphoreType.DMA((brow,)),
        ],
    )(rank, *in_vmem(source_map), chunks)
    parts_in = swap_parts(parts_out)
    rhs, field, *rim = add_loads(chunks, field, halo, weights[0])
    halo = exchange(*rim)
    field = sweep(field, rhs, weights[1])
    halo_next = exchange(*rims(field, halo, weights[1]))
    field = sweep(field, rhs, weights[2], halo, weights[1])
    field, chunks, *rim = call(
        functools.partial(finish_kernel, parts, brow, bcol, panel_dev, slot_rows, weights[2]),
        (field_shape, chunk_shape(used + LOAD_ROWS, 8), rim_shape, rim_shape),
        1_000_000_000,
        in_specs=[smem] + [vmem] * 7,
        out_specs=(vmem,) * 4,
    )(rank, *in_vmem(own_map, nodes), field, *halo_next, *in_vmem(mass), parts_in)

    halo = exchange(*rim)
    chunks = swap_all(chunks)
    field = sweep(field, *in_vmem(forcing_kept), weights[0])
    parts_out = call(
        functools.partial(potential_kernel, *sizes),
        parts_shape,
        2_000_000_000,
        limit=16 + tile_mib,
        in_specs=[vmem, vmem, hbm],
        out_specs=vmem,
        scratch_shapes=[pltpu.VMEM(tile_shape, BF16), pltpu.SemaphoreType.DMA((brow,))],
    )(*in_vmem(source_map), chunks, *in_hbm(tiles))
    parts_in = swap_parts(parts_out)
    rhs, field, *rim = add_loads(chunks, field, halo, weights[0])
    halo = exchange(*rim)
    field = sweep(field, rhs, weights[1])
    halo_next = exchange(*rims(field, halo, weights[1]))
    field = sweep(field, rhs, weights[2], halo, weights[1])
    return call(
        functools.partial(last_kernel, weights[2]),
        (field_shape, shape_of((columns, panel_dev), F32)),
        100_000_000,
        in_specs=[smem] + [vmem] * 5,
        out_specs=(vmem, vmem),
    )(rank, field, *halo_next, *in_vmem(mass), parts_in)


def solution(mesh):
    placed = (
        P(None, AXES),
        P(),
        P(None, AXES),
        P(AXES),
        P(),
        P(AXES),
        P(None, AXES),
        P(None, AXES),
        P(None, AXES),
    )
    return jax.shard_map(
        per_device,
        mesh=mesh,
        in_specs=placed,
        out_specs=(P(None, AXES), P(None, AXES)),
        check_vma=False,
    )
```

```python
import functools
import math

import jax
import jax.numpy as jnp
from jax import lax
from jax.experimental import pallas as pl
from jax.experimental.pallas import tpu as pltpu
from jax.sharding import PartitionSpec as P

RIM = 128
SWEEPS = 3
LANES = 128
LOAD_ROWS = 8
POINT_ROWS = 8
HALVES = 2
GROUP = 2
BLOCKS = 4

wave_number = 20.0
penalty = 0.5

AXES = ("brow", "bcol")
F32 = jnp.float32
BF16 = jnp.bfloat16

SIN_POLY = (3.14159264, -5.16771008, 2.55007752, -0.59829129, 0.07765766)

ROUNDER = 1.5 * 2.0**23
MIB = 1024 * 1024


def weight_of(sweep):
    return 1.0 / (1.25 + 0.75 * math.cos(math.pi * (2 * sweep + 1) / (2.0 * SWEEPS)))


def call(kernel, out_shape, cost, limit=28, **more):
    return pl.pallas_call(
        kernel,
        out_shape=out_shape,
        compiler_params=pltpu.CompilerParams(vmem_limit_bytes=limit * MIB),
        cost_estimate=pl.CostEstimate(flops=cost, bytes_accessed=1 << 20, transcendentals=0),
        **more,
    )


def shape_of(shape, dtype):
    return jax.ShapeDtypeStruct(shape, dtype)


def kept(shape, dtype):
    return pltpu.VMEM(shape, dtype)


def in_hbm(*arrays):
    return tuple(pltpu.with_memory_space_constraint(array, pltpu.HBM) for array in arrays)


def in_vmem(*arrays):
    return tuple(pltpu.with_memory_space_constraint(array, pltpu.VMEM) for array in arrays)


def dot(a, b):
    return jnp.dot(a, b, preferred_element_type=F32)


def dot_nt(a, b):
    return lax.dot_general(a, b, (((1,), (1,)), ((), ())), preferred_element_type=F32)


def split_two(value):
    high = value.astype(BF16)
    return high, (value - high.astype(F32)).astype(BF16)


def low_part(value, size):
    return value & (size - 1) if size & (size - 1) == 0 else value % size


def high_part(value, size):
    return value >> (size.bit_length() - 1) if size & (size - 1) == 0 else value // size


def stack_parts(value, parts):
    width = value.shape[1] // parts
    return jnp.concatenate([value[:, i * width : (i + 1) * width] for i in range(parts)], axis=0)


def one_hot_rows(key, rows):
    seen = lax.broadcasted_iota(jnp.int16, (rows, key.shape[1]), 0)
    return jnp.where(seen == key.astype(jnp.int16), BF16(1), BF16(0))


def pick_part(stacked, part, parts):
    rows = stacked.shape[0] // parts
    picked = stacked[(parts - 1) * rows :]
    for i in reversed(range(parts - 1)):
        picked = jnp.where(part == i, stacked[i * rows : (i + 1) * rows], picked)
    return picked


def gather_nodes(field, nodes, parts):
    width = field.shape[1] // parts
    hot = one_hot_rows(jnp.where(nodes < 0, -1, low_part(nodes, width)), width)
    found = dot(stack_parts(field.astype(BF16), parts), hot)
    return pick_part(found, high_part(nodes, width), parts)


def scatter_nodes(values, nodes, parts, count):
    width = count // parts
    hot = one_hot_rows(jnp.where(nodes < 0, -1, low_part(nodes, width)), width)
    masked = jnp.concatenate(
        [jnp.where(high_part(nodes, width) == i, values, 0.0) for i in range(parts)], axis=0
    ).astype(BF16)
    added = dot_nt(masked, hot)
    rows = values.shape[0]
    return jnp.concatenate([added[i * rows : (i + 1) * rows] for i in range(parts)], axis=1)


def halves_of(slot, rows):
    half = jnp.where(slot >= rows, 1, 0)
    return half, slot - half * rows


def trace_rows(field, nodes, parts, groups, used):
    turned = jnp.transpose(gather_nodes(field, nodes, parts))
    pieces = []
    for group in range(groups):
        base = group * HALVES * used
        pieces.append(
            jnp.concatenate([turned[base : base + used], turned[base + used : base + 2 * used]], axis=1)
        )
    return pieces


def own_panels(map_ref, rank, panel_dev):
    first = rank * panel_dev
    base = (first >> 7) << 7
    window = -(-panel_dev // LANES) * LANES
    near = map_ref[:, pl.ds(pl.multiple_of(base, LANES), window)]
    return jnp.where(first == base, near[:, :panel_dev], near[:, window - panel_dev :])


def load_rows(potential, own_map, devices, slot_rows):
    owner, slot = own_map[0:1], own_map[1:2]
    half, low = halves_of(slot, slot_rows)
    rows = devices * LOAD_ROWS
    key = half * rows + owner * LOAD_ROWS + low
    found = dot_nt(one_hot_rows(key, HALVES * rows), potential.astype(BF16))
    return jnp.concatenate([found[:rows], found[rows:]], axis=1).reshape(devices, LOAD_ROWS, LANES)


def node_tables(map_ref, rank, brow, bcol, panel_dev, slot_rows):
    row_panels = bcol * panel_dev
    trace_slots, load_slots = table_lanes(brow, bcol, slot_rows)
    lane = lax.broadcasted_iota(jnp.int32, (1, row_panels), 1).astype(F32)
    block = jnp.floor((lane + 0.5) * (1.0 / panel_dev)).astype(jnp.int32)
    row_id = lax.broadcasted_iota(jnp.int32, (8, row_panels), 0)
    loads = []
    for r in range(brow):
        span = slice(r * row_panels, (r + 1) * row_panels)
        owner, slot, node = map_ref[0:1, span], map_ref[1:2, span], map_ref[2:3, span]
        half, low = halves_of(slot, slot_rows)
        values = jnp.where(
            row_id == 0, high_part(node, 256), jnp.where(row_id == 1, low_part(node, 256), 1)
        ).astype(F32).astype(BF16)
        key = jnp.where(owner == rank, (half * bcol + block) * LOAD_ROWS + low, -1)
        loads.append(dot_nt(values, one_hot_rows(key, load_slots // brow)))
    loads = jnp.concatenate(loads, axis=1)
    place = lax.broadcasted_iota(jnp.int32, (1, load_slots), 1)
    row, inside = place // (load_slots // brow), place % (load_slots // brow)
    half, inside = inside // (bcol * LOAD_ROWS), inside % (bcol * LOAD_ROWS)
    column, low = inside // LOAD_ROWS, inside % LOAD_ROWS
    key = ((column * HALVES + half) * brow + row) * slot_rows + low
    key = jnp.where((low < slot_rows) & (half < HALVES), key, -1)
    traces = dot_nt(loads.astype(BF16), one_hot_rows(key, trace_slots))
    tables = []
    for found in (traces, loads):
        table = jnp.where(found[2:3] > 0.5, found[0:1] * 256.0 + found[1:2], -1.0)
        tables.append(table.astype(jnp.int32))
    return tables


def table_lanes(brow, bcol, slot_rows):
    trace_slots = -(-HALVES * brow * bcol * slot_rows // LANES) * LANES
    return trace_slots, brow * (-(-HALVES * bcol * LOAD_ROWS // LANES) * LANES)


def point_rows(points):
    row_id = lax.broadcasted_iota(jnp.int32, (POINT_ROWS, LANES), 0)
    each = POINT_ROWS // 3
    width = points.shape[1]
    value = jnp.zeros((POINT_ROWS, LANES), F32)
    for axis in range(3):
        for part in range(-(-width // LANES)):
            piece = points[axis : axis + 1, part * LANES : (part + 1) * LANES]
            short = LANES - piece.shape[1]
            if short:
                piece = jnp.concatenate([piece, jnp.zeros((1, short), F32)], axis=1)
            value = jnp.where(row_id == axis * each + part, piece, value)
    return value


def write_chunks(chunk_ref, pieces, loads, points=None):
    used = pieces[0].shape[0]
    for device in range(chunk_ref.shape[0]):
        rows = [pieces[device % len(pieces)], loads[device]] + ([] if points is None else [points])
        left = chunk_ref.shape[1] - sum(piece.shape[0] for piece in rows)
        if left:
            rows.append(jnp.zeros((left, LANES), F32))
        chunk_ref[device] = jnp.concatenate(rows, axis=0).astype(BF16)


def write_rims(field, even, first_ref, second_ref):
    low = field[:, :RIM]
    high = field[:, field.shape[1] - RIM :]
    first_ref[...] = jnp.where(even, high, low).astype(BF16)
    second_ref[...] = jnp.where(even, low, high).astype(BF16)


def setup_kernel(
    parts, brow, bcol, panel_dev, slot_rows, rank_ref, map_ref, field_ref, potential_ref, points_ref,
    element_nodes_ref, element_matrix_ref, node_mass_ref,
    nodes_ref, load_nodes_ref, source_map_ref, own_map_ref, keys_ref, matrix_ref, mass_ref,
    chunk_ref, rim_first_ref, rim_second_ref,
):
    rank = rank_ref[0]
    source_map_ref[...] = jnp.concatenate(
        [
            own_panels(map_ref, r * bcol + low_part(rank, bcol), panel_dev)
            for r in range(brow)
        ],
        axis=1,
    )
    own_map = own_panels(map_ref, rank, panel_dev)
    own_map_ref[...] = own_map
    keys_ref[...] = jnp.zeros_like(keys_ref)
    keys_ref[:, : element_nodes_ref.shape[1]] = element_nodes_ref[...]
    matrix_ref[...] = jnp.zeros_like(matrix_ref)
    matrix_ref[: element_matrix_ref.shape[0], : element_matrix_ref.shape[1]] = element_matrix_ref[...]
    mass_ref[...] = node_mass_ref[...]
    nodes, load_nodes = node_tables(map_ref, rank, brow, bcol, panel_dev, slot_rows)
    nodes_ref[...] = jnp.broadcast_to(nodes, nodes_ref.shape)
    load_nodes_ref[...] = jnp.broadcast_to(load_nodes, load_nodes_ref.shape)
    field = field_ref[...]
    write_rims(field, low_part(rank, 2) == 0, rim_first_ref, rim_second_ref)
    loads = load_rows(potential_ref[...], own_map, brow * bcol, slot_rows)
    pieces = trace_rows(field, nodes, parts, bcol, brow * slot_rows)
    write_chunks(chunk_ref, pieces, loads, point_rows(points_ref[...].astype(F32)))


def rim_correction(value, even, first_ref, second_ref, mass, weight):
    step = weight * penalty
    first, second = first_ref[...].astype(F32), second_ref[...].astype(F32)
    left, right = jnp.where(even, second, first), jnp.where(even, first, second)
    last = value.shape[1] - RIM
    low = value[:, :RIM] + left * (step / mass[:, :RIM])
    high = value[:, last:] + right * (step / mass[:, last:])
    return jnp.concatenate([low, value[:, RIM:last], high], axis=1)


def received_loads(chunk_ref, used, brow, columns):
    received = chunk_ref[...].astype(F32)[:, used : used + LOAD_ROWS]
    received = received.reshape(received.shape[0] * LOAD_ROWS, LANES)
    span = received.shape[0] // brow
    rows = []
    for r in range(brow):
        piece = received[r * span : (r + 1) * span]
        rows += [piece[:, :columns], piece[:, columns : HALVES * columns]]
    return jnp.transpose(jnp.concatenate(rows, axis=0))


def sweep_kernel(
    parts, weight, weight_before, keep, rank_ref, coef_ref, field_ref, rhs_ref, mass_ref, keys_ref,
    matrix_ref, *more_refs,
):
    if keep:
        out_ref, kept_ref, sem, *scratch = more_refs
        copy = pltpu.make_async_copy(rhs_ref, kept_ref, sem)
        copy.start()
        rhs_ref = kept_ref
    elif weight_before is None:
        out_ref, *scratch = more_refs
    else:
        first_ref, second_ref, out_ref, field_scr, *scratch = more_refs
    hot_ref, high_ref, low_ref, found_ref, local_ref, product_ref, yhigh_ref, ylow_ref, sum_ref = scratch
    groups = hot_ref.shape[0]
    columns, count = field_ref.shape
    width = count // parts
    mass = mass_ref[...]
    if weight_before is None:
        field = field_ref[...]
        field_now = field_ref
    else:
        even = low_part(rank_ref[0], 2) == 0
        field = rim_correction(field_ref[...], even, first_ref, second_ref, mass, weight_before)
        field_scr[...] = field
        field_now = field_scr
    high, low = split_two(field)
    for h in range(parts):
        high_ref[h * columns : (h + 1) * columns] = high[:, h * width : (h + 1) * width]
        low_ref[h * columns : (h + 1) * columns] = low[:, h * width : (h + 1) * width]
    mat_high, mat_low = split_two(matrix_ref[...])
    matrix = jnp.concatenate(
        [
            jnp.concatenate([mat_high, mat_low], axis=1),
            jnp.concatenate([mat_high, jnp.zeros_like(mat_low)], axis=1),
        ],
        axis=0,
    )

    def build(group):
        for e in range(GROUP):
            key = keys_ref[group * GROUP + e : group * GROUP + e + 1, :]
            hot_ref[group, :, e * LANES : (e + 1) * LANES] = one_hot_rows(low_part(key, width), width)

    def gather(group):
        hot = hot_ref[group]
        found_ref[group % 2] = dot(high_ref[...], hot) + dot(low_ref[...], hot)

    def pick(group):
        slot = group % 2
        for e in range(GROUP):
            element = group * GROUP + e
            key = keys_ref[element : element + 1, :]
            got = pick_part(found_ref[slot, :, e * LANES : (e + 1) * LANES], high_part(key, width), parts)
            got_high, got_low = split_two(got)
            local_ref[slot, e * columns : (e + 1) * columns, :LANES] = got_high
            local_ref[slot, e * columns : (e + 1) * columns, LANES:] = got_low


    def multiply(group):
        product_ref[group % 2] = dot(local_ref[group % 2], matrix)

    def scale(group):
        slot = group % 2
        for e in range(GROUP):
            element = group * GROUP + e
            part = high_part(keys_ref[element : element + 1, :], width)
            rows = product_ref[slot, e * columns : (e + 1) * columns]
            value = (rows[:, :LANES] + rows[:, LANES:]) * coef_ref[element]
            value_high, value_low = split_two(value)
            span = slice(e * LANES, (e + 1) * LANES)
            for h in range(parts):
                mask = jnp.where(part == h, 1.0, 0.0).astype(BF16)
                yhigh_ref[slot, h * columns : (h + 1) * columns, span] = value_high * mask
                ylow_ref[slot, h * columns : (h + 1) * columns, span] = value_low * mask

    def scatter(group):
        hot = hot_ref[group]
        added = dot_nt(yhigh_ref[group % 2], hot) + dot_nt(ylow_ref[group % 2], hot)
        sum_ref[...] = added if group == 0 else sum_ref[...] + added

    build(0)
    gather(0)
    build(1)
    for group in range(groups):
        pick(group)
        if group + 1 < groups:
            gather(group + 1)
        if group + 2 < groups:
            build(group + 2)
        multiply(group)
        if group:
            scatter(group - 1)
        scale(group)
    scatter(groups - 1)
    if keep:
        copy.wait()
    for h in range(parts):
        span = slice(h * width, (h + 1) * width)
        stiff = sum_ref[h * columns : (h + 1) * columns]
        out_ref[:, span] = (1.0 - weight) * field_now[:, span] + (rhs_ref[:, span] - stiff) * (
            weight / mass[:, span]
        )


def loads_kernel(
    parts, brow, weight, used, rank_ref, nodes_ref, chunk_ref, forcing_ref, field_ref, first_ref,
    second_ref, mass_ref, rhs_ref, out_ref, rim_first_ref, rim_second_ref,
):
    columns, count = field_ref.shape
    loads = received_loads(chunk_ref, used, brow, columns)
    added = scatter_nodes(loads, nodes_ref[0:1, :], parts, count)
    rhs_ref[...] = forcing_ref[...] + added
    mass = mass_ref[...]
    even = low_part(rank_ref[0], 2) == 0
    field = field_ref[...] + added * (weight / mass)
    field = rim_correction(field, even, first_ref, second_ref, mass, weight)
    out_ref[...] = field
    write_rims(field, even, rim_first_ref, rim_second_ref)


def total(parts_ref):
    value = parts_ref[0]
    for r in range(1, parts_ref.shape[0]):
        value = value + parts_ref[r]
    return value


def finish_kernel(
    parts, brow, bcol, panel_dev, slot_rows, weight, rank_ref, own_map_ref, nodes_ref, field_ref,
    first_ref, second_ref, mass_ref, parts_ref, out_ref, chunk_ref, rim_first_ref, rim_second_ref,
):
    rank = rank_ref[0]
    even = low_part(rank, 2) == 0
    field = rim_correction(field_ref[...], even, first_ref, second_ref, mass_ref[...], weight)
    out_ref[...] = field
    write_rims(field, even, rim_first_ref, rim_second_ref)
    loads = load_rows(total(parts_ref), own_map_ref[...], brow * bcol, slot_rows)
    pieces = trace_rows(field, nodes_ref[0:1, :], parts, bcol, brow * slot_rows)
    write_chunks(chunk_ref, pieces, loads)


def last_kernel(
    weight, rank_ref, field_ref, first_ref, second_ref, mass_ref, parts_ref, out_ref, potential_ref
):
    even = low_part(rank_ref[0], 2) == 0
    out_ref[...] = rim_correction(field_ref[...], even, first_ref, second_ref, mass_ref[...], weight)
    potential_ref[...] = total(parts_ref)


def density_groups(map_ref, chunk_ref, brow, bcol, panel_dev, slot_rows):
    devices = brow * bcol
    columns = LANES // HALVES
    rows = BLOCKS * slot_rows
    panels = BLOCKS * panel_dev
    lane = lax.broadcasted_iota(jnp.int32, (1, panels), 1).astype(F32)
    block = jnp.floor((lane + 0.5) * (1.0 / panel_dev)).astype(jnp.int32)
    traces = chunk_ref[...].astype(F32)
    for group in range(brow // BLOCKS):
        span = slice(group * panels, (group + 1) * panels)
        owner, slot = map_ref[0:1, span], map_ref[1:2, span]
        half, low = halves_of(slot, slot_rows)
        key = owner * rows + block * slot_rows + low
        near = traces[:, group * rows : (group + 1) * rows].reshape(devices * rows, LANES)
        found = dot(jnp.transpose(near).astype(BF16), one_hot_rows(key, devices * rows))
        density = jnp.where(half == 0, found[:columns], found[columns:])
        turned = jnp.concatenate([-density[columns // 2 :], density[: columns // 2]], axis=0)
        yield density.astype(BF16), turned.astype(BF16)


def write_parts(out_ref, total, panel_dev):
    for r in range(out_ref.shape[0]):
        out_ref[r] = total[:, r * panel_dev : (r + 1) * panel_dev]


def split_three(value):
    high = value.astype(BF16).astype(F32)
    middle = (value - high).astype(BF16).astype(F32)
    return [high, middle, value - high - middle]


def squares(axes):
    return sum(row * row for row in axes[1:]) + axes[0] * axes[0]


def rows_of(rows, dtype=BF16):
    row_id = lax.broadcasted_iota(jnp.int32, (16, rows[0].shape[1]), 0)
    value = jnp.zeros(row_id.shape, F32)
    for index, row in enumerate(rows):
        value = jnp.where(row_id == index, row, value)
    return value.astype(dtype)


def tile_kernel(
    brow, bcol, panel_dev, slot_rows, rank_ref, map_ref, chunk_ref, out_ref, tile_ref,
    target_ref, density_ref, turned_ref, distance_ref, built_ref, sum_ref, sems,
):
    count_all = brow * bcol * panel_dev
    soften = 0.5 * float(count_all) ** (-1.0 / 3.0)
    each = POINT_ROWS // 3
    row_index, col_index = high_part(rank_ref[0], bcol), low_part(rank_ref[0], bcol)
    start = brow * slot_rows + LOAD_ROWS
    block = pl.program_id(0)

    def points_of(device):
        return chunk_ref[device].astype(F32)[start : start + POINT_ROWS]

    def copy_of(index):
        return pltpu.make_async_copy(built_ref.at[index], tile_ref.at[index], sems.at[index])

    @pl.when(block == 0)
    def prepare():
        near = [points_of(row_index * bcol + c) for c in range(bcol)]
        axes = []
        for axis in range(3):
            rows = []
            for piece in near:
                for part in range(each):
                    wide = min(LANES, panel_dev - part * LANES)
                    rows.append(piece[axis * each + part : axis * each + part + 1, :wide])
            axes.append(jnp.concatenate(rows, axis=1))
        norms = split_three(squares(axes) + soften * soften)
        target_ref[...] = rows_of([-2.0 * row for row in axes] + [jnp.ones_like(axes[0])] * 3 + norms)
        sum_ref[...] = jnp.zeros_like(sum_ref)
        groups = density_groups(map_ref, chunk_ref, brow, bcol, panel_dev, slot_rows)
        for group, (density, turned) in enumerate(groups):
            for k in range(BLOCKS):
                span = slice(k * panel_dev, (k + 1) * panel_dev)
                density_ref[group * BLOCKS + k] = density[:, span]
                turned_ref[group * BLOCKS + k] = turned[:, span]

    piece = points_of(block * bcol + col_index)
    axes = [
        jnp.concatenate([piece[axis * each + part : axis * each + part + 1] for part in range(each)], axis=1)
        for axis in range(3)
    ]
    norms = split_three(squares(axes))
    source = jnp.transpose(rows_of(axes + norms + [jnp.ones_like(axes[0])] * 3, F32)).astype(BF16)
    distance_ref[...] = dot(source[:panel_dev], target_ref[...])
    step = 16
    for top in range(0, panel_dev, step):
        squared = distance_ref[top : top + step]
        inverse = lax.rsqrt(squared)
        turns = (squared * inverse) * (wave_number / (2.0 * math.pi))
        turns = turns - ((turns + ROUNDER) - ROUNDER)
        z = turns * turns
        sine = jnp.full_like(z, SIN_POLY[-1])
        for factor in SIN_POLY[-2::-1]:
            sine = sine * z + factor
        sine = sine * turns
        rest = 1.0 - sine * sine
        safe = jnp.maximum(rest, 1e-12)
        cosine = safe * lax.rsqrt(safe)
        double = inverse * (2.0 / math.sqrt(float(count_all)))
        built_ref[block, 0, top : top + step] = ((rest - 0.5) * double).astype(BF16)
        built_ref[block, 1, top : top + step] = (sine * cosine * double).astype(BF16)
    copy_of(block).start()
    sum_ref[...] += dot(density_ref[block], built_ref[block, 0]) + dot(
        turned_ref[block], built_ref[block, 1]
    )

    @pl.when(block == brow - 1)
    def end():
        write_parts(out_ref, sum_ref[...], panel_dev)
        for index in range(brow):
            copy_of(index).wait()


def potential_kernel(
    brow, bcol, panel_dev, slot_rows, map_ref, chunk_ref, tile_ref, out_ref, held_ref, sems,
):
    copies = [
        pltpu.make_async_copy(tile_ref.at[block], held_ref.at[block], sems.at[block])
        for block in range(brow)
    ]
    for copy in copies:
        copy.start()
    whole = None
    groups = density_groups(map_ref, chunk_ref, brow, bcol, panel_dev, slot_rows)
    for group, (density, turned) in enumerate(groups):
        for k in range(BLOCKS):
            block = group * BLOCKS + k
            copies[block].wait()
            span = slice(k * panel_dev, (k + 1) * panel_dev)
            part = dot(density[:, span], held_ref[block, 0]) + dot(turned[:, span], held_ref[block, 1])
            whole = part if whole is None else whole + part
    write_parts(out_ref, whole, panel_dev)


def per_device(
    panel_points,
    panel_map,
    element_nodes,
    element_coef,
    element_matrix,
    node_mass,
    forcing,
    field_start,
    potential_start,
):
    columns, panel_dev = potential_start.shape
    count = field_start.shape[1]
    brow, bcol = lax.axis_size("brow"), lax.axis_size("bcol")
    devices = brow * bcol
    capacity = max(2, 2 * panel_dev // devices)
    slot_rows = -(-capacity // HALVES)
    used = brow * slot_rows
    assert slot_rows <= LOAD_ROWS and columns * HALVES == LANES and brow % BLOCKS == 0
    parts = 256 // columns
    width = count // parts
    row_panels = bcol * panel_dev
    row_index, col_index = lax.axis_index("brow"), lax.axis_index("bcol")
    rank = (row_index * bcol + col_index).reshape(1)
    nodes_each, elements = element_nodes.shape
    assert elements % GROUP == 0
    smem = pl.BlockSpec(memory_space=pltpu.SMEM)
    vmem = pl.BlockSpec(memory_space=pltpu.VMEM)
    rim_shape = shape_of((columns, RIM), BF16)
    field_shape = shape_of((columns, count), F32)
    weights = [weight_of(sweep_index) for sweep_index in range(SWEEPS)]
    even_pairs = [(i, i ^ 1) for i in range(devices)]
    odd_pairs = [pair for i in range(1, devices - 1, 2) for pair in ((i, i + 1), (i + 1, i))]
    even = (rank[0] & 1) == 0

    def chunk_shape(rows, unit):
        return shape_of((devices, -(-rows // unit) * unit, LANES), BF16)

    def exchange(first, second):
        return lax.ppermute(first, AXES, even_pairs), lax.ppermute(second, AXES, odd_pairs)

    def rims(field, halo, weight):
        first, second = (piece.astype(F32) for piece in halo)
        left, right = jnp.where(even, second, first), jnp.where(even, first, second)
        last = count - RIM
        low = field[:, :RIM] + (weight * penalty) * left / mass[:, :RIM]
        high = field[:, last:] + (weight * penalty) * right / mass[:, last:]
        return jnp.where(even, high, low).astype(BF16), jnp.where(even, low, high).astype(BF16)

    def swap_all(chunks):
        return lax.all_to_all(chunks, AXES, split_axis=0, concat_axis=0, tiled=True)

    hbm = pl.BlockSpec(memory_space=pltpu.HBM)
    hot_shape = (elements // GROUP, width, GROUP * LANES)
    tile_shape = (brow, HALVES, panel_dev, bcol * panel_dev)

    def sweep(field, rhs, weight, halo=(), weight_before=None, keep=False):
        rows = parts * columns
        lanes = GROUP * LANES
        large = in_hbm(field, rhs) if keep else (field, rhs)
        given = (rank, *in_hbm(element_coef), *large, *in_vmem(mass, keys, matrix), *halo)
        return call(
            functools.partial(sweep_kernel, parts, weight, weight_before, keep),
            (field_shape, kept((columns, count), F32)) if keep else field_shape,
            5_000_000_000,
            in_specs=[smem, smem, vmem, hbm if keep else vmem] + [vmem] * (len(given) - 4),
            out_specs=(vmem, vmem) if keep else vmem,
            scratch_shapes=[pltpu.SemaphoreType.DMA] * keep
            + [pltpu.VMEM((columns, count), F32)] * bool(halo)
            + [
                pltpu.VMEM(hot_shape, BF16),
                pltpu.VMEM((rows, width), BF16),
                pltpu.VMEM((rows, width), BF16),
                pltpu.VMEM((2, rows, lanes), F32),
                pltpu.VMEM((2, GROUP * columns, 2 * LANES), BF16),
                pltpu.VMEM((2, GROUP * columns, 2 * LANES), F32),
                pltpu.VMEM((2, rows, lanes), BF16),
                pltpu.VMEM((2, rows, lanes), BF16),
                pltpu.VMEM((rows, width), F32),
            ],
        )(*given)

    def add_loads(chunks, field, halo, weight):
        return call(
            functools.partial(loads_kernel, parts, brow, weight, used),
            (field_shape, field_shape, rim_shape, rim_shape),
            500_000_000,
            in_specs=[smem] + [vmem] * 7,
            out_specs=(vmem,) * 4,
        )(rank, *in_vmem(load_nodes), chunks, *in_vmem(forcing_kept), field, *halo, *in_vmem(mass))

    parts_shape = shape_of((bcol, columns, panel_dev), F32)
    sizes = (brow, bcol, panel_dev, slot_rows)
    tile_mib = -(-(2 * math.prod(tile_shape)) // MIB)

    def swap_parts(parts_out):
        return lax.all_to_all(parts_out, "bcol", split_axis=0, concat_axis=0, tiled=True)

    trace_slots, load_slots = table_lanes(brow, bcol, slot_rows)
    (nodes, load_nodes, source_map, own_map, keys, matrix, mass, chunks, *rim) = call(
        functools.partial(setup_kernel, parts, brow, bcol, panel_dev, slot_rows),
        (
            kept((8, trace_slots), jnp.int32),
            kept((8, load_slots), jnp.int32),
            kept((3, brow * panel_dev), jnp.int32),
            kept((3, panel_dev), jnp.int32),
            kept((elements, LANES), jnp.int32),
            kept((LANES, LANES), F32),
            kept((1, count), F32),
            chunk_shape(used + LOAD_ROWS + POINT_ROWS, 8),
            kept(rim_shape.shape, BF16),
            kept(rim_shape.shape, BF16),
        ),
        2_000_000_000,
        in_specs=[smem] + [vmem] * 7,
        out_specs=(vmem,) * 10,
    )(
        rank,
        *in_hbm(
            panel_map, field_start, potential_start, panel_points, element_nodes.T, element_matrix,
            node_mass.reshape(1, count),
        ),
    )
    halo = exchange(*rim)
    chunks = swap_all(chunks)
    field, forcing_kept = sweep(field_start, forcing, weights[0], keep=True)
    parts_out, tiles = call(
        functools.partial(tile_kernel, *sizes),
        (parts_shape, pltpu.HBM(tile_shape, BF16)),
        8_000_000_000,
        grid=(brow,),
        limit=16 + tile_mib,
        in_specs=[smem, vmem, vmem],
        out_specs=(vmem, hbm),
        scratch_shapes=[
            pltpu.VMEM((16, bcol * panel_dev), BF16),
            pltpu.VMEM((brow, columns, panel_dev), BF16),
            pltpu.VMEM((brow, columns, panel_dev), BF16),
            pltpu.VMEM((panel_dev, bcol * panel_dev), F32),
            pltpu.VMEM(tile_shape, BF16),
            pltpu.VMEM((columns, bcol * panel_dev), F32),
            pltpu.SemaphoreType.DMA((brow,)),
        ],
    )(rank, *in_vmem(source_map), chunks)
    parts_in = swap_parts(parts_out)
    rhs, field, *rim = add_loads(chunks, field, halo, weights[0])
    halo = exchange(*rim)
    field = sweep(field, rhs, weights[1])
    halo_next = exchange(*rims(field, halo, weights[1]))
    field = sweep(field, rhs, weights[2], halo, weights[1])
    field, chunks, *rim = call(
        functools.partial(finish_kernel, parts, brow, bcol, panel_dev, slot_rows, weights[2]),
        (field_shape, chunk_shape(used + LOAD_ROWS, 8), rim_shape, rim_shape),
        1_000_000_000,
        in_specs=[smem] + [vmem] * 7,
        out_specs=(vmem,) * 4,
    )(rank, *in_vmem(own_map, nodes), field, *halo_next, *in_vmem(mass), parts_in)

    halo = exchange(*rim)
    chunks = swap_all(chunks)
    field = sweep(field, *in_vmem(forcing_kept), weights[0])
    parts_out = call(
        functools.partial(potential_kernel, *sizes),
        parts_shape,
        2_000_000_000,
        limit=16 + tile_mib,
        in_specs=[vmem, vmem, hbm],
        out_specs=vmem,
        scratch_shapes=[pltpu.VMEM(tile_shape, BF16), pltpu.SemaphoreType.DMA((brow,))],
    )(*in_vmem(source_map), chunks, *in_hbm(tiles))
    parts_in = swap_parts(parts_out)
    rhs, field, *rim = add_loads(chunks, field, halo, weights[0])
    halo = exchange(*rim)
    field = sweep(field, rhs, weights[1])
    halo_next = exchange(*rims(field, halo, weights[1]))
    field = sweep(field, rhs, weights[2], halo, weights[1])
    return call(
        functools.partial(last_kernel, weights[2]),
        (field_shape, shape_of((columns, panel_dev), F32)),
        100_000_000,
        in_specs=[smem] + [vmem] * 5,
        out_specs=(vmem, vmem),
    )(rank, field, *halo_next, *in_vmem(mass), parts_in)


def solution(mesh):
    placed = (
        P(None, AXES),
        P(),
        P(None, AXES),
        P(AXES),
        P(),
        P(AXES),
        P(None, AXES),
        P(None, AXES),
        P(None, AXES),
    )
    return jax.shard_map(
        per_device,
        mesh=mesh,
        in_specs=placed,
        out_specs=(P(None, AXES), P(None, AXES)),
        check_vma=False,
    )
```

```python
import functools
import math

import jax
import jax.numpy as jnp
from jax import lax
from jax.experimental import pallas as pl
from jax.experimental.pallas import tpu as pltpu
from jax.sharding import PartitionSpec as P

RIM = 128
SWEEPS = 3
LANES = 128
LOAD_ROWS = 8
POINT_ROWS = 8
HALVES = 2
GROUP = 4
BLOCKS = 4

wave_number = 20.0
penalty = 0.5

AXES = ("brow", "bcol")
F32 = jnp.float32
BF16 = jnp.bfloat16

SIN_POLY = (3.14159264, -5.16771008, 2.55007752, -0.59829129, 0.07765766)

ROUNDER = 1.5 * 2.0**23
MIB = 1024 * 1024


def weight_of(sweep):
    return 1.0 / (1.25 + 0.75 * math.cos(math.pi * (2 * sweep + 1) / (2.0 * SWEEPS)))


def call(kernel, out_shape, cost, limit=28, **more):
    return pl.pallas_call(
        kernel,
        out_shape=out_shape,
        compiler_params=pltpu.CompilerParams(vmem_limit_bytes=limit * MIB),
        cost_estimate=pl.CostEstimate(flops=cost, bytes_accessed=1 << 20, transcendentals=0),
        **more,
    )


def shape_of(shape, dtype):
    return jax.ShapeDtypeStruct(shape, dtype)


def kept(shape, dtype):
    return pltpu.VMEM(shape, dtype)


def in_hbm(*arrays):
    return tuple(pltpu.with_memory_space_constraint(array, pltpu.HBM) for array in arrays)


def in_vmem(*arrays):
    return tuple(pltpu.with_memory_space_constraint(array, pltpu.VMEM) for array in arrays)


def dot(a, b):
    return jnp.dot(a, b, preferred_element_type=F32)


def dot_nt(a, b):
    return lax.dot_general(a, b, (((1,), (1,)), ((), ())), preferred_element_type=F32)


def split_two(value):
    high = value.astype(BF16)
    return high, (value - high.astype(F32)).astype(BF16)


def low_part(value, size):
    return value & (size - 1) if size & (size - 1) == 0 else value % size


def high_part(value, size):
    return value >> (size.bit_length() - 1) if size & (size - 1) == 0 else value // size


def stack_parts(value, parts):
    width = value.shape[1] // parts
    return jnp.concatenate([value[:, i * width : (i + 1) * width] for i in range(parts)], axis=0)


def one_hot_rows(key, rows):
    seen = lax.broadcasted_iota(jnp.int16, (rows, key.shape[1]), 0)
    return jnp.where(seen == key.astype(jnp.int16), BF16(1), BF16(0))


def pick_part(stacked, part, parts):
    rows = stacked.shape[0] // parts
    picked = stacked[(parts - 1) * rows :]
    for i in reversed(range(parts - 1)):
        picked = jnp.where(part == i, stacked[i * rows : (i + 1) * rows], picked)
    return picked


def gather_nodes(field, nodes, parts):
    width = field.shape[1] // parts
    hot = one_hot_rows(jnp.where(nodes < 0, -1, low_part(nodes, width)), width)
    found = dot(stack_parts(field.astype(BF16), parts), hot)
    return pick_part(found, high_part(nodes, width), parts)


def scatter_nodes(values, nodes, parts, count):
    width = count // parts
    hot = one_hot_rows(jnp.where(nodes < 0, -1, low_part(nodes, width)), width)
    masked = jnp.concatenate(
        [jnp.where(high_part(nodes, width) == i, values, 0.0) for i in range(parts)], axis=0
    ).astype(BF16)
    added = dot_nt(masked, hot)
    rows = values.shape[0]
    return jnp.concatenate([added[i * rows : (i + 1) * rows] for i in range(parts)], axis=1)


def halves_of(slot, rows):
    half = jnp.where(slot >= rows, 1, 0)
    return half, slot - half * rows


def trace_rows(field, nodes, parts, groups, used):
    turned = jnp.transpose(gather_nodes(field, nodes, parts))
    pieces = []
    for group in range(groups):
        base = group * HALVES * used
        pieces.append(
            jnp.concatenate([turned[base : base + used], turned[base + used : base + 2 * used]], axis=1)
        )
    return pieces


def own_panels(map_ref, rank, panel_dev):
    first = rank * panel_dev
    base = (first >> 7) << 7
    window = -(-panel_dev // LANES) * LANES
    near = map_ref[:, pl.ds(pl.multiple_of(base, LANES), window)]
    return jnp.where(first == base, near[:, :panel_dev], near[:, window - panel_dev :])


def load_rows(potential, own_map, devices, slot_rows):
    owner, slot = own_map[0:1], own_map[1:2]
    half, low = halves_of(slot, slot_rows)
    rows = devices * LOAD_ROWS
    key = half * rows + owner * LOAD_ROWS + low
    found = dot_nt(one_hot_rows(key, HALVES * rows), potential.astype(BF16))
    return jnp.concatenate([found[:rows], found[rows:]], axis=1).reshape(devices, LOAD_ROWS, LANES)


def node_tables(map_ref, rank, brow, bcol, panel_dev, slot_rows):
    row_panels = bcol * panel_dev
    trace_slots, load_slots = table_lanes(brow, bcol, slot_rows)
    lane = lax.broadcasted_iota(jnp.int32, (1, row_panels), 1).astype(F32)
    block = jnp.floor((lane + 0.5) * (1.0 / panel_dev)).astype(jnp.int32)
    row_id = lax.broadcasted_iota(jnp.int32, (8, row_panels), 0)
    loads = []
    for r in range(brow):
        span = slice(r * row_panels, (r + 1) * row_panels)
        owner, slot, node = map_ref[0:1, span], map_ref[1:2, span], map_ref[2:3, span]
        half, low = halves_of(slot, slot_rows)
        values = jnp.where(
            row_id == 0, high_part(node, 256), jnp.where(row_id == 1, low_part(node, 256), 1)
        ).astype(F32).astype(BF16)
        key = jnp.where(owner == rank, (half * bcol + block) * LOAD_ROWS + low, -1)
        loads.append(dot_nt(values, one_hot_rows(key, load_slots // brow)))
    loads = jnp.concatenate(loads, axis=1)
    place = lax.broadcasted_iota(jnp.int32, (1, load_slots), 1)
    row, inside = place // (load_slots // brow), place % (load_slots // brow)
    half, inside = inside // (bcol * LOAD_ROWS), inside % (bcol * LOAD_ROWS)
    column, low = inside // LOAD_ROWS, inside % LOAD_ROWS
    key = ((column * HALVES + half) * brow + row) * slot_rows + low
    key = jnp.where((low < slot_rows) & (half < HALVES), key, -1)
    traces = dot_nt(loads.astype(BF16), one_hot_rows(key, trace_slots))
    tables = []
    for found in (traces, loads):
        table = jnp.where(found[2:3] > 0.5, found[0:1] * 256.0 + found[1:2], -1.0)
        tables.append(table.astype(jnp.int32))
    return tables


def table_lanes(brow, bcol, slot_rows):
    trace_slots = -(-HALVES * brow * bcol * slot_rows // LANES) * LANES
    return trace_slots, brow * (-(-HALVES * bcol * LOAD_ROWS // LANES) * LANES)


def point_rows(points):
    row_id = lax.broadcasted_iota(jnp.int32, (POINT_ROWS, LANES), 0)
    each = POINT_ROWS // 3
    width = points.shape[1]
    value = jnp.zeros((POINT_ROWS, LANES), F32)
    for axis in range(3):
        for part in range(-(-width // LANES)):
            piece = points[axis : axis + 1, part * LANES : (part + 1) * LANES]
            short = LANES - piece.shape[1]
            if short:
                piece = jnp.concatenate([piece, jnp.zeros((1, short), F32)], axis=1)
            value = jnp.where(row_id == axis * each + part, piece, value)
    return value


def write_chunks(chunk_ref, pieces, loads, points=None):
    used = pieces[0].shape[0]
    for device in range(chunk_ref.shape[0]):
        rows = [pieces[device % len(pieces)], loads[device]] + ([] if points is None else [points])
        left = chunk_ref.shape[1] - sum(piece.shape[0] for piece in rows)
        if left:
            rows.append(jnp.zeros((left, LANES), F32))
        chunk_ref[device] = jnp.concatenate(rows, axis=0).astype(BF16)


def write_rims(field, even, first_ref, second_ref):
    low = field[:, :RIM]
    high = field[:, field.shape[1] - RIM :]
    first_ref[...] = jnp.where(even, high, low).astype(BF16)
    second_ref[...] = jnp.where(even, low, high).astype(BF16)


def setup_kernel(
    parts, brow, bcol, panel_dev, slot_rows, rank_ref, map_ref, field_ref, potential_ref, points_ref,
    element_nodes_ref, element_matrix_ref, node_mass_ref,
    nodes_ref, load_nodes_ref, source_map_ref, own_map_ref, keys_ref, matrix_ref, mass_ref,
    chunk_ref, rim_first_ref, rim_second_ref,
):
    rank = rank_ref[0]
    source_map_ref[...] = jnp.concatenate(
        [
            own_panels(map_ref, r * bcol + low_part(rank, bcol), panel_dev)
            for r in range(brow)
        ],
        axis=1,
    )
    own_map = own_panels(map_ref, rank, panel_dev)
    own_map_ref[...] = own_map
    keys_ref[...] = jnp.zeros_like(keys_ref)
    keys_ref[:, : element_nodes_ref.shape[1]] = element_nodes_ref[...]
    matrix_ref[...] = jnp.zeros_like(matrix_ref)
    matrix_ref[: element_matrix_ref.shape[0], : element_matrix_ref.shape[1]] = element_matrix_ref[...]
    mass_ref[...] = node_mass_ref[...]
    nodes, load_nodes = node_tables(map_ref, rank, brow, bcol, panel_dev, slot_rows)
    nodes_ref[...] = jnp.broadcast_to(nodes, nodes_ref.shape)
    load_nodes_ref[...] = jnp.broadcast_to(load_nodes, load_nodes_ref.shape)
    field = field_ref[...]
    write_rims(field, low_part(rank, 2) == 0, rim_first_ref, rim_second_ref)
    loads = load_rows(potential_ref[...], own_map, brow * bcol, slot_rows)
    pieces = trace_rows(field, nodes, parts, bcol, brow * slot_rows)
    write_chunks(chunk_ref, pieces, loads, point_rows(points_ref[...].astype(F32)))


def rim_correction(value, even, first_ref, second_ref, mass, weight):
    step = weight * penalty
    first, second = first_ref[...].astype(F32), second_ref[...].astype(F32)
    left, right = jnp.where(even, second, first), jnp.where(even, first, second)
    last = value.shape[1] - RIM
    low = value[:, :RIM] + left * (step / mass[:, :RIM])
    high = value[:, last:] + right * (step / mass[:, last:])
    return jnp.concatenate([low, value[:, RIM:last], high], axis=1)


def received_loads(chunk_ref, used, brow, columns):
    received = chunk_ref[...].astype(F32)[:, used : used + LOAD_ROWS]
    received = received.reshape(received.shape[0] * LOAD_ROWS, LANES)
    span = received.shape[0] // brow
    rows = []
    for r in range(brow):
        piece = received[r * span : (r + 1) * span]
        rows += [piece[:, :columns], piece[:, columns : HALVES * columns]]
    return jnp.transpose(jnp.concatenate(rows, axis=0))


def sweep_kernel(
    parts, weight, weight_before, keep, rank_ref, coef_ref, field_ref, rhs_ref, mass_ref, keys_ref,
    matrix_ref, *more_refs,
):
    if keep:
        out_ref, kept_ref, sem, *scratch = more_refs
        copy = pltpu.make_async_copy(rhs_ref, kept_ref, sem)
        copy.start()
        rhs_ref = kept_ref
    elif weight_before is None:
        out_ref, *scratch = more_refs
    else:
        first_ref, second_ref, out_ref, field_scr, *scratch = more_refs
    hot_ref, high_ref, low_ref, found_ref, local_ref, product_ref, yhigh_ref, ylow_ref, sum_ref = scratch
    groups = hot_ref.shape[0]
    columns, count = field_ref.shape
    width = count // parts
    mass = mass_ref[...]
    if weight_before is None:
        field = field_ref[...]
        field_now = field_ref
    else:
        even = low_part(rank_ref[0], 2) == 0
        field = rim_correction(field_ref[...], even, first_ref, second_ref, mass, weight_before)
        field_scr[...] = field
        field_now = field_scr
    high, low = split_two(field)
    for h in range(parts):
        high_ref[h * columns : (h + 1) * columns] = high[:, h * width : (h + 1) * width]
        low_ref[h * columns : (h + 1) * columns] = low[:, h * width : (h + 1) * width]
    mat_high, mat_low = split_two(matrix_ref[...])
    matrix = jnp.concatenate(
        [
            jnp.concatenate([mat_high, mat_low], axis=1),
            jnp.concatenate([mat_high, jnp.zeros_like(mat_low)], axis=1),
        ],
        axis=0,
    )

    def build(group):
        for e in range(GROUP):
            key = keys_ref[group * GROUP + e : group * GROUP + e + 1, :]
            hot_ref[group, :, e * LANES : (e + 1) * LANES] = one_hot_rows(low_part(key, width), width)

    def gather(group):
        hot = hot_ref[group]
        found_ref[group % 2] = dot(high_ref[...], hot) + dot(low_ref[...], hot)

    def pick(group):
        slot = group % 2
        for e in range(GROUP):
            element = group * GROUP + e
            key = keys_ref[element : element + 1, :]
            got = pick_part(found_ref[slot, :, e * LANES : (e + 1) * LANES], high_part(key, width), parts)
            got_high, got_low = split_two(got)
            local_ref[slot, e * columns : (e + 1) * columns, :LANES] = got_high
            local_ref[slot, e * columns : (e + 1) * columns, LANES:] = got_low


    def multiply(group):
        product_ref[group % 2] = dot(local_ref[group % 2], matrix)

    def scale(group):
        slot = group % 2
        for e in range(GROUP):
            element = group * GROUP + e
            part = high_part(keys_ref[element : element + 1, :], width)
            rows = product_ref[slot, e * columns : (e + 1) * columns]
            value = (rows[:, :LANES] + rows[:, LANES:]) * coef_ref[element]
            value_high, value_low = split_two(value)
            span = slice(e * LANES, (e + 1) * LANES)
            for h in range(parts):
                mask = jnp.where(part == h, 1.0, 0.0).astype(BF16)
                yhigh_ref[slot, h * columns : (h + 1) * columns, span] = value_high * mask
                ylow_ref[slot, h * columns : (h + 1) * columns, span] = value_low * mask

    def scatter(group):
        hot = hot_ref[group]
        added = dot_nt(yhigh_ref[group % 2], hot) + dot_nt(ylow_ref[group % 2], hot)
        sum_ref[...] = added if group == 0 else sum_ref[...] + added

    build(0)
    gather(0)
    build(1)
    for group in range(groups):
        pick(group)
        if group + 1 < groups:
            gather(group + 1)
        if group + 2 < groups:
            build(group + 2)
        multiply(group)
        if group:
            scatter(group - 1)
        scale(group)
    scatter(groups - 1)
    if keep:
        copy.wait()
    for h in range(parts):
        span = slice(h * width, (h + 1) * width)
        stiff = sum_ref[h * columns : (h + 1) * columns]
        out_ref[:, span] = (1.0 - weight) * field_now[:, span] + (rhs_ref[:, span] - stiff) * (
            weight / mass[:, span]
        )


def loads_kernel(
    parts, brow, weight, used, rank_ref, nodes_ref, chunk_ref, forcing_ref, field_ref, first_ref,
    second_ref, mass_ref, rhs_ref, out_ref, rim_first_ref, rim_second_ref,
):
    columns, count = field_ref.shape
    loads = received_loads(chunk_ref, used, brow, columns)
    added = scatter_nodes(loads, nodes_ref[0:1, :], parts, count)
    rhs_ref[...] = forcing_ref[...] + added
    mass = mass_ref[...]
    even = low_part(rank_ref[0], 2) == 0
    field = field_ref[...] + added * (weight / mass)
    field = rim_correction(field, even, first_ref, second_ref, mass, weight)
    out_ref[...] = field
    write_rims(field, even, rim_first_ref, rim_second_ref)


def total(parts_ref):
    value = parts_ref[0]
    for r in range(1, parts_ref.shape[0]):
        value = value + parts_ref[r]
    return value


def finish_kernel(
    parts, brow, bcol, panel_dev, slot_rows, weight, rank_ref, own_map_ref, nodes_ref, field_ref,
    first_ref, second_ref, mass_ref, parts_ref, out_ref, chunk_ref, rim_first_ref, rim_second_ref,
):
    rank = rank_ref[0]
    even = low_part(rank, 2) == 0
    field = rim_correction(field_ref[...], even, first_ref, second_ref, mass_ref[...], weight)
    out_ref[...] = field
    write_rims(field, even, rim_first_ref, rim_second_ref)
    loads = load_rows(total(parts_ref), own_map_ref[...], brow * bcol, slot_rows)
    pieces = trace_rows(field, nodes_ref[0:1, :], parts, bcol, brow * slot_rows)
    write_chunks(chunk_ref, pieces, loads)


def last_kernel(
    weight, rank_ref, field_ref, first_ref, second_ref, mass_ref, parts_ref, out_ref, potential_ref
):
    even = low_part(rank_ref[0], 2) == 0
    out_ref[...] = rim_correction(field_ref[...], even, first_ref, second_ref, mass_ref[...], weight)
    potential_ref[...] = total(parts_ref)


def density_groups(map_ref, chunk_ref, brow, bcol, panel_dev, slot_rows):
    devices = brow * bcol
    columns = LANES // HALVES
    rows = BLOCKS * slot_rows
    panels = BLOCKS * panel_dev
    lane = lax.broadcasted_iota(jnp.int32, (1, panels), 1).astype(F32)
    block = jnp.floor((lane + 0.5) * (1.0 / panel_dev)).astype(jnp.int32)
    traces = chunk_ref[...].astype(F32)
    for group in range(brow // BLOCKS):
        span = slice(group * panels, (group + 1) * panels)
        owner, slot = map_ref[0:1, span], map_ref[1:2, span]
        half, low = halves_of(slot, slot_rows)
        key = owner * rows + block * slot_rows + low
        near = traces[:, group * rows : (group + 1) * rows].reshape(devices * rows, LANES)
        found = dot(jnp.transpose(near).astype(BF16), one_hot_rows(key, devices * rows))
        density = jnp.where(half == 0, found[:columns], found[columns:])
        turned = jnp.concatenate([-density[columns // 2 :], density[: columns // 2]], axis=0)
        yield density.astype(BF16), turned.astype(BF16)


def write_parts(out_ref, total, panel_dev):
    for r in range(out_ref.shape[0]):
        out_ref[r] = total[:, r * panel_dev : (r + 1) * panel_dev]


def split_three(value):
    high = value.astype(BF16).astype(F32)
    middle = (value - high).astype(BF16).astype(F32)
    return [high, middle, value - high - middle]


def squares(axes):
    return sum(row * row for row in axes[1:]) + axes[0] * axes[0]


def rows_of(rows, dtype=BF16):
    row_id = lax.broadcasted_iota(jnp.int32, (16, rows[0].shape[1]), 0)
    value = jnp.zeros(row_id.shape, F32)
    for index, row in enumerate(rows):
        value = jnp.where(row_id == index, row, value)
    return value.astype(dtype)


def tile_kernel(
    brow, bcol, panel_dev, slot_rows, rank_ref, map_ref, chunk_ref, out_ref, tile_ref,
    target_ref, density_ref, turned_ref, distance_ref, built_ref, sum_ref, sems,
):
    count_all = brow * bcol * panel_dev
    soften = 0.5 * float(count_all) ** (-1.0 / 3.0)
    each = POINT_ROWS // 3
    row_index, col_index = high_part(rank_ref[0], bcol), low_part(rank_ref[0], bcol)
    start = brow * slot_rows + LOAD_ROWS
    block = pl.program_id(0)

    def points_of(device):
        return chunk_ref[device].astype(F32)[start : start + POINT_ROWS]

    def copy_of(index):
        return pltpu.make_async_copy(built_ref.at[index], tile_ref.at[index], sems.at[index])

    @pl.when(block == 0)
    def prepare():
        near = [points_of(row_index * bcol + c) for c in range(bcol)]
        axes = []
        for axis in range(3):
            rows = []
            for piece in near:
                for part in range(each):
                    wide = min(LANES, panel_dev - part * LANES)
                    rows.append(piece[axis * each + part : axis * each + part + 1, :wide])
            axes.append(jnp.concatenate(rows, axis=1))
        norms = split_three(squares(axes) + soften * soften)
        target_ref[...] = rows_of([-2.0 * row for row in axes] + [jnp.ones_like(axes[0])] * 3 + norms)
        sum_ref[...] = jnp.zeros_like(sum_ref)
        groups = density_groups(map_ref, chunk_ref, brow, bcol, panel_dev, slot_rows)
        for group, (density, turned) in enumerate(groups):
            for k in range(BLOCKS):
                span = slice(k * panel_dev, (k + 1) * panel_dev)
                density_ref[group * BLOCKS + k] = density[:, span]
                turned_ref[group * BLOCKS + k] = turned[:, span]

    piece = points_of(block * bcol + col_index)
    axes = [
        jnp.concatenate([piece[axis * each + part : axis * each + part + 1] for part in range(each)], axis=1)
        for axis in range(3)
    ]
    norms = split_three(squares(axes))
    source = jnp.transpose(rows_of(axes + norms + [jnp.ones_like(axes[0])] * 3, F32)).astype(BF16)
    distance_ref[...] = dot(source[:panel_dev], target_ref[...])
    step, lanes = 16, 4 * LANES
    wide = distance_ref.shape[1]
    places = [
        (slice(top, top + step), slice(left, min(left + lanes, wide)))
        for top in range(0, panel_dev, step)
        for left in range(0, wide, lanes)
    ]
    for rows, span in places:
        squared = distance_ref[rows, span]
        inverse = lax.rsqrt(squared)
        turns = (squared * inverse) * (wave_number / (2.0 * math.pi))
        turns = turns - ((turns + ROUNDER) - ROUNDER)
        z = turns * turns
        sine = jnp.full_like(z, SIN_POLY[-1])
        for factor in SIN_POLY[-2::-1]:
            sine = sine * z + factor
        sine = sine * turns
        rest = 1.0 - sine * sine
        safe = jnp.maximum(rest, 1e-12)
        cosine = safe * lax.rsqrt(safe)
        double = inverse * (2.0 / math.sqrt(float(count_all)))
        built_ref[block, 0, rows, span] = ((rest - 0.5) * double).astype(BF16)
        built_ref[block, 1, rows, span] = (sine * cosine * double).astype(BF16)
    copy_of(block).start()
    sum_ref[...] += dot(density_ref[block], built_ref[block, 0]) + dot(
        turned_ref[block], built_ref[block, 1]
    )

    @pl.when(block == brow - 1)
    def end():
        write_parts(out_ref, sum_ref[...], panel_dev)
        for index in range(brow):
            copy_of(index).wait()


def potential_kernel(
    brow, bcol, panel_dev, slot_rows, map_ref, chunk_ref, tile_ref, out_ref, held_ref, sems,
):
    copies = [
        pltpu.make_async_copy(tile_ref.at[block], held_ref.at[block], sems.at[block])
        for block in range(brow)
    ]
    for copy in copies:
        copy.start()
    whole = None
    groups = density_groups(map_ref, chunk_ref, brow, bcol, panel_dev, slot_rows)
    for group, (density, turned) in enumerate(groups):
        for k in range(BLOCKS):
            block = group * BLOCKS + k
            copies[block].wait()
            span = slice(k * panel_dev, (k + 1) * panel_dev)
            part = dot(density[:, span], held_ref[block, 0]) + dot(turned[:, span], held_ref[block, 1])
            whole = part if whole is None else whole + part
    write_parts(out_ref, whole, panel_dev)


def per_device(
    panel_points,
    panel_map,
    element_nodes,
    element_coef,
    element_matrix,
    node_mass,
    forcing,
    field_start,
    potential_start,
):
    columns, panel_dev = potential_start.shape
    count = field_start.shape[1]
    brow, bcol = lax.axis_size("brow"), lax.axis_size("bcol")
    devices = brow * bcol
    capacity = max(2, 2 * panel_dev // devices)
    slot_rows = -(-capacity // HALVES)
    used = brow * slot_rows
    assert slot_rows <= LOAD_ROWS and columns * HALVES == LANES and brow % BLOCKS == 0
    parts = 256 // columns
    width = count // parts
    row_panels = bcol * panel_dev
    row_index, col_index = lax.axis_index("brow"), lax.axis_index("bcol")
    rank = (row_index * bcol + col_index).reshape(1)
    nodes_each, elements = element_nodes.shape
    assert elements % GROUP == 0
    smem = pl.BlockSpec(memory_space=pltpu.SMEM)
    vmem = pl.BlockSpec(memory_space=pltpu.VMEM)
    rim_shape = shape_of((columns, RIM), BF16)
    field_shape = shape_of((columns, count), F32)
    weights = [weight_of(sweep_index) for sweep_index in range(SWEEPS)]
    even_pairs = [(i, i ^ 1) for i in range(devices)]
    odd_pairs = [pair for i in range(1, devices - 1, 2) for pair in ((i, i + 1), (i + 1, i))]
    even = (rank[0] & 1) == 0

    def chunk_shape(rows, unit):
        return shape_of((devices, -(-rows // unit) * unit, LANES), BF16)

    def exchange(first, second):
        return lax.ppermute(first, AXES, even_pairs), lax.ppermute(second, AXES, odd_pairs)

    def rims(field, halo, weight):
        first, second = (piece.astype(F32) for piece in halo)
        left, right = jnp.where(even, second, first), jnp.where(even, first, second)
        last = count - RIM
        low = field[:, :RIM] + (weight * penalty) * left / mass[:, :RIM]
        high = field[:, last:] + (weight * penalty) * right / mass[:, last:]
        return jnp.where(even, high, low).astype(BF16), jnp.where(even, low, high).astype(BF16)

    def swap_all(chunks):
        return lax.all_to_all(chunks, AXES, split_axis=0, concat_axis=0, tiled=True)

    hbm = pl.BlockSpec(memory_space=pltpu.HBM)
    hot_shape = (elements // GROUP, width, GROUP * LANES)
    tile_shape = (brow, HALVES, panel_dev, bcol * panel_dev)

    def sweep(field, rhs, weight, halo=(), weight_before=None, keep=False):
        rows = parts * columns
        lanes = GROUP * LANES
        large = in_hbm(field, rhs) if keep else (field, rhs)
        given = (rank, *in_hbm(element_coef), *large, *in_vmem(mass, keys, matrix), *halo)
        return call(
            functools.partial(sweep_kernel, parts, weight, weight_before, keep),
            (field_shape, kept((columns, count), F32)) if keep else field_shape,
            5_000_000_000,
            in_specs=[smem, smem, vmem, hbm if keep else vmem] + [vmem] * (len(given) - 4),
            out_specs=(vmem, vmem) if keep else vmem,
            scratch_shapes=[pltpu.SemaphoreType.DMA] * keep
            + [pltpu.VMEM((columns, count), F32)] * bool(halo)
            + [
                pltpu.VMEM(hot_shape, BF16),
                pltpu.VMEM((rows, width), BF16),
                pltpu.VMEM((rows, width), BF16),
                pltpu.VMEM((2, rows, lanes), F32),
                pltpu.VMEM((2, GROUP * columns, 2 * LANES), BF16),
                pltpu.VMEM((2, GROUP * columns, 2 * LANES), F32),
                pltpu.VMEM((2, rows, lanes), BF16),
                pltpu.VMEM((2, rows, lanes), BF16),
                pltpu.VMEM((rows, width), F32),
            ],
        )(*given)

    def add_loads(chunks, field, halo, weight):
        return call(
            functools.partial(loads_kernel, parts, brow, weight, used),
            (field_shape, field_shape, rim_shape, rim_shape),
            500_000_000,
            in_specs=[smem] + [vmem] * 7,
            out_specs=(vmem,) * 4,
        )(rank, *in_vmem(load_nodes), chunks, *in_vmem(forcing_kept), field, *halo, *in_vmem(mass))

    parts_shape = shape_of((bcol, columns, panel_dev), F32)
    sizes = (brow, bcol, panel_dev, slot_rows)
    tile_mib = -(-(2 * math.prod(tile_shape)) // MIB)

    def swap_parts(parts_out):
        return lax.all_to_all(parts_out, "bcol", split_axis=0, concat_axis=0, tiled=True)

    trace_slots, load_slots = table_lanes(brow, bcol, slot_rows)
    (nodes, load_nodes, source_map, own_map, keys, matrix, mass, chunks, *rim) = call(
        functools.partial(setup_kernel, parts, brow, bcol, panel_dev, slot_rows),
        (
            kept((8, trace_slots), jnp.int32),
            kept((8, load_slots), jnp.int32),
            kept((3, brow * panel_dev), jnp.int32),
            kept((3, panel_dev), jnp.int32),
            kept((elements, LANES), jnp.int32),
            kept((LANES, LANES), F32),
            kept((1, count), F32),
            chunk_shape(used + LOAD_ROWS + POINT_ROWS, 8),
            kept(rim_shape.shape, BF16),
            kept(rim_shape.shape, BF16),
        ),
        2_000_000_000,
        in_specs=[smem] + [vmem] * 7,
        out_specs=(vmem,) * 10,
    )(
        rank,
        *in_hbm(
            panel_map, field_start, potential_start, panel_points, element_nodes.T, element_matrix,
            node_mass.reshape(1, count),
        ),
    )
    halo = exchange(*rim)
    chunks = swap_all(chunks)
    field, forcing_kept = sweep(field_start, forcing, weights[0], keep=True)
    parts_out, tiles = call(
        functools.partial(tile_kernel, *sizes),
        (parts_shape, pltpu.HBM(tile_shape, BF16)),
        8_000_000_000,
        grid=(brow,),
        limit=16 + tile_mib,
        in_specs=[smem, vmem, vmem],
        out_specs=(vmem, hbm),
        scratch_shapes=[
            pltpu.VMEM((16, bcol * panel_dev), BF16),
            pltpu.VMEM((brow, columns, panel_dev), BF16),
            pltpu.VMEM((brow, columns, panel_dev), BF16),
            pltpu.VMEM((panel_dev, bcol * panel_dev), F32),
            pltpu.VMEM(tile_shape, BF16),
            pltpu.VMEM((columns, bcol * panel_dev), F32),
            pltpu.SemaphoreType.DMA((brow,)),
        ],
    )(rank, *in_vmem(source_map), chunks)
    parts_in = swap_parts(parts_out)
    rhs, field, *rim = add_loads(chunks, field, halo, weights[0])
    halo = exchange(*rim)
    field = sweep(field, rhs, weights[1])
    halo_next = exchange(*rims(field, halo, weights[1]))
    field = sweep(field, rhs, weights[2], halo, weights[1])
    field, chunks, *rim = call(
        functools.partial(finish_kernel, parts, brow, bcol, panel_dev, slot_rows, weights[2]),
        (field_shape, chunk_shape(used + LOAD_ROWS, 8), rim_shape, rim_shape),
        1_000_000_000,
        in_specs=[smem] + [vmem] * 7,
        out_specs=(vmem,) * 4,
    )(rank, *in_vmem(own_map, nodes), field, *halo_next, *in_vmem(mass), parts_in)

    halo = exchange(*rim)
    chunks = swap_all(chunks)
    field = sweep(field, *in_vmem(forcing_kept), weights[0])
    parts_out = call(
        functools.partial(potential_kernel, *sizes),
        parts_shape,
        2_000_000_000,
        limit=16 + tile_mib,
        in_specs=[vmem, vmem, hbm],
        out_specs=vmem,
        scratch_shapes=[pltpu.VMEM(tile_shape, BF16), pltpu.SemaphoreType.DMA((brow,))],
    )(*in_vmem(source_map), chunks, *in_hbm(tiles))
    parts_in = swap_parts(parts_out)
    rhs, field, *rim = add_loads(chunks, field, halo, weights[0])
    halo = exchange(*rim)
    field = sweep(field, rhs, weights[1])
    halo_next = exchange(*rims(field, halo, weights[1]))
    field = sweep(field, rhs, weights[2], halo, weights[1])
    return call(
        functools.partial(last_kernel, weights[2]),
        (field_shape, shape_of((columns, panel_dev), F32)),
        100_000_000,
        in_specs=[smem] + [vmem] * 5,
        out_specs=(vmem, vmem),
    )(rank, field, *halo_next, *in_vmem(mass), parts_in)


def solution(mesh):
    placed = (
        P(None, AXES),
        P(),
        P(None, AXES),
        P(AXES),
        P(),
        P(AXES),
        P(None, AXES),
        P(None, AXES),
        P(None, AXES),
    )
    return jax.shard_map(
        per_device,
        mesh=mesh,
        in_specs=placed,
        out_specs=(P(None, AXES), P(None, AXES)),
        check_vma=False,
    )
```

```python
import functools
import math

import jax
import jax.numpy as jnp
from jax import lax
from jax.experimental import pallas as pl
from jax.experimental.pallas import tpu as pltpu
from jax.sharding import PartitionSpec as P

RIM = 128
SWEEPS = 3
LANES = 128
LOAD_ROWS = 8
POINT_ROWS = 8
HALVES = 2
GROUP = 8
BLOCKS = 4

wave_number = 20.0
penalty = 0.5

AXES = ("brow", "bcol")
F32 = jnp.float32
BF16 = jnp.bfloat16

SIN_POLY = (3.14159264, -5.16771008, 2.55007752, -0.59829129, 0.07765766)

ROUNDER = 1.5 * 2.0**23
MIB = 1024 * 1024


def weight_of(sweep):
    return 1.0 / (1.25 + 0.75 * math.cos(math.pi * (2 * sweep + 1) / (2.0 * SWEEPS)))


def call(kernel, out_shape, cost, limit=28, **more):
    return pl.pallas_call(
        kernel,
        out_shape=out_shape,
        compiler_params=pltpu.CompilerParams(vmem_limit_bytes=limit * MIB),
        cost_estimate=pl.CostEstimate(flops=cost, bytes_accessed=1 << 20, transcendentals=0),
        **more,
    )


def shape_of(shape, dtype):
    return jax.ShapeDtypeStruct(shape, dtype)


def kept(shape, dtype):
    return pltpu.VMEM(shape, dtype)


def in_hbm(*arrays):
    return tuple(pltpu.with_memory_space_constraint(array, pltpu.HBM) for array in arrays)


def in_vmem(*arrays):
    return tuple(pltpu.with_memory_space_constraint(array, pltpu.VMEM) for array in arrays)


def dot(a, b):
    return jnp.dot(a, b, preferred_element_type=F32)


def dot_nt(a, b):
    return lax.dot_general(a, b, (((1,), (1,)), ((), ())), preferred_element_type=F32)


def split_two(value):
    high = value.astype(BF16)
    return high, (value - high.astype(F32)).astype(BF16)


def low_part(value, size):
    return value & (size - 1) if size & (size - 1) == 0 else value % size


def high_part(value, size):
    return value >> (size.bit_length() - 1) if size & (size - 1) == 0 else value // size


def stack_parts(value, parts):
    width = value.shape[1] // parts
    return jnp.concatenate([value[:, i * width : (i + 1) * width] for i in range(parts)], axis=0)


def one_hot_rows(key, rows):
    seen = lax.broadcasted_iota(jnp.int16, (rows, key.shape[1]), 0)
    return jnp.where(seen == key.astype(jnp.int16), BF16(1), BF16(0))


def pick_part(stacked, part, parts):
    rows = stacked.shape[0] // parts
    picked = stacked[(parts - 1) * rows :]
    for i in reversed(range(parts - 1)):
        picked = jnp.where(part == i, stacked[i * rows : (i + 1) * rows], picked)
    return picked


def gather_nodes(field, nodes, parts):
    width = field.shape[1] // parts
    hot = one_hot_rows(jnp.where(nodes < 0, -1, low_part(nodes, width)), width)
    found = dot(stack_parts(field.astype(BF16), parts), hot)
    return pick_part(found, high_part(nodes, width), parts)


def scatter_nodes(values, nodes, parts, count):
    width = count // parts
    hot = one_hot_rows(jnp.where(nodes < 0, -1, low_part(nodes, width)), width)
    masked = jnp.concatenate(
        [jnp.where(high_part(nodes, width) == i, values, 0.0) for i in range(parts)], axis=0
    ).astype(BF16)
    added = dot_nt(masked, hot)
    rows = values.shape[0]
    return jnp.concatenate([added[i * rows : (i + 1) * rows] for i in range(parts)], axis=1)


def halves_of(slot, rows):
    half = jnp.where(slot >= rows, 1, 0)
    return half, slot - half * rows


def trace_rows(field, nodes, parts, groups, used):
    turned = jnp.transpose(gather_nodes(field, nodes, parts))
    pieces = []
    for group in range(groups):
        base = group * HALVES * used
        pieces.append(
            jnp.concatenate([turned[base : base + used], turned[base + used : base + 2 * used]], axis=1)
        )
    return pieces


def own_panels(map_ref, rank, panel_dev):
    first = rank * panel_dev
    base = (first >> 7) << 7
    window = -(-panel_dev // LANES) * LANES
    near = map_ref[:, pl.ds(pl.multiple_of(base, LANES), window)]
    return jnp.where(first == base, near[:, :panel_dev], near[:, window - panel_dev :])


def load_rows(potential, own_map, devices, slot_rows):
    owner, slot = own_map[0:1], own_map[1:2]
    half, low = halves_of(slot, slot_rows)
    rows = devices * LOAD_ROWS
    key = half * rows + owner * LOAD_ROWS + low
    found = dot_nt(one_hot_rows(key, HALVES * rows), potential.astype(BF16))
    return jnp.concatenate([found[:rows], found[rows:]], axis=1).reshape(devices, LOAD_ROWS, LANES)


def node_tables(map_ref, rank, brow, bcol, panel_dev, slot_rows):
    row_panels = bcol * panel_dev
    trace_slots, load_slots = table_lanes(brow, bcol, slot_rows)
    lane = lax.broadcasted_iota(jnp.int32, (1, row_panels), 1).astype(F32)
    block = jnp.floor((lane + 0.5) * (1.0 / panel_dev)).astype(jnp.int32)
    row_id = lax.broadcasted_iota(jnp.int32, (8, row_panels), 0)
    loads = []
    for r in range(brow):
        span = slice(r * row_panels, (r + 1) * row_panels)
        owner, slot, node = map_ref[0:1, span], map_ref[1:2, span], map_ref[2:3, span]
        half, low = halves_of(slot, slot_rows)
        values = jnp.where(
            row_id == 0, high_part(node, 256), jnp.where(row_id == 1, low_part(node, 256), 1)
        ).astype(F32).astype(BF16)
        key = jnp.where(owner == rank, (half * bcol + block) * LOAD_ROWS + low, -1)
        loads.append(dot_nt(values, one_hot_rows(key, load_slots // brow)))
    loads = jnp.concatenate(loads, axis=1)
    place = lax.broadcasted_iota(jnp.int32, (1, load_slots), 1)
    row, inside = place // (load_slots // brow), place % (load_slots // brow)
    half, inside = inside // (bcol * LOAD_ROWS), inside % (bcol * LOAD_ROWS)
    column, low = inside // LOAD_ROWS, inside % LOAD_ROWS
    key = ((column * HALVES + half) * brow + row) * slot_rows + low
    key = jnp.where((low < slot_rows) & (half < HALVES), key, -1)
    traces = dot_nt(loads.astype(BF16), one_hot_rows(key, trace_slots))
    tables = []
    for found in (traces, loads):
        table = jnp.where(found[2:3] > 0.5, found[0:1] * 256.0 + found[1:2], -1.0)
        tables.append(table.astype(jnp.int32))
    return tables


def table_lanes(brow, bcol, slot_rows):
    trace_slots = -(-HALVES * brow * bcol * slot_rows // LANES) * LANES
    return trace_slots, brow * (-(-HALVES * bcol * LOAD_ROWS // LANES) * LANES)


def point_rows(points):
    row_id = lax.broadcasted_iota(jnp.int32, (POINT_ROWS, LANES), 0)
    each = POINT_ROWS // 3
    width = points.shape[1]
    value = jnp.zeros((POINT_ROWS, LANES), F32)
    for axis in range(3):
        for part in range(-(-width // LANES)):
            piece = points[axis : axis + 1, part * LANES : (part + 1) * LANES]
            short = LANES - piece.shape[1]
            if short:
                piece = jnp.concatenate([piece, jnp.zeros((1, short), F32)], axis=1)
            value = jnp.where(row_id == axis * each + part, piece, value)
    return value


def write_chunks(chunk_ref, pieces, loads, points=None):
    used = pieces[0].shape[0]
    for device in range(chunk_ref.shape[0]):
        rows = [pieces[device % len(pieces)], loads[device]] + ([] if points is None else [points])
        left = chunk_ref.shape[1] - sum(piece.shape[0] for piece in rows)
        if left:
            rows.append(jnp.zeros((left, LANES), F32))
        chunk_ref[device] = jnp.concatenate(rows, axis=0).astype(BF16)


def write_rims(field, even, first_ref, second_ref):
    low = field[:, :RIM]
    high = field[:, field.shape[1] - RIM :]
    first_ref[...] = jnp.where(even, high, low).astype(BF16)
    second_ref[...] = jnp.where(even, low, high).astype(BF16)


def setup_kernel(
    parts, brow, bcol, panel_dev, slot_rows, rank_ref, map_ref, field_ref, potential_ref, points_ref,
    element_nodes_ref, element_matrix_ref, node_mass_ref,
    nodes_ref, load_nodes_ref, source_map_ref, own_map_ref, keys_ref, matrix_ref, mass_ref,
    field_kept_ref, chunk_ref, rim_first_ref, rim_second_ref,
):
    rank = rank_ref[0]
    source_map_ref[...] = jnp.concatenate(
        [
            own_panels(map_ref, r * bcol + low_part(rank, bcol), panel_dev)
            for r in range(brow)
        ],
        axis=1,
    )
    own_map = own_panels(map_ref, rank, panel_dev)
    own_map_ref[...] = own_map
    keys_ref[...] = jnp.zeros_like(keys_ref)
    keys_ref[:, : element_nodes_ref.shape[1]] = element_nodes_ref[...]
    matrix_ref[...] = jnp.zeros_like(matrix_ref)
    matrix_ref[: element_matrix_ref.shape[0], : element_matrix_ref.shape[1]] = element_matrix_ref[...]
    mass_ref[...] = node_mass_ref[...]
    nodes, load_nodes = node_tables(map_ref, rank, brow, bcol, panel_dev, slot_rows)
    nodes_ref[...] = jnp.broadcast_to(nodes, nodes_ref.shape)
    load_nodes_ref[...] = jnp.broadcast_to(load_nodes, load_nodes_ref.shape)
    field = field_ref[...]
    field_kept_ref[...] = field
    write_rims(field, low_part(rank, 2) == 0, rim_first_ref, rim_second_ref)
    loads = load_rows(potential_ref[...], own_map, brow * bcol, slot_rows)
    pieces = trace_rows(field, nodes, parts, bcol, brow * slot_rows)
    write_chunks(chunk_ref, pieces, loads, point_rows(points_ref[...].astype(F32)))


def rim_correction(value, even, first_ref, second_ref, mass, weight):
    step = weight * penalty
    first, second = first_ref[...].astype(F32), second_ref[...].astype(F32)
    left, right = jnp.where(even, second, first), jnp.where(even, first, second)
    last = value.shape[1] - RIM
    low = value[:, :RIM] + left * (step / mass[:, :RIM])
    high = value[:, last:] + right * (step / mass[:, last:])
    return jnp.concatenate([low, value[:, RIM:last], high], axis=1)


def received_loads(chunk_ref, used, brow, columns):
    received = chunk_ref[...].astype(F32)[:, used : used + LOAD_ROWS]
    received = received.reshape(received.shape[0] * LOAD_ROWS, LANES)
    span = received.shape[0] // brow
    rows = []
    for r in range(brow):
        piece = received[r * span : (r + 1) * span]
        rows += [piece[:, :columns], piece[:, columns : HALVES * columns]]
    return jnp.transpose(jnp.concatenate(rows, axis=0))


def sweep_kernel(
    parts, weight, weight_before, keep, rank_ref, coef_ref, field_ref, rhs_ref, mass_ref, keys_ref,
    matrix_ref, *more_refs,
):
    if keep:
        out_ref, kept_ref, sem, *scratch = more_refs
        copy = pltpu.make_async_copy(rhs_ref, kept_ref, sem)
        copy.start()
        rhs_ref = kept_ref
    elif weight_before is None:
        out_ref, *scratch = more_refs
    else:
        first_ref, second_ref, out_ref, field_scr, *scratch = more_refs
    hot_ref, high_ref, low_ref, found_ref, local_ref, product_ref, yhigh_ref, ylow_ref, sum_ref = scratch
    groups = hot_ref.shape[0]
    columns, count = field_ref.shape
    width = count // parts
    mass = mass_ref[...]
    if weight_before is None:
        field = field_ref[...]
        field_now = field_ref
    else:
        even = low_part(rank_ref[0], 2) == 0
        field = rim_correction(field_ref[...], even, first_ref, second_ref, mass, weight_before)
        field_scr[...] = field
        field_now = field_scr
    high, low = split_two(field)
    for h in range(parts):
        high_ref[h * columns : (h + 1) * columns] = high[:, h * width : (h + 1) * width]
        low_ref[h * columns : (h + 1) * columns] = low[:, h * width : (h + 1) * width]
    mat_high, mat_low = split_two(matrix_ref[...])
    matrix = jnp.concatenate(
        [
            jnp.concatenate([mat_high, mat_low], axis=1),
            jnp.concatenate([mat_high, jnp.zeros_like(mat_low)], axis=1),
        ],
        axis=0,
    )

    def build(group):
        for e in range(GROUP):
            key = keys_ref[group * GROUP + e : group * GROUP + e + 1, :]
            hot_ref[group, :, e * LANES : (e + 1) * LANES] = one_hot_rows(low_part(key, width), width)

    def gather(group):
        hot = hot_ref[group]
        found_ref[group % 2] = dot(high_ref[...], hot) + dot(low_ref[...], hot)

    def pick(group):
        slot = group % 2
        for e in range(GROUP):
            element = group * GROUP + e
            key = keys_ref[element : element + 1, :]
            got = pick_part(found_ref[slot, :, e * LANES : (e + 1) * LANES], high_part(key, width), parts)
            got_high, got_low = split_two(got)
            local_ref[slot, e * columns : (e + 1) * columns, :LANES] = got_high
            local_ref[slot, e * columns : (e + 1) * columns, LANES:] = got_low


    def multiply(group):
        product_ref[group % 2] = dot(local_ref[group % 2], matrix)

    def scale(group):
        slot = group % 2
        for e in range(GROUP):
            element = group * GROUP + e
            part = high_part(keys_ref[element : element + 1, :], width)
            rows = product_ref[slot, e * columns : (e + 1) * columns]
            value = (rows[:, :LANES] + rows[:, LANES:]) * coef_ref[element]
            value_high, value_low = split_two(value)
            span = slice(e * LANES, (e + 1) * LANES)
            for h in range(parts):
                mask = jnp.where(part == h, 1.0, 0.0).astype(BF16)
                yhigh_ref[slot, h * columns : (h + 1) * columns, span] = value_high * mask
                ylow_ref[slot, h * columns : (h + 1) * columns, span] = value_low * mask

    def scatter(group):
        hot = hot_ref[group]
        added = dot_nt(yhigh_ref[group % 2], hot) + dot_nt(ylow_ref[group % 2], hot)
        sum_ref[...] = added if group == 0 else sum_ref[...] + added

    build(0)
    gather(0)
    build(1)
    for group in range(groups):
        pick(group)
        if group + 1 < groups:
            gather(group + 1)
        if group + 2 < groups:
            build(group + 2)
        multiply(group)
        if group:
            scatter(group - 1)
        scale(group)
    scatter(groups - 1)
    if keep:
        copy.wait()
    for h in range(parts):
        span = slice(h * width, (h + 1) * width)
        stiff = sum_ref[h * columns : (h + 1) * columns]
        out_ref[:, span] = (1.0 - weight) * field_now[:, span] + (rhs_ref[:, span] - stiff) * (
            weight / mass[:, span]
        )


def loads_kernel(
    parts, brow, weight, used, rank_ref, nodes_ref, chunk_ref, forcing_ref, field_ref, first_ref,
    second_ref, mass_ref, rhs_ref, out_ref, rim_first_ref, rim_second_ref,
):
    columns, count = field_ref.shape
    loads = received_loads(chunk_ref, used, brow, columns)
    added = scatter_nodes(loads, nodes_ref[0:1, :], parts, count)
    rhs_ref[...] = forcing_ref[...] + added
    mass = mass_ref[...]
    even = low_part(rank_ref[0], 2) == 0
    field = field_ref[...] + added * (weight / mass)
    field = rim_correction(field, even, first_ref, second_ref, mass, weight)
    out_ref[...] = field
    write_rims(field, even, rim_first_ref, rim_second_ref)


def total(parts_ref):
    value = parts_ref[0]
    for r in range(1, parts_ref.shape[0]):
        value = value + parts_ref[r]
    return value


def finish_kernel(
    parts, brow, bcol, panel_dev, slot_rows, weight, rank_ref, own_map_ref, nodes_ref, field_ref,
    first_ref, second_ref, mass_ref, parts_ref, out_ref, chunk_ref, rim_first_ref, rim_second_ref,
):
    rank = rank_ref[0]
    even = low_part(rank, 2) == 0
    field = rim_correction(field_ref[...], even, first_ref, second_ref, mass_ref[...], weight)
    out_ref[...] = field
    write_rims(field, even, rim_first_ref, rim_second_ref)
    loads = load_rows(total(parts_ref), own_map_ref[...], brow * bcol, slot_rows)
    pieces = trace_rows(field, nodes_ref[0:1, :], parts, bcol, brow * slot_rows)
    write_chunks(chunk_ref, pieces, loads)


def last_kernel(
    weight, rank_ref, field_ref, first_ref, second_ref, mass_ref, parts_ref, out_ref, potential_ref
):
    even = low_part(rank_ref[0], 2) == 0
    out_ref[...] = rim_correction(field_ref[...], even, first_ref, second_ref, mass_ref[...], weight)
    potential_ref[...] = total(parts_ref)


def density_groups(map_ref, chunk_ref, brow, bcol, panel_dev, slot_rows):
    devices = brow * bcol
    columns = LANES // HALVES
    rows = BLOCKS * slot_rows
    panels = BLOCKS * panel_dev
    lane = lax.broadcasted_iota(jnp.int32, (1, panels), 1).astype(F32)
    block = jnp.floor((lane + 0.5) * (1.0 / panel_dev)).astype(jnp.int32)
    traces = chunk_ref[...].astype(F32)
    for group in range(brow // BLOCKS):
        span = slice(group * panels, (group + 1) * panels)
        owner, slot = map_ref[0:1, span], map_ref[1:2, span]
        half, low = halves_of(slot, slot_rows)
        key = owner * rows + block * slot_rows + low
        near = traces[:, group * rows : (group + 1) * rows].reshape(devices * rows, LANES)
        found = dot(jnp.transpose(near).astype(BF16), one_hot_rows(key, devices * rows))
        density = jnp.where(half == 0, found[:columns], found[columns:])
        turned = jnp.concatenate([-density[columns // 2 :], density[: columns // 2]], axis=0)
        yield density.astype(BF16), turned.astype(BF16)


def write_parts(out_ref, total, panel_dev):
    for r in range(out_ref.shape[0]):
        out_ref[r] = total[:, r * panel_dev : (r + 1) * panel_dev]


def split_three(value):
    high = value.astype(BF16).astype(F32)
    middle = (value - high).astype(BF16).astype(F32)
    return [high, middle, value - high - middle]


def squares(axes):
    return sum(row * row for row in axes[1:]) + axes[0] * axes[0]


def rows_of(rows, dtype=BF16):
    row_id = lax.broadcasted_iota(jnp.int32, (16, rows[0].shape[1]), 0)
    value = jnp.zeros(row_id.shape, F32)
    for index, row in enumerate(rows):
        value = jnp.where(row_id == index, row, value)
    return value.astype(dtype)


def tile_kernel(
    brow, bcol, panel_dev, slot_rows, rank_ref, map_ref, chunk_ref, out_ref, tile_ref,
    target_ref, density_ref, turned_ref, distance_ref, built_ref, sum_ref, sems,
):
    count_all = brow * bcol * panel_dev
    soften = 0.5 * float(count_all) ** (-1.0 / 3.0)
    each = POINT_ROWS // 3
    row_index, col_index = high_part(rank_ref[0], bcol), low_part(rank_ref[0], bcol)
    start = brow * slot_rows + LOAD_ROWS
    block = pl.program_id(0)

    def points_of(device):
        return chunk_ref[device].astype(F32)[start : start + POINT_ROWS]

    def copy_of(index):
        return pltpu.make_async_copy(built_ref.at[index], tile_ref.at[index], sems.at[index])

    @pl.when(block == 0)
    def prepare():
        near = [points_of(row_index * bcol + c) for c in range(bcol)]
        axes = []
        for axis in range(3):
            rows = []
            for piece in near:
                for part in range(each):
                    wide = min(LANES, panel_dev - part * LANES)
                    rows.append(piece[axis * each + part : axis * each + part + 1, :wide])
            axes.append(jnp.concatenate(rows, axis=1))
        norms = split_three(squares(axes) + soften * soften)
        target_ref[...] = rows_of([-2.0 * row for row in axes] + [jnp.ones_like(axes[0])] * 3 + norms)
        sum_ref[...] = jnp.zeros_like(sum_ref)
        groups = density_groups(map_ref, chunk_ref, brow, bcol, panel_dev, slot_rows)
        for group, (density, turned) in enumerate(groups):
            for k in range(BLOCKS):
                span = slice(k * panel_dev, (k + 1) * panel_dev)
                density_ref[group * BLOCKS + k] = density[:, span]
                turned_ref[group * BLOCKS + k] = turned[:, span]

    piece = points_of(block * bcol + col_index)
    axes = [
        jnp.concatenate([piece[axis * each + part : axis * each + part + 1] for part in range(each)], axis=1)
        for axis in range(3)
    ]
    norms = split_three(squares(axes))
    source = jnp.transpose(rows_of(axes + norms + [jnp.ones_like(axes[0])] * 3, F32)).astype(BF16)
    distance_ref[...] = dot(source[:panel_dev], target_ref[...])
    step, lanes = 16, 4 * LANES
    wide = distance_ref.shape[1]
    places = [
        (slice(top, top + step), slice(left, min(left + lanes, wide)))
        for top in range(0, panel_dev, step)
        for left in range(0, wide, lanes)
    ]
    for rows, span in places:
        squared = distance_ref[rows, span]
        inverse = lax.rsqrt(squared)
        turns = (squared * inverse) * (wave_number / (2.0 * math.pi))
        turns = turns - ((turns + ROUNDER) - ROUNDER)
        z = turns * turns
        sine = jnp.full_like(z, SIN_POLY[-1])
        for factor in SIN_POLY[-2::-1]:
            sine = sine * z + factor
        sine = sine * turns
        rest = 1.0 - sine * sine
        safe = jnp.maximum(rest, 1e-12)
        cosine = safe * lax.rsqrt(safe)
        double = inverse * (2.0 / math.sqrt(float(count_all)))
        built_ref[block, 0, rows, span] = ((rest - 0.5) * double).astype(BF16)
        built_ref[block, 1, rows, span] = (sine * cosine * double).astype(BF16)
    copy_of(block).start()
    sum_ref[...] += dot(density_ref[block], built_ref[block, 0]) + dot(
        turned_ref[block], built_ref[block, 1]
    )

    @pl.when(block == brow - 1)
    def end():
        write_parts(out_ref, sum_ref[...], panel_dev)
        for index in range(brow):
            copy_of(index).wait()


def potential_kernel(
    brow, bcol, panel_dev, slot_rows, map_ref, chunk_ref, tile_ref, out_ref, held_ref, sems,
):
    copies = [
        pltpu.make_async_copy(tile_ref.at[block], held_ref.at[block], sems.at[block])
        for block in range(brow)
    ]
    for copy in copies:
        copy.start()
    whole = None
    groups = density_groups(map_ref, chunk_ref, brow, bcol, panel_dev, slot_rows)
    for group, (density, turned) in enumerate(groups):
        for k in range(BLOCKS):
            block = group * BLOCKS + k
            copies[block].wait()
            span = slice(k * panel_dev, (k + 1) * panel_dev)
            part = dot(density[:, span], held_ref[block, 0]) + dot(turned[:, span], held_ref[block, 1])
            whole = part if whole is None else whole + part
    write_parts(out_ref, whole, panel_dev)


def per_device(
    panel_points,
    panel_map,
    element_nodes,
    element_coef,
    element_matrix,
    node_mass,
    forcing,
    field_start,
    potential_start,
):
    columns, panel_dev = potential_start.shape
    count = field_start.shape[1]
    brow, bcol = lax.axis_size("brow"), lax.axis_size("bcol")
    devices = brow * bcol
    capacity = max(2, 2 * panel_dev // devices)
    slot_rows = -(-capacity // HALVES)
    used = brow * slot_rows
    assert slot_rows <= LOAD_ROWS and columns * HALVES == LANES and brow % BLOCKS == 0
    parts = 256 // columns
    width = count // parts
    row_panels = bcol * panel_dev
    row_index, col_index = lax.axis_index("brow"), lax.axis_index("bcol")
    rank = (row_index * bcol + col_index).reshape(1)
    nodes_each, elements = element_nodes.shape
    assert elements % GROUP == 0
    smem = pl.BlockSpec(memory_space=pltpu.SMEM)
    vmem = pl.BlockSpec(memory_space=pltpu.VMEM)
    rim_shape = shape_of((columns, RIM), BF16)
    field_shape = shape_of((columns, count), F32)
    weights = [weight_of(sweep_index) for sweep_index in range(SWEEPS)]
    even_pairs = [(i, i ^ 1) for i in range(devices)]
    odd_pairs = [pair for i in range(1, devices - 1, 2) for pair in ((i, i + 1), (i + 1, i))]
    even = (rank[0] & 1) == 0

    def chunk_shape(rows, unit):
        return shape_of((devices, -(-rows // unit) * unit, LANES), BF16)

    def exchange(first, second):
        return lax.ppermute(first, AXES, even_pairs), lax.ppermute(second, AXES, odd_pairs)

    def rims(field, halo, weight):
        first, second = (piece.astype(F32) for piece in halo)
        left, right = jnp.where(even, second, first), jnp.where(even, first, second)
        last = count - RIM
        low = field[:, :RIM] + (weight * penalty) * left / mass[:, :RIM]
        high = field[:, last:] + (weight * penalty) * right / mass[:, last:]
        return jnp.where(even, high, low).astype(BF16), jnp.where(even, low, high).astype(BF16)

    def swap_all(chunks):
        return lax.all_to_all(chunks, AXES, split_axis=0, concat_axis=0, tiled=True)

    hbm = pl.BlockSpec(memory_space=pltpu.HBM)
    hot_shape = (elements // GROUP, width, GROUP * LANES)
    tile_shape = (brow, HALVES, panel_dev, bcol * panel_dev)

    def sweep(field, rhs, weight, halo=(), weight_before=None, keep=False):
        rows = parts * columns
        lanes = GROUP * LANES
        large = (*in_vmem(field), *in_hbm(rhs)) if keep else (field, rhs)
        given = (rank, *in_hbm(element_coef), *large, *in_vmem(mass, keys, matrix), *halo)
        return call(
            functools.partial(sweep_kernel, parts, weight, weight_before, keep),
            (field_shape, kept((columns, count), F32)) if keep else field_shape,
            5_000_000_000,
            in_specs=[smem, smem, vmem, hbm if keep else vmem] + [vmem] * (len(given) - 4),
            out_specs=(vmem, vmem) if keep else vmem,
            scratch_shapes=[pltpu.SemaphoreType.DMA] * keep
            + [pltpu.VMEM((columns, count), F32)] * bool(halo)
            + [
                pltpu.VMEM(hot_shape, BF16),
                pltpu.VMEM((rows, width), BF16),
                pltpu.VMEM((rows, width), BF16),
                pltpu.VMEM((2, rows, lanes), F32),
                pltpu.VMEM((2, GROUP * columns, 2 * LANES), BF16),
                pltpu.VMEM((2, GROUP * columns, 2 * LANES), F32),
                pltpu.VMEM((2, rows, lanes), BF16),
                pltpu.VMEM((2, rows, lanes), BF16),
                pltpu.VMEM((rows, width), F32),
            ],
        )(*given)

    def add_loads(chunks, field, halo, weight):
        return call(
            functools.partial(loads_kernel, parts, brow, weight, used),
            (field_shape, field_shape, rim_shape, rim_shape),
            500_000_000,
            in_specs=[smem] + [vmem] * 7,
            out_specs=(vmem,) * 4,
        )(rank, *in_vmem(load_nodes), chunks, *in_vmem(forcing_kept), field, *halo, *in_vmem(mass))

    parts_shape = shape_of((bcol, columns, panel_dev), F32)
    sizes = (brow, bcol, panel_dev, slot_rows)
    tile_mib = -(-(2 * math.prod(tile_shape)) // MIB)

    def swap_parts(parts_out):
        return lax.all_to_all(parts_out, "bcol", split_axis=0, concat_axis=0, tiled=True)

    trace_slots, load_slots = table_lanes(brow, bcol, slot_rows)
    (nodes, load_nodes, source_map, own_map, keys, matrix, mass, field_kept, chunks, *rim) = call(
        functools.partial(setup_kernel, parts, brow, bcol, panel_dev, slot_rows),
        (
            kept((8, trace_slots), jnp.int32),
            kept((8, load_slots), jnp.int32),
            kept((3, brow * panel_dev), jnp.int32),
            kept((3, panel_dev), jnp.int32),
            kept((elements, LANES), jnp.int32),
            kept((LANES, LANES), F32),
            kept((1, count), F32),
            kept((columns, count), F32),
            chunk_shape(used + LOAD_ROWS + POINT_ROWS, 8),
            kept(rim_shape.shape, BF16),
            kept(rim_shape.shape, BF16),
        ),
        2_000_000_000,
        in_specs=[smem] + [vmem] * 7,
        out_specs=(vmem,) * 11,
    )(
        rank,
        *in_hbm(
            panel_map, field_start, potential_start, panel_points, element_nodes.T, element_matrix,
            node_mass.reshape(1, count),
        ),
    )
    halo = exchange(*rim)
    chunks = swap_all(chunks)
    field, forcing_kept = sweep(field_kept, forcing, weights[0], keep=True)
    parts_out, tiles = call(
        functools.partial(tile_kernel, *sizes),
        (parts_shape, pltpu.HBM(tile_shape, BF16)),
        8_000_000_000,
        grid=(brow,),
        limit=16 + tile_mib,
        in_specs=[smem, vmem, vmem],
        out_specs=(vmem, hbm),
        scratch_shapes=[
            pltpu.VMEM((16, bcol * panel_dev), BF16),
            pltpu.VMEM((brow, columns, panel_dev), BF16),
            pltpu.VMEM((brow, columns, panel_dev), BF16),
            pltpu.VMEM((panel_dev, bcol * panel_dev), F32),
            pltpu.VMEM(tile_shape, BF16),
            pltpu.VMEM((columns, bcol * panel_dev), F32),
            pltpu.SemaphoreType.DMA((brow,)),
        ],
    )(rank, *in_vmem(source_map), chunks)
    parts_in = swap_parts(parts_out)
    rhs, field, *rim = add_loads(chunks, field, halo, weights[0])
    halo = exchange(*rim)
    field = sweep(field, rhs, weights[1])
    halo_next = exchange(*rims(field, halo, weights[1]))
    field = sweep(field, rhs, weights[2], halo, weights[1])
    field, chunks, *rim = call(
        functools.partial(finish_kernel, parts, brow, bcol, panel_dev, slot_rows, weights[2]),
        (field_shape, chunk_shape(used + LOAD_ROWS, 8), rim_shape, rim_shape),
        1_000_000_000,
        in_specs=[smem] + [vmem] * 7,
        out_specs=(vmem,) * 4,
    )(rank, *in_vmem(own_map, nodes), field, *halo_next, *in_vmem(mass), parts_in)

    halo = exchange(*rim)
    chunks = swap_all(chunks)
    field = sweep(field, *in_vmem(forcing_kept), weights[0])
    parts_out = call(
        functools.partial(potential_kernel, *sizes),
        parts_shape,
        2_000_000_000,
        limit=16 + tile_mib,
        in_specs=[vmem, vmem, hbm],
        out_specs=vmem,
        scratch_shapes=[pltpu.VMEM(tile_shape, BF16), pltpu.SemaphoreType.DMA((brow,))],
    )(*in_vmem(source_map), chunks, *in_hbm(tiles))
    parts_in = swap_parts(parts_out)
    rhs, field, *rim = add_loads(chunks, field, halo, weights[0])
    halo = exchange(*rim)
    field = sweep(field, rhs, weights[1])
    halo_next = exchange(*rims(field, halo, weights[1]))
    field = sweep(field, rhs, weights[2], halo, weights[1])
    return call(
        functools.partial(last_kernel, weights[2]),
        (field_shape, shape_of((columns, panel_dev), F32)),
        100_000_000,
        in_specs=[smem] + [vmem] * 5,
        out_specs=(vmem, vmem),
    )(rank, field, *halo_next, *in_vmem(mass), parts_in)


def solution(mesh):
    placed = (
        P(None, AXES),
        P(),
        P(None, AXES),
        P(AXES),
        P(),
        P(AXES),
        P(None, AXES),
        P(None, AXES),
        P(None, AXES),
    )
    return jax.shard_map(
        per_device,
        mesh=mesh,
        in_specs=placed,
        out_specs=(P(None, AXES), P(None, AXES)),
        check_vma=False,
    )
```

```python
import functools
import math

import jax
import jax.numpy as jnp
from jax import lax
from jax.experimental import pallas as pl
from jax.experimental.pallas import tpu as pltpu
from jax.sharding import PartitionSpec as P

RIM = 128
SWEEPS = 3
LANES = 128
LOAD_ROWS = 8
POINT_ROWS = 8
HALVES = 2
GROUP = 4
BLOCKS = 4

wave_number = 20.0
penalty = 0.5

AXES = ("brow", "bcol")
F32 = jnp.float32
BF16 = jnp.bfloat16

SIN_POLY = (3.14159264, -5.16771008, 2.55007752, -0.59829129, 0.07765766)

ROUNDER = 1.5 * 2.0**23
MIB = 1024 * 1024


def weight_of(sweep):
    return 1.0 / (1.25 + 0.75 * math.cos(math.pi * (2 * sweep + 1) / (2.0 * SWEEPS)))


def call(kernel, out_shape, cost, limit=28, **more):
    return pl.pallas_call(
        kernel,
        out_shape=out_shape,
        compiler_params=pltpu.CompilerParams(vmem_limit_bytes=limit * MIB),
        cost_estimate=pl.CostEstimate(flops=cost, bytes_accessed=1 << 20, transcendentals=0),
        **more,
    )


def shape_of(shape, dtype):
    return jax.ShapeDtypeStruct(shape, dtype)


def kept(shape, dtype):
    return pltpu.VMEM(shape, dtype)


def in_hbm(*arrays):
    return tuple(pltpu.with_memory_space_constraint(array, pltpu.HBM) for array in arrays)


def in_vmem(*arrays):
    return tuple(pltpu.with_memory_space_constraint(array, pltpu.VMEM) for array in arrays)


def dot(a, b):
    return jnp.dot(a, b, preferred_element_type=F32)


def dot_nt(a, b):
    return lax.dot_general(a, b, (((1,), (1,)), ((), ())), preferred_element_type=F32)


def split_two(value):
    high = value.astype(BF16)
    return high, (value - high.astype(F32)).astype(BF16)


def low_part(value, size):
    return value & (size - 1) if size & (size - 1) == 0 else value % size


def high_part(value, size):
    return value >> (size.bit_length() - 1) if size & (size - 1) == 0 else value // size


def stack_parts(value, parts):
    width = value.shape[1] // parts
    return jnp.concatenate([value[:, i * width : (i + 1) * width] for i in range(parts)], axis=0)


def one_hot_rows(key, rows):
    seen = lax.broadcasted_iota(jnp.int16, (rows, key.shape[1]), 0)
    return jnp.where(seen == key.astype(jnp.int16), BF16(1), BF16(0))


def pick_part(stacked, part, parts):
    rows = stacked.shape[0] // parts
    picked = stacked[(parts - 1) * rows :]
    for i in reversed(range(parts - 1)):
        picked = jnp.where(part == i, stacked[i * rows : (i + 1) * rows], picked)
    return picked


def gather_nodes(field, nodes, parts):
    width = field.shape[1] // parts
    hot = one_hot_rows(jnp.where(nodes < 0, -1, low_part(nodes, width)), width)
    found = dot(stack_parts(field.astype(BF16), parts), hot)
    return pick_part(found, high_part(nodes, width), parts)


def scatter_nodes(values, nodes, parts, count):
    width = count // parts
    hot = one_hot_rows(jnp.where(nodes < 0, -1, low_part(nodes, width)), width)
    masked = jnp.concatenate(
        [jnp.where(high_part(nodes, width) == i, values, 0.0) for i in range(parts)], axis=0
    ).astype(BF16)
    added = dot_nt(masked, hot)
    rows = values.shape[0]
    return jnp.concatenate([added[i * rows : (i + 1) * rows] for i in range(parts)], axis=1)


def halves_of(slot, rows):
    half = jnp.where(slot >= rows, 1, 0)
    return half, slot - half * rows


def trace_rows(field, nodes, parts, groups, used):
    turned = jnp.transpose(gather_nodes(field, nodes, parts))
    pieces = []
    for group in range(groups):
        base = group * HALVES * used
        pieces.append(
            jnp.concatenate([turned[base : base + used], turned[base + used : base + 2 * used]], axis=1)
        )
    return pieces


def own_panels(map_ref, rank, panel_dev):
    first = rank * panel_dev
    base = (first >> 7) << 7
    window = -(-panel_dev // LANES) * LANES
    near = map_ref[:, pl.ds(pl.multiple_of(base, LANES), window)]
    return jnp.where(first == base, near[:, :panel_dev], near[:, window - panel_dev :])


def load_rows(potential, own_map, devices, slot_rows):
    owner, slot = own_map[0:1], own_map[1:2]
    half, low = halves_of(slot, slot_rows)
    rows = devices * LOAD_ROWS
    key = half * rows + owner * LOAD_ROWS + low
    found = dot_nt(one_hot_rows(key, HALVES * rows), potential.astype(BF16))
    return jnp.concatenate([found[:rows], found[rows:]], axis=1).reshape(devices, LOAD_ROWS, LANES)


def node_tables(map_ref, rank, brow, bcol, panel_dev, slot_rows):
    row_panels = bcol * panel_dev
    trace_slots, load_slots = table_lanes(brow, bcol, slot_rows)
    lane = lax.broadcasted_iota(jnp.int32, (1, row_panels), 1).astype(F32)
    block = jnp.floor((lane + 0.5) * (1.0 / panel_dev)).astype(jnp.int32)
    row_id = lax.broadcasted_iota(jnp.int32, (8, row_panels), 0)
    loads = []
    for r in range(brow):
        span = slice(r * row_panels, (r + 1) * row_panels)
        owner, slot, node = map_ref[0:1, span], map_ref[1:2, span], map_ref[2:3, span]
        half, low = halves_of(slot, slot_rows)
        values = jnp.where(
            row_id == 0, high_part(node, 256), jnp.where(row_id == 1, low_part(node, 256), 1)
        ).astype(F32).astype(BF16)
        key = jnp.where(owner == rank, (half * bcol + block) * LOAD_ROWS + low, -1)
        loads.append(dot_nt(values, one_hot_rows(key, load_slots // brow)))
    loads = jnp.concatenate(loads, axis=1)
    place = lax.broadcasted_iota(jnp.int32, (1, load_slots), 1)
    row, inside = place // (load_slots // brow), place % (load_slots // brow)
    half, inside = inside // (bcol * LOAD_ROWS), inside % (bcol * LOAD_ROWS)
    column, low = inside // LOAD_ROWS, inside % LOAD_ROWS
    key = ((column * HALVES + half) * brow + row) * slot_rows + low
    key = jnp.where((low < slot_rows) & (half < HALVES), key, -1)
    traces = dot_nt(loads.astype(BF16), one_hot_rows(key, trace_slots))
    tables = []
    for found in (traces, loads):
        table = jnp.where(found[2:3] > 0.5, found[0:1] * 256.0 + found[1:2], -1.0)
        tables.append(table.astype(jnp.int32))
    return tables


def table_lanes(brow, bcol, slot_rows):
    trace_slots = -(-HALVES * brow * bcol * slot_rows // LANES) * LANES
    return trace_slots, brow * (-(-HALVES * bcol * LOAD_ROWS // LANES) * LANES)


def point_rows(points):
    row_id = lax.broadcasted_iota(jnp.int32, (POINT_ROWS, LANES), 0)
    each = POINT_ROWS // 3
    width = points.shape[1]
    value = jnp.zeros((POINT_ROWS, LANES), F32)
    for axis in range(3):
        for part in range(-(-width // LANES)):
            piece = points[axis : axis + 1, part * LANES : (part + 1) * LANES]
            short = LANES - piece.shape[1]
            if short:
                piece = jnp.concatenate([piece, jnp.zeros((1, short), F32)], axis=1)
            value = jnp.where(row_id == axis * each + part, piece, value)
    return value


def write_chunks(chunk_ref, pieces, loads, points=None):
    used = pieces[0].shape[0]
    for device in range(chunk_ref.shape[0]):
        rows = [pieces[device % len(pieces)], loads[device]] + ([] if points is None else [points])
        left = chunk_ref.shape[1] - sum(piece.shape[0] for piece in rows)
        if left:
            rows.append(jnp.zeros((left, LANES), F32))
        chunk_ref[device] = jnp.concatenate(rows, axis=0).astype(BF16)


def write_rims(field, even, first_ref, second_ref):
    low = field[:, :RIM]
    high = field[:, field.shape[1] - RIM :]
    first_ref[...] = jnp.where(even, high, low).astype(BF16)
    second_ref[...] = jnp.where(even, low, high).astype(BF16)


def setup_kernel(
    parts, brow, bcol, panel_dev, slot_rows, rank_ref, map_ref, field_ref, potential_ref, points_ref,
    element_nodes_ref, element_matrix_ref, node_mass_ref,
    nodes_ref, load_nodes_ref, source_map_ref, own_map_ref, keys_ref, matrix_ref, mass_ref,
    field_kept_ref, chunk_ref, rim_first_ref, rim_second_ref,
):
    rank = rank_ref[0]
    source_map_ref[...] = jnp.concatenate(
        [
            own_panels(map_ref, r * bcol + low_part(rank, bcol), panel_dev)
            for r in range(brow)
        ],
        axis=1,
    )
    own_map = own_panels(map_ref, rank, panel_dev)
    own_map_ref[...] = own_map
    keys_ref[...] = jnp.zeros_like(keys_ref)
    keys_ref[:, : element_nodes_ref.shape[1]] = element_nodes_ref[...]
    matrix_ref[...] = jnp.zeros_like(matrix_ref)
    matrix_ref[: element_matrix_ref.shape[0], : element_matrix_ref.shape[1]] = element_matrix_ref[...]
    mass_ref[...] = node_mass_ref[...]
    nodes, load_nodes = node_tables(map_ref, rank, brow, bcol, panel_dev, slot_rows)
    nodes_ref[...] = jnp.broadcast_to(nodes, nodes_ref.shape)
    load_nodes_ref[...] = jnp.broadcast_to(load_nodes, load_nodes_ref.shape)
    field = field_ref[...]
    field_kept_ref[...] = field
    write_rims(field, low_part(rank, 2) == 0, rim_first_ref, rim_second_ref)
    loads = load_rows(potential_ref[...], own_map, brow * bcol, slot_rows)
    pieces = trace_rows(field, nodes, parts, bcol, brow * slot_rows)
    write_chunks(chunk_ref, pieces, loads, point_rows(points_ref[...].astype(F32)))


def rim_correction(value, even, first_ref, second_ref, mass, weight):
    step = weight * penalty
    first, second = first_ref[...].astype(F32), second_ref[...].astype(F32)
    left, right = jnp.where(even, second, first), jnp.where(even, first, second)
    last = value.shape[1] - RIM
    low = value[:, :RIM] + left * (step / mass[:, :RIM])
    high = value[:, last:] + right * (step / mass[:, last:])
    return jnp.concatenate([low, value[:, RIM:last], high], axis=1)


def received_loads(chunk_ref, used, brow, columns):
    received = chunk_ref[...].astype(F32)[:, used : used + LOAD_ROWS]
    received = received.reshape(received.shape[0] * LOAD_ROWS, LANES)
    span = received.shape[0] // brow
    rows = []
    for r in range(brow):
        piece = received[r * span : (r + 1) * span]
        rows += [piece[:, :columns], piece[:, columns : HALVES * columns]]
    return jnp.transpose(jnp.concatenate(rows, axis=0))


def sweep_kernel(
    parts, weight, weight_before, keep, rank_ref, coef_ref, field_ref, rhs_ref, mass_ref, keys_ref,
    matrix_ref, *more_refs,
):
    if keep:
        out_ref, kept_ref, sem, *scratch = more_refs
        copy = pltpu.make_async_copy(rhs_ref, kept_ref, sem)
        copy.start()
        rhs_ref = kept_ref
    elif weight_before is None:
        out_ref, *scratch = more_refs
    else:
        first_ref, second_ref, out_ref, field_scr, *scratch = more_refs
    hot_ref, high_ref, low_ref, found_ref, local_ref, product_ref, yhigh_ref, ylow_ref, sum_ref = scratch
    groups = hot_ref.shape[0]
    columns, count = field_ref.shape
    width = count // parts
    mass = mass_ref[...]
    if weight_before is None:
        field = field_ref[...]
        field_now = field_ref
    else:
        even = low_part(rank_ref[0], 2) == 0
        field = rim_correction(field_ref[...], even, first_ref, second_ref, mass, weight_before)
        field_scr[...] = field
        field_now = field_scr
    high, low = split_two(field)
    for h in range(parts):
        high_ref[h * columns : (h + 1) * columns] = high[:, h * width : (h + 1) * width]
        low_ref[h * columns : (h + 1) * columns] = low[:, h * width : (h + 1) * width]
    mat_high, mat_low = split_two(matrix_ref[...])
    matrix = jnp.concatenate(
        [
            jnp.concatenate([mat_high, mat_low], axis=1),
            jnp.concatenate([mat_high, jnp.zeros_like(mat_low)], axis=1),
        ],
        axis=0,
    )

    def build(group):
        for e in range(GROUP):
            key = keys_ref[group * GROUP + e : group * GROUP + e + 1, :]
            hot_ref[group, :, e * LANES : (e + 1) * LANES] = one_hot_rows(low_part(key, width), width)

    def gather(group):
        hot = hot_ref[group]
        found_ref[group % 2] = dot(high_ref[...], hot) + dot(low_ref[...], hot)

    def pick(group):
        slot = group % 2
        for e in range(GROUP):
            element = group * GROUP + e
            key = keys_ref[element : element + 1, :]
            got = pick_part(found_ref[slot, :, e * LANES : (e + 1) * LANES], high_part(key, width), parts)
            got_high, got_low = split_two(got)
            local_ref[slot, e * columns : (e + 1) * columns, :LANES] = got_high
            local_ref[slot, e * columns : (e + 1) * columns, LANES:] = got_low


    def multiply(group):
        product_ref[group % 2] = dot(local_ref[group % 2], matrix)

    def scale(group):
        slot = group % 2
        for e in range(GROUP):
            element = group * GROUP + e
            part = high_part(keys_ref[element : element + 1, :], width)
            rows = product_ref[slot, e * columns : (e + 1) * columns]
            value = (rows[:, :LANES] + rows[:, LANES:]) * coef_ref[element]
            value_high, value_low = split_two(value)
            span = slice(e * LANES, (e + 1) * LANES)
            for h in range(parts):
                mask = jnp.where(part == h, 1.0, 0.0).astype(BF16)
                yhigh_ref[slot, h * columns : (h + 1) * columns, span] = value_high * mask
                ylow_ref[slot, h * columns : (h + 1) * columns, span] = value_low * mask

    def scatter(group):
        hot = hot_ref[group]
        added = dot_nt(yhigh_ref[group % 2], hot) + dot_nt(ylow_ref[group % 2], hot)
        sum_ref[...] = added if group == 0 else sum_ref[...] + added

    build(0)
    gather(0)
    build(1)
    for group in range(groups):
        pick(group)
        if group + 1 < groups:
            gather(group + 1)
        if group + 2 < groups:
            build(group + 2)
        multiply(group)
        if group:
            scatter(group - 1)
        scale(group)
    scatter(groups - 1)
    if keep:
        copy.wait()
    for h in range(parts):
        span = slice(h * width, (h + 1) * width)
        stiff = sum_ref[h * columns : (h + 1) * columns]
        out_ref[:, span] = (1.0 - weight) * field_now[:, span] + (rhs_ref[:, span] - stiff) * (
            weight / mass[:, span]
        )


def loads_kernel(
    parts, brow, weight, used, rank_ref, nodes_ref, chunk_ref, forcing_ref, field_ref, first_ref,
    second_ref, mass_ref, rhs_ref, out_ref, rim_first_ref, rim_second_ref,
):
    columns, count = field_ref.shape
    loads = received_loads(chunk_ref, used, brow, columns)
    added = scatter_nodes(loads, nodes_ref[0:1, :], parts, count)
    rhs_ref[...] = forcing_ref[...] + added
    mass = mass_ref[...]
    even = low_part(rank_ref[0], 2) == 0
    field = field_ref[...] + added * (weight / mass)
    field = rim_correction(field, even, first_ref, second_ref, mass, weight)
    out_ref[...] = field
    write_rims(field, even, rim_first_ref, rim_second_ref)


def total(parts_ref):
    value = parts_ref[0]
    for r in range(1, parts_ref.shape[0]):
        value = value + parts_ref[r]
    return value


def finish_kernel(
    parts, brow, bcol, panel_dev, slot_rows, weight, rank_ref, own_map_ref, nodes_ref, field_ref,
    first_ref, second_ref, mass_ref, parts_ref, out_ref, chunk_ref, rim_first_ref, rim_second_ref,
):
    rank = rank_ref[0]
    even = low_part(rank, 2) == 0
    field = rim_correction(field_ref[...], even, first_ref, second_ref, mass_ref[...], weight)
    out_ref[...] = field
    write_rims(field, even, rim_first_ref, rim_second_ref)
    loads = load_rows(total(parts_ref), own_map_ref[...], brow * bcol, slot_rows)
    pieces = trace_rows(field, nodes_ref[0:1, :], parts, bcol, brow * slot_rows)
    write_chunks(chunk_ref, pieces, loads)


def last_kernel(
    weight, rank_ref, field_ref, first_ref, second_ref, mass_ref, parts_ref, out_ref, potential_ref
):
    even = low_part(rank_ref[0], 2) == 0
    out_ref[...] = rim_correction(field_ref[...], even, first_ref, second_ref, mass_ref[...], weight)
    potential_ref[...] = total(parts_ref)


def density_groups(map_ref, chunk_ref, brow, bcol, panel_dev, slot_rows):
    devices = brow * bcol
    columns = LANES // HALVES
    rows = BLOCKS * slot_rows
    panels = BLOCKS * panel_dev
    lane = lax.broadcasted_iota(jnp.int32, (1, panels), 1).astype(F32)
    block = jnp.floor((lane + 0.5) * (1.0 / panel_dev)).astype(jnp.int32)
    traces = chunk_ref[...].astype(F32)
    for group in range(brow // BLOCKS):
        span = slice(group * panels, (group + 1) * panels)
        owner, slot = map_ref[0:1, span], map_ref[1:2, span]
        half, low = halves_of(slot, slot_rows)
        key = owner * rows + block * slot_rows + low
        near = traces[:, group * rows : (group + 1) * rows].reshape(devices * rows, LANES)
        found = dot(jnp.transpose(near).astype(BF16), one_hot_rows(key, devices * rows))
        density = jnp.where(half == 0, found[:columns], found[columns:])
        turned = jnp.concatenate([-density[columns // 2 :], density[: columns // 2]], axis=0)
        yield density.astype(BF16), turned.astype(BF16)


def write_parts(out_ref, total, panel_dev):
    for r in range(out_ref.shape[0]):
        out_ref[r] = total[:, r * panel_dev : (r + 1) * panel_dev]


def split_three(value):
    high = value.astype(BF16).astype(F32)
    middle = (value - high).astype(BF16).astype(F32)
    return [high, middle, value - high - middle]


def squares(axes):
    return sum(row * row for row in axes[1:]) + axes[0] * axes[0]


def rows_of(rows, dtype=BF16):
    row_id = lax.broadcasted_iota(jnp.int32, (16, rows[0].shape[1]), 0)
    value = jnp.zeros(row_id.shape, F32)
    for index, row in enumerate(rows):
        value = jnp.where(row_id == index, row, value)
    return value.astype(dtype)


def tile_kernel(
    brow, bcol, panel_dev, slot_rows, rank_ref, map_ref, chunk_ref, out_ref, tile_ref,
    target_ref, density_ref, turned_ref, distance_ref, built_ref, sum_ref, sems,
):
    count_all = brow * bcol * panel_dev
    soften = 0.5 * float(count_all) ** (-1.0 / 3.0)
    each = POINT_ROWS // 3
    row_index, col_index = high_part(rank_ref[0], bcol), low_part(rank_ref[0], bcol)
    start = brow * slot_rows + LOAD_ROWS
    block = pl.program_id(0)

    def points_of(device):
        return chunk_ref[device].astype(F32)[start : start + POINT_ROWS]

    def copy_of(index):
        return pltpu.make_async_copy(built_ref.at[index], tile_ref.at[index], sems.at[index])

    @pl.when(block == 0)
    def prepare():
        near = [points_of(row_index * bcol + c) for c in range(bcol)]
        axes = []
        for axis in range(3):
            rows = []
            for piece in near:
                for part in range(each):
                    wide = min(LANES, panel_dev - part * LANES)
                    rows.append(piece[axis * each + part : axis * each + part + 1, :wide])
            axes.append(jnp.concatenate(rows, axis=1))
        norms = split_three(squares(axes) + soften * soften)
        target_ref[...] = rows_of([-2.0 * row for row in axes] + [jnp.ones_like(axes[0])] * 3 + norms)
        sum_ref[...] = jnp.zeros_like(sum_ref)
        groups = density_groups(map_ref, chunk_ref, brow, bcol, panel_dev, slot_rows)
        for group, (density, turned) in enumerate(groups):
            for k in range(BLOCKS):
                span = slice(k * panel_dev, (k + 1) * panel_dev)
                density_ref[group * BLOCKS + k] = density[:, span]
                turned_ref[group * BLOCKS + k] = turned[:, span]

    piece = points_of(block * bcol + col_index)
    axes = [
        jnp.concatenate([piece[axis * each + part : axis * each + part + 1] for part in range(each)], axis=1)
        for axis in range(3)
    ]
    norms = split_three(squares(axes))
    source = jnp.transpose(rows_of(axes + norms + [jnp.ones_like(axes[0])] * 3, F32)).astype(BF16)
    distance_ref[...] = dot(source[:panel_dev], target_ref[...])
    step, lanes = 16, 4 * LANES
    wide = distance_ref.shape[1]
    places = [
        (slice(top, top + step), slice(left, min(left + lanes, wide)))
        for top in range(0, panel_dev, step)
        for left in range(0, wide, lanes)
    ]
    for rows, span in places:
        squared = distance_ref[rows, span]
        inverse = lax.rsqrt(squared)
        turns = (squared * inverse) * (wave_number / (2.0 * math.pi))
        turns = turns - ((turns + ROUNDER) - ROUNDER)
        z = turns * turns
        sine = jnp.full_like(z, SIN_POLY[-1])
        for factor in SIN_POLY[-2::-1]:
            sine = sine * z + factor
        sine = sine * turns
        rest = 1.0 - sine * sine
        safe = jnp.maximum(rest, 1e-12)
        cosine = safe * lax.rsqrt(safe)
        double = inverse * (2.0 / math.sqrt(float(count_all)))
        built_ref[block, 0, rows, span] = ((rest - 0.5) * double).astype(BF16)
        built_ref[block, 1, rows, span] = (sine * cosine * double).astype(BF16)
    copy_of(block).start()
    sum_ref[...] += dot(density_ref[block], built_ref[block, 0]) + dot(
        turned_ref[block], built_ref[block, 1]
    )

    @pl.when(block == brow - 1)
    def end():
        write_parts(out_ref, sum_ref[...], panel_dev)
        for index in range(brow):
            copy_of(index).wait()


def potential_kernel(
    brow, bcol, panel_dev, slot_rows, map_ref, chunk_ref, tile_ref, out_ref, held_ref, sems,
):
    copies = [
        pltpu.make_async_copy(tile_ref.at[block], held_ref.at[block], sems.at[block])
        for block in range(brow)
    ]
    for copy in copies:
        copy.start()
    whole = None
    groups = density_groups(map_ref, chunk_ref, brow, bcol, panel_dev, slot_rows)
    for group, (density, turned) in enumerate(groups):
        for k in range(BLOCKS):
            block = group * BLOCKS + k
            copies[block].wait()
            span = slice(k * panel_dev, (k + 1) * panel_dev)
            part = dot(density[:, span], held_ref[block, 0]) + dot(turned[:, span], held_ref[block, 1])
            whole = part if whole is None else whole + part
    write_parts(out_ref, whole, panel_dev)


def per_device(
    panel_points,
    panel_map,
    element_nodes,
    element_coef,
    element_matrix,
    node_mass,
    forcing,
    field_start,
    potential_start,
):
    columns, panel_dev = potential_start.shape
    count = field_start.shape[1]
    brow, bcol = lax.axis_size("brow"), lax.axis_size("bcol")
    devices = brow * bcol
    capacity = max(2, 2 * panel_dev // devices)
    slot_rows = -(-capacity // HALVES)
    used = brow * slot_rows
    assert slot_rows <= LOAD_ROWS and columns * HALVES == LANES and brow % BLOCKS == 0
    parts = 256 // columns
    width = count // parts
    row_panels = bcol * panel_dev
    row_index, col_index = lax.axis_index("brow"), lax.axis_index("bcol")
    rank = (row_index * bcol + col_index).reshape(1)
    nodes_each, elements = element_nodes.shape
    assert elements % GROUP == 0
    smem = pl.BlockSpec(memory_space=pltpu.SMEM)
    vmem = pl.BlockSpec(memory_space=pltpu.VMEM)
    rim_shape = shape_of((columns, RIM), BF16)
    field_shape = shape_of((columns, count), F32)
    weights = [weight_of(sweep_index) for sweep_index in range(SWEEPS)]
    even_pairs = [(i, i ^ 1) for i in range(devices)]
    odd_pairs = [pair for i in range(1, devices - 1, 2) for pair in ((i, i + 1), (i + 1, i))]
    even = (rank[0] & 1) == 0

    def chunk_shape(rows, unit):
        return shape_of((devices, -(-rows // unit) * unit, LANES), BF16)

    def exchange(first, second):
        return lax.ppermute(first, AXES, even_pairs), lax.ppermute(second, AXES, odd_pairs)

    def rims(field, halo, weight):
        first, second = (piece.astype(F32) for piece in halo)
        left, right = jnp.where(even, second, first), jnp.where(even, first, second)
        last = count - RIM
        low = field[:, :RIM] + (weight * penalty) * left / mass[:, :RIM]
        high = field[:, last:] + (weight * penalty) * right / mass[:, last:]
        return jnp.where(even, high, low).astype(BF16), jnp.where(even, low, high).astype(BF16)

    def swap_all(chunks):
        return lax.all_to_all(chunks, AXES, split_axis=0, concat_axis=0, tiled=True)

    hbm = pl.BlockSpec(memory_space=pltpu.HBM)
    hot_shape = (elements // GROUP, width, GROUP * LANES)
    tile_shape = (brow, HALVES, panel_dev, bcol * panel_dev)

    def sweep(field, rhs, weight, halo=(), weight_before=None, keep=False):
        rows = parts * columns
        lanes = GROUP * LANES
        large = (*in_vmem(field), *in_hbm(rhs)) if keep else (field, rhs)
        given = (rank, *in_hbm(element_coef), *large, *in_vmem(mass, keys, matrix), *halo)
        return call(
            functools.partial(sweep_kernel, parts, weight, weight_before, keep),
            (field_shape, kept((columns, count), F32)) if keep else field_shape,
            5_000_000_000,
            in_specs=[smem, smem, vmem, hbm if keep else vmem] + [vmem] * (len(given) - 4),
            out_specs=(vmem, vmem) if keep else vmem,
            scratch_shapes=[pltpu.SemaphoreType.DMA] * keep
            + [pltpu.VMEM((columns, count), F32)] * bool(halo)
            + [
                pltpu.VMEM(hot_shape, BF16),
                pltpu.VMEM((rows, width), BF16),
                pltpu.VMEM((rows, width), BF16),
                pltpu.VMEM((2, rows, lanes), F32),
                pltpu.VMEM((2, GROUP * columns, 2 * LANES), BF16),
                pltpu.VMEM((2, GROUP * columns, 2 * LANES), F32),
                pltpu.VMEM((2, rows, lanes), BF16),
                pltpu.VMEM((2, rows, lanes), BF16),
                pltpu.VMEM((rows, width), F32),
            ],
        )(*given)

    def add_loads(chunks, field, halo, weight):
        return call(
            functools.partial(loads_kernel, parts, brow, weight, used),
            (field_shape, field_shape, rim_shape, rim_shape),
            500_000_000,
            in_specs=[smem] + [vmem] * 7,
            out_specs=(vmem,) * 4,
        )(rank, *in_vmem(load_nodes), chunks, *in_vmem(forcing_kept), field, *halo, *in_vmem(mass))

    parts_shape = shape_of((bcol, columns, panel_dev), F32)
    sizes = (brow, bcol, panel_dev, slot_rows)
    tile_mib = -(-(2 * math.prod(tile_shape)) // MIB)

    def swap_parts(parts_out):
        return lax.all_to_all(parts_out, "bcol", split_axis=0, concat_axis=0, tiled=True)

    trace_slots, load_slots = table_lanes(brow, bcol, slot_rows)
    (nodes, load_nodes, source_map, own_map, keys, matrix, mass, field_kept, chunks, *rim) = call(
        functools.partial(setup_kernel, parts, brow, bcol, panel_dev, slot_rows),
        (
            kept((8, trace_slots), jnp.int32),
            kept((8, load_slots), jnp.int32),
            kept((3, brow * panel_dev), jnp.int32),
            kept((3, panel_dev), jnp.int32),
            kept((elements, LANES), jnp.int32),
            kept((LANES, LANES), F32),
            kept((1, count), F32),
            kept((columns, count), F32),
            chunk_shape(used + LOAD_ROWS + POINT_ROWS, 8),
            kept(rim_shape.shape, BF16),
            kept(rim_shape.shape, BF16),
        ),
        2_000_000_000,
        in_specs=[smem] + [vmem] * 7,
        out_specs=(vmem,) * 11,
    )(
        rank,
        *in_hbm(
            panel_map, field_start, potential_start, panel_points, element_nodes.T, element_matrix,
            node_mass.reshape(1, count),
        ),
    )
    halo = exchange(*rim)
    chunks = swap_all(chunks)
    field, forcing_kept = sweep(field_kept, forcing, weights[0], keep=True)
    parts_out, tiles = call(
        functools.partial(tile_kernel, *sizes),
        (parts_shape, pltpu.HBM(tile_shape, BF16)),
        8_000_000_000,
        grid=(brow,),
        limit=16 + tile_mib,
        in_specs=[smem, vmem, vmem],
        out_specs=(vmem, hbm),
        scratch_shapes=[
            pltpu.VMEM((16, bcol * panel_dev), BF16),
            pltpu.VMEM((brow, columns, panel_dev), BF16),
            pltpu.VMEM((brow, columns, panel_dev), BF16),
            pltpu.VMEM((panel_dev, bcol * panel_dev), F32),
            pltpu.VMEM(tile_shape, BF16),
            pltpu.VMEM((columns, bcol * panel_dev), F32),
            pltpu.SemaphoreType.DMA((brow,)),
        ],
    )(rank, *in_vmem(source_map), chunks)
    parts_in = swap_parts(parts_out)
    rhs, field, *rim = add_loads(chunks, field, halo, weights[0])
    halo = exchange(*rim)
    field = sweep(field, rhs, weights[1])
    halo_next = exchange(*rims(field, halo, weights[1]))
    field = sweep(field, rhs, weights[2], halo, weights[1])
    field, chunks, *rim = call(
        functools.partial(finish_kernel, parts, brow, bcol, panel_dev, slot_rows, weights[2]),
        (field_shape, chunk_shape(used + LOAD_ROWS, 8), rim_shape, rim_shape),
        1_000_000_000,
        in_specs=[smem] + [vmem] * 7,
        out_specs=(vmem,) * 4,
    )(rank, *in_vmem(own_map, nodes), field, *halo_next, *in_vmem(mass), parts_in)

    halo = exchange(*rim)
    chunks = swap_all(chunks)
    field = sweep(field, *in_vmem(forcing_kept), weights[0])
    parts_out = call(
        functools.partial(potential_kernel, *sizes),
        parts_shape,
        2_000_000_000,
        limit=16 + tile_mib,
        in_specs=[vmem, vmem, hbm],
        out_specs=vmem,
        scratch_shapes=[pltpu.VMEM(tile_shape, BF16), pltpu.SemaphoreType.DMA((brow,))],
    )(*in_vmem(source_map), chunks, *in_hbm(tiles))
    parts_in = swap_parts(parts_out)
    rhs, field, *rim = add_loads(chunks, field, halo, weights[0])
    halo = exchange(*rim)
    field = sweep(field, rhs, weights[1])
    halo_next = exchange(*rims(field, halo, weights[1]))
    field = sweep(field, rhs, weights[2], halo, weights[1])
    return call(
        functools.partial(last_kernel, weights[2]),
        (field_shape, shape_of((columns, panel_dev), F32)),
        100_000_000,
        in_specs=[smem] + [vmem] * 5,
        out_specs=(vmem, vmem),
    )(rank, field, *halo_next, *in_vmem(mass), parts_in)


def solution(mesh):
    placed = (
        P(None, AXES),
        P(),
        P(None, AXES),
        P(AXES),
        P(),
        P(AXES),
        P(None, AXES),
        P(None, AXES),
        P(None, AXES),
    )
    return jax.shard_map(
        per_device,
        mesh=mesh,
        in_specs=placed,
        out_specs=(P(None, AXES), P(None, AXES)),
        check_vma=False,
    )
```
